32 devices in a mesh: ctx: 8 (over z, core), fsdp: 4 (over y, x).
Axes of the slice: x: 2, y: 2, z: 4, core: 2. Of those that a mesh axis runs over, the one named last changes fastest.
Arguments:
- layer_input: bfloat16 [4, 1024, 2304], P('fsdp', 'ctx'), may hold values from -6 to 6
- attn_weights: bfloat16 [2304, 6144], P('fsdp'), may hold values from -0.125 to 0.125
- mlp_in_weights: bfloat16 [2304, 18432], P('fsdp'), may hold values from -0.125 to 0.125
- mlp_out_weights: bfloat16 [2304, 9216], P('fsdp'), may hold values from -0.0625 to 0.0625
- norm_gains: bfloat16 [2304, 4], P('fsdp'), may hold values from 0.5 to 1.5
- output_grad: bfloat16 [4, 1024, 2304], P('fsdp', 'ctx'), may hold values from -6 to 6
Outputs:
- layer_output: bfloat16 [4, 1024, 2304], P('fsdp', 'ctx')
- input_grad: float32 [4, 1024, 2304], P('fsdp', 'ctx')
- attn_weights_grad: float32 [2304, 6144], P(('ctx', 'fsdp'))
- mlp_in_grad: float32 [2304, 18432], P(('ctx', 'fsdp'))
- mlp_out_grad: float32 [2304, 9216], P(('ctx', 'fsdp'))
- norm_gains_grad: float32 [2304, 4], P(('ctx', 'fsdp'))
The draws below stay inside these ranges and needn't reach their ends.
All inputs are finite; a program needn't handle non-finite values.
Results may differ from the reference program's by a relative error of at most 0.02.
Values may be sent and summed in bfloat16 or wider, within the bound.
No kernel may reach another device: no remote copies, remote signals or barrier semaphores. Data moves between devices by JAX's collectives and lax.ppermute only.
A program may use at most 448 MiB of HBM per device.

```python
import math
import jax
import jax.numpy as jnp
from jax import lax

D = 2304
FF = 9216
HEADS = 8
KV_HEADS = 4
HEAD_DIM = 256
BLOCK = 64
LEN = 1024
SEQS = 4
ATTN_COLS = 6144
N_CTX = 8


def strengthened(values, key, source, target, shards_of, factor):
    def block_of(position):
        return (jnp.arange(values.shape[position]) // (values.shape[position] // shards_of)).reshape((-1,) + (1,) * (values.ndim - 1 - position))

    near = jax.random.permutation(key, shards_of)[block_of(target)]
    second = (block_of(target) + shards_of // 2) % shards_of
    return jnp.where((block_of(source) == near) | (block_of(source) == second), factor * values, values)


def block_levels(own_key, shape, split, low, top_value):
    loudness = 1.0
    for axis_at, shards_of in split:
        heights = jax.random.uniform(jax.random.fold_in(jax.random.fold_in(own_key, 6), axis_at), (shards_of,), jnp.float32, low / len(split), top_value / len(split))
        loudness = loudness * jnp.repeat(jnp.exp(heights), shape[axis_at] // shards_of).reshape((-1,) + (1,) * (len(shape) - 1 - axis_at))
    return loudness


def noise(stream_key, dims, scale, bound, split=(), kind=jnp.bfloat16):
    loudness = block_levels(stream_key, dims, split, -0.22, 0.18) if split else 1.0
    drawn = jax.random.normal(stream_key, dims, jnp.float32) * scale * loudness
    return jnp.minimum(jnp.maximum(drawn, -bound), bound).astype(kind)


def gaussian_with(key, dims, scale, bound, split, heavy, held_as=jnp.bfloat16):
    values = scale * jax.random.normal(key, dims, jnp.float32)
    if split:
        values = values * block_levels(key, dims, split, -0.22, 0.18)
    return jnp.clip(strengthened(values, jax.random.fold_in(key, 3), *heavy), -bound, bound).astype(held_as)


def setup_inputs(seed: int = 0) -> dict:
    seeds = jax.random.split(jax.random.key(seed), 7)
    return {
        "layer_input": noise(seeds[0], (SEQS, LEN, D), 1.0, 6.0, ((0, 4), (1, 8))),
        "attn_weights": noise(seeds[1], (D, ATTN_COLS), D ** -0.5, 0.125, ((0, 4),)),
        "mlp_in_weights": noise(seeds[2], (D, 2 * FF), D ** -0.5, 0.125, ((0, 4),)),
        "mlp_out_weights": noise(seeds[3], (D, FF), FF ** -0.5, 0.0625, ((0, 4),)),
        "norm_gains": jnp.clip(1.0 + 0.1 * jax.random.normal(seeds[4], (D, 4), jnp.float32), 0.5, 1.5).astype(jnp.bfloat16),
        "output_grad": gaussian_with(seeds[5], (SEQS, LEN, D), 1.0, 6.0, ((0, 4), (1, 8)), (1, 2, 8, 2.0)),
    }


@jax.custom_vjp
def low(v):
    return lax.optimization_barrier(v.astype(jnp.bfloat16)).astype(jnp.float32)

@jax.custom_vjp
def low_back(v):
    return v

def low_keep(v):
    return (low(v), None)

def low_pass(kept, grad):
    return (grad,)

def back_keep(v):
    return (v, None)

def back_low(kept, grad):
    return (low(grad),)
low.defvjp(low_keep, low_pass)
low_back.defvjp(back_keep, back_low)
EPSILON = 1e-06
SOFT_CAP = 50.0
ROTARY_BASE = 10000.0
MASKED_SCORE = -1e+30
PRECISE = lax.Precision.HIGHEST

def positions():
    rows = jnp.arange(LEN, dtype=jnp.int32)
    owners = rows // (2 * BLOCK)
    within = rows % (2 * BLOCK)
    return jnp.where(within < BLOCK, owners * BLOCK + within, (2 * N_CTX - 1 - owners) * BLOCK + within - BLOCK)

def rms_norm(values, gain):
    return values * lax.rsqrt(lax.optimization_barrier(jnp.mean(values * values, -1, keepdims=True)) + EPSILON) * gain

def rotary(values, places):
    half_width = values.shape[-1] // 2
    frequency = ROTARY_BASE ** (-jnp.arange(half_width, dtype=jnp.float32) * 2.0 / values.shape[-1])
    angles = places.astype(jnp.float32)[:, None] * frequency[None, :]
    cosine = jnp.concatenate([jnp.cos(angles), jnp.cos(angles)], -1)[:, None, :]
    sine_table = jnp.concatenate([jnp.sin(angles), jnp.sin(angles)], -1)[:, None, :]
    turned = jnp.concatenate([-values[..., half_width:], values[..., :half_width]], -1)
    return values * cosine + turned * sine_table

def attend(query_block, place_block, key_all, value_all, places):
    raw_scores = low_back(jnp.einsum('tkgd,lkd->kgtl', query_block, key_all, precision=PRECISE))
    capped = SOFT_CAP * jnp.tanh(raw_scores * HEAD_DIM ** (-0.5) / SOFT_CAP)
    allowed = places[None, :] <= place_block[:, None]
    capped = jnp.where(allowed, capped, MASKED_SCORE)
    row_max = lax.optimization_barrier(jnp.max(capped, -1, keepdims=True))
    weights = jnp.exp(capped - row_max)
    chances = low(weights / lax.optimization_barrier(jnp.sum(weights, -1, keepdims=True)))
    return jnp.einsum('kgtl,lkd->tkgd', chances, value_all, precision=PRECISE)

def forward(source, attn_mat, mlp_in_mat, mlp_out_mat, gain_mat, places):
    query_cols = HEADS * HEAD_DIM
    key_cols = KV_HEADS * HEAD_DIM
    groups = HEADS // KV_HEADS
    normed_in = low(rms_norm(source, gain_mat[:, 0]))
    projected = jnp.dot(normed_in, attn_mat[:, :query_cols + 2 * key_cols], precision=PRECISE)
    query_raw = low_back(projected[:, :query_cols]).reshape(LEN, HEADS, HEAD_DIM)
    key_raw = low_back(projected[:, query_cols:query_cols + key_cols]).reshape(LEN, KV_HEADS, HEAD_DIM)
    value_all = low(low_back(projected[:, query_cols + key_cols:])).reshape(LEN, KV_HEADS, HEAD_DIM)
    query = low(rotary(query_raw, places)).reshape(LEN, KV_HEADS, groups, HEAD_DIM)
    key_all = low(rotary(key_raw, places))
    block_rows = math.gcd(LEN, 512)
    query_blocks = query.reshape(LEN // block_rows, block_rows, KV_HEADS, groups, HEAD_DIM)
    place_blocks = places.reshape(LEN // block_rows, block_rows)
    attend_saved = jax.checkpoint(attend)

    def attend_block(pieces):
        return attend_saved(pieces[0], pieces[1], key_all, value_all, places)
    attended = lax.map(attend_block, (query_blocks, place_blocks)).reshape(LEN, query_cols)
    attended = low(low_back(attended))
    branch = low_back(jnp.dot(attended, attn_mat[:, query_cols + 2 * key_cols:].T, precision=PRECISE))
    residual = source + rms_norm(branch, gain_mat[:, 1])
    normed_mid = low(rms_norm(residual, gain_mat[:, 2]))
    gate_up = low_back(jnp.dot(normed_mid, mlp_in_mat, precision=PRECISE))
    hidden = low(jax.nn.gelu(gate_up[:, :FF], approximate=True) * gate_up[:, FF:])
    mixed = low_back(jnp.dot(hidden, mlp_out_mat.T, precision=PRECISE))
    return residual + rms_norm(mixed, gain_mat[:, 3])

def reference(layer_input, attn_weights, mlp_in_weights, mlp_out_weights, norm_gains, output_grad):
    places = positions()
    params = tuple((weight.astype(jnp.float32) for weight in (attn_weights, mlp_in_weights, mlp_out_weights, norm_gains)))

    def layer_of(source, attn_mat, mlp_in_mat, mlp_out_mat, gain_mat):
        return forward(source, attn_mat, mlp_in_mat, mlp_out_mat, gain_mat, places)

    def one_sequence(totals, pieces):
        inputs, cotangent = pieces
        result, pullback = jax.vjp(layer_of, inputs.astype(jnp.float32), *params)
        grads = pullback(cotangent.astype(jnp.float32))
        totals = tuple((running + addend for running, addend in zip(totals, grads[1:])))
        return (totals, (result.astype(jnp.bfloat16), grads[0]))
    zero_sums = tuple((jnp.zeros_like(weight) for weight in params))
    totals, (results, input_grads) = lax.scan(one_sequence, zero_sums, (layer_input, output_grad))
    return (results, input_grads, totals[0], totals[1], totals[2], totals[3])
```

```python
import jax
import jax.numpy as jnp
from jax import lax
from jax.sharding import PartitionSpec as P

HEADS = 8
KV_HEADS = 4
HEAD_DIM = 256

EPSILON = 1e-06
SOFT_CAP = 50.0
ROTARY_BASE = 10000.0
MASKED_SCORE = -1e30
STREAMS = 2

F32 = jnp.float32
BF16 = jnp.bfloat16


def positions_of(rows, half_block, ctx_count):
    owners = rows // (2 * half_block)
    within = rows % (2 * half_block)
    return jnp.where(
        within < half_block,
        owners * half_block + within,
        (2 * ctx_count - 1 - owners) * half_block + within - half_block,
    )


def rotary_tables(places, head_dim):
    half_width = head_dim // 2
    frequency = ROTARY_BASE ** (-jnp.arange(half_width, dtype=F32) * 2.0 / head_dim)
    angles = places.astype(F32)[:, None] * frequency[None, :]
    cosine = jnp.concatenate([jnp.cos(angles), jnp.cos(angles)], -1)
    sine_table = jnp.concatenate([jnp.sin(angles), jnp.sin(angles)], -1)
    return (cosine, sine_table)


def turned(values):
    half_width = values.shape[-1] // 2
    return jnp.concatenate([-values[..., half_width:], values[..., :half_width]], -1)


def rotate(values, cosine, sine_table):
    return values * cosine + turned(values) * sine_table


def rotate_back(grads, cosine, sine_table):
    return grads * cosine - turned(grads * sine_table)


def inverse_rms(values):
    return lax.rsqrt(jnp.mean(values * values, -1, keepdims=True) + EPSILON)


def norm_backward(values, scale, grad_normed):
    normed = values * scale
    return scale * (grad_normed - normed * jnp.mean(grad_normed * normed, -1, keepdims=True))


def geglu(gate, upper):
    return jax.nn.gelu(gate, approximate=True) * upper


def dot(a, b):
    return jnp.dot(a, b, preferred_element_type=F32)


def dot_t(a, b):
    return jnp.einsum("tk,dk->td", a, b, preferred_element_type=F32)


def shift(values, step, first, last):
    pairs = [
        (2 * r + core, 2 * (r + step) + core) for r in range(first, last + 1) for core in (0, 1)
    ]
    return lax.ppermute(values, "ctx", pairs)


def from_partner(values, ctx_count):
    return lax.ppermute(values, "ctx", [(i, i ^ 1) for i in range(ctx_count)])


def line_gather(values, rank, ranks):
    ups, downs = [values], [values]
    for k in range(1, ranks):
        ups.append(shift(ups[-1], 1, k - 1, ranks - 2))
        downs.append(shift(downs[-1], -1, 1, ranks - k))
    return [values] + [
        jnp.where(rank + k < ranks, downs[k], ups[ranks - k]) for k in range(1, ranks)
    ]


def line_scatter(parts, ranks):
    up = down = None
    for k in range(ranks - 1, 0, -1):
        up = parts[k] if up is None else parts[k] + up.astype(F32)
        up = shift(up.astype(BF16), 1, 0, ranks - 1 - k)
        down = parts[ranks - k] if down is None else parts[ranks - k] + down.astype(F32)
        down = shift(down.astype(BF16), -1, k, ranks - 1)
    return parts[0] + up.astype(F32) + down.astype(F32)


def local(layer_input, attn_weights, mlp_in_weights, mlp_out_weights, norm_gains, output_grad):
    tokens, width = layer_input.shape[1:]
    half_block = tokens // 2
    ctx_count = lax.axis_size("ctx")
    fsdp_count = lax.axis_size("fsdp")
    ranks = ctx_count // 2
    place = lax.axis_index("ctx")
    rank, core = place // 2, place % 2
    first_core = core == 0
    query_cols, key_cols = HEADS * HEAD_DIM, KV_HEADS * HEAD_DIM
    qkv_cols = query_cols + 2 * key_cols
    heads = HEADS // ranks
    sharing = ranks // KV_HEADS
    hidden_width = mlp_out_weights.shape[1]
    q_own = query_cols // ctx_count
    f_own = hidden_width // ctx_count
    shard_rows = width // (ctx_count * fsdp_count)
    scaling = HEAD_DIM**-0.5

    def partner(values):
        return from_partner(values, ctx_count)

    def columns(array, start, size):
        return lax.dynamic_slice_in_dim(array, start, size, 1)

    def gathered(*pieces):
        piece = pieces[0] if len(pieces) == 1 else jnp.concatenate(pieces, 1)
        return lax.all_gather(piece, "fsdp", axis=0, tiled=True)

    kv_start = query_cols + core * key_cols + rank // sharing * HEAD_DIM
    attn_own = gathered(
        columns(attn_weights, place * q_own, q_own),
        columns(attn_weights, kv_start, HEAD_DIM),
        columns(attn_weights, qkv_cols + place * q_own, q_own),
    )
    in_own = gathered(
        columns(mlp_in_weights, place * f_own, f_own),
        columns(mlp_in_weights, hidden_width + place * f_own, f_own),
    )
    out_own = gathered(columns(mlp_out_weights, place * f_own, f_own))
    gains = lax.all_gather(norm_gains, "fsdp", axis=0, tiled=True).astype(F32)
    g_pre, g_post, g_mid, g_out = [gains[:, i] for i in range(4)]
    attn_other, in_other, out_other = partner(attn_own), partner(in_own), partner(out_own)
    qkv_own, proj_own = attn_own[:, : q_own + HEAD_DIM], attn_own[:, q_own + HEAD_DIM :]
    qkv_other, proj_other = attn_other[:, : q_own + HEAD_DIM], attn_other[:, q_own + HEAD_DIM :]

    own_input = layer_input.reshape(tokens, width)
    source = own_input.astype(F32)
    upstream = output_grad.reshape(tokens, width).astype(F32)
    inputs = jnp.concatenate(line_gather(own_input, rank, ranks), 0).astype(F32)
    scale_in = inverse_rms(inputs)
    plain_in = inputs * scale_in
    normed_in = (plain_in * g_pre).astype(BF16)

    def places_of(which):
        slots = (rank + jnp.arange(ranks, dtype=jnp.int32)) % ranks
        owners = (2 * slots + which)[:, None] * tokens
        rows = owners + jnp.arange(tokens, dtype=jnp.int32)[None, :]
        return positions_of(rows.reshape(-1), half_block, ctx_count)

    own_places, other_places = places_of(core), places_of(1 - core)
    cosine, sine_table = rotary_tables(own_places, HEAD_DIM)
    all_places = jnp.concatenate([own_places, other_places], 0)
    allowed = all_places[None, :] <= own_places[:, None]
    rows = ranks * tokens

    def ordered(mine, theirs):
        return jnp.where(first_core, mine, theirs), jnp.where(first_core, theirs, mine)

    proj_a, proj_b = dot(normed_in, qkv_own), dot(normed_in, qkv_other)
    query_raw = jnp.concatenate(ordered(proj_a[:, :q_own], proj_b[:, :q_own]), 1)
    key_raw, value_raw = ordered(proj_a[:, q_own:], proj_b[:, q_own:])
    query = rotate(
        query_raw.reshape(rows, heads, HEAD_DIM), cosine[:, None], sine_table[:, None]
    ).astype(BF16)
    key_own = rotate(key_raw, cosine, sine_table).astype(BF16)
    value_own = value_raw.astype(BF16)
    key_value = jnp.concatenate([key_own, value_own], 1)
    key_value = jnp.concatenate([key_value, partner(key_value)], 0)
    keys, values = key_value[:, :HEAD_DIM], key_value[:, HEAD_DIM:]

    def score_rows():
        raw_scores = jnp.einsum("tgd,ld->gtl", query, keys, preferred_element_type=F32)
        tanh_part = jnp.tanh(raw_scores * scaling / SOFT_CAP)
        return tanh_part, jnp.where(allowed, SOFT_CAP * tanh_part, MASKED_SCORE)

    tanh_part, capped = score_rows()
    row_max = jnp.max(capped, -1, keepdims=True)
    weights = jnp.exp(capped - row_max)
    row_total = jnp.sum(weights, -1, keepdims=True)
    log_total = row_max + jnp.log(row_total)
    chances = (weights / row_total).astype(BF16)
    attended = jnp.einsum("gtl,ld->tgd", chances, values, preferred_element_type=F32)
    attended = attended.reshape(rows, heads * HEAD_DIM).astype(BF16)
    att_own, att_other = ordered(attended[:, :q_own], attended[:, q_own:])
    branch_parts = (dot_t(att_own, proj_own) + dot_t(att_other, proj_other)).reshape(
        ranks, tokens, width
    )

    span = tokens // STREAMS
    gains_sums = {"out": 0.0, "mid": 0.0, "post": 0.0}
    streams = []
    for s in range(STREAMS):
        cut = slice(s * span, (s + 1) * span)
        st = {"cut": cut}
        branch = line_scatter([branch_parts[k, cut] for k in range(ranks)], ranks)
        scale_branch = inverse_rms(branch)
        residual = source[cut] + branch * scale_branch * g_post
        scale_mid = inverse_rms(residual)
        normed_mid = (residual * scale_mid * g_mid).astype(BF16)
        mids = jnp.concatenate(line_gather(normed_mid, rank, ranks), 0)
        hiddens, backs, mixed = [], [], 0.0
        for w_in, w_out in ((in_own, out_own), (in_other, out_other)):
            gate_up = dot(mids, w_in)
            hidden, back = jax.vjp(geglu, gate_up[:, :f_own], gate_up[:, f_own:])
            hidden = hidden.astype(BF16)
            hiddens.append(hidden)
            backs.append(back)
            mixed = mixed + dot_t(hidden, w_out)
        mixed = mixed.reshape(ranks, span, width)
        mixed = line_scatter([mixed[k] for k in range(ranks)], ranks)
        scale_mixed = inverse_rms(mixed)
        st["out"] = (residual + mixed * scale_mixed * g_out).astype(BF16)
        up = upstream[cut]
        gains_sums["out"] += jnp.sum(up * mixed * scale_mixed, 0)
        d_mixed = norm_backward(mixed, scale_mixed, up * g_out).astype(BF16)
        d_mixeds = jnp.concatenate(line_gather(d_mixed, rank, ranks), 0)
        d_mid, d_gate_ups = 0.0, []
        for w_in, w_out, back in ((in_own, out_own, backs[0]), (in_other, out_other, backs[1])):
            d_gate, d_upper = back(dot(d_mixeds, w_out))
            d_gate_up = jnp.concatenate([d_gate, d_upper], 1).astype(BF16)
            d_gate_ups.append(d_gate_up)
            d_mid = d_mid + dot_t(d_gate_up, w_in)
        d_mid = d_mid.reshape(ranks, span, width)
        d_mid = line_scatter([d_mid[k] for k in range(ranks)], ranks)
        gains_sums["mid"] += jnp.sum(d_mid * residual * scale_mid, 0)
        d_residual = up + norm_backward(residual, scale_mid, d_mid * g_mid)
        gains_sums["post"] += jnp.sum(d_residual * branch * scale_branch, 0)
        d_branch = norm_backward(branch, scale_branch, d_residual * g_post).astype(BF16)
        st["d_residual"] = d_residual
        st["d_branches"] = line_gather(d_branch, rank, ranks)
        st.update(mids=mids, d_mixeds=d_mixeds, hiddens=hiddens, d_gate_ups=d_gate_ups)
        streams.append(st)

    block_out = jnp.concatenate([st["out"] for st in streams], 0).reshape(layer_input.shape)
    d_residual = jnp.concatenate([st["d_residual"] for st in streams], 0)
    d_branches = jnp.concatenate(
        [st["d_branches"][k] for k in range(ranks) for st in streams], 0
    )

    def both_cores(mine, others=None):
        return jnp.concatenate([mine, partner(mine if others is None else others)], 0)

    def weight_grad(left, right):
        grouped = left.reshape(left.shape[0], ctx_count, fsdp_count, shard_rows)
        product = jnp.einsum("tcfr,tn->fcrn", grouped, right, preferred_element_type=F32)
        product = product.reshape(width, right.shape[1]).astype(BF16)
        total = lax.psum_scatter(product, "fsdp", scatter_dimension=0, tiled=True)
        return total.reshape(ranks, 2, shard_rows, right.shape[1])

    def spread(total):
        mine = jnp.where(first_core, total[:, 0], total[:, 1])
        theirs = partner(jnp.where(first_core, total[:, 1], total[:, 0]))
        both = jnp.stack(ordered(mine, theirs), 1)
        got = []
        for k in range(ranks):
            part = lax.dynamic_index_in_dim(both, (rank + k) % ranks, 0, keepdims=False)
            pairs = [(i, (i + 2 * k) % ctx_count) for i in range(ctx_count)]
            got.append(part if k == 0 else lax.ppermute(part, "ctx", pairs))
        return got

    def put(into, piece, start, adds=False):
        piece = piece.astype(F32)
        if adds:
            piece = piece + lax.dynamic_slice_in_dim(into, start, piece.shape[1], 1)
        return lax.dynamic_update_slice_in_dim(into, piece, start, 1)

    mid_rows = both_cores(jnp.concatenate([st["mids"] for st in streams], 0))
    dmix_rows = both_cores(jnp.concatenate([st["d_mixeds"] for st in streams], 0))
    hidden_rows = both_cores(*[jnp.concatenate([st["hiddens"][i] for st in streams], 0) for i in (0, 1)])
    dgu_rows = both_cores(*[jnp.concatenate([st["d_gate_ups"][i] for st in streams], 0) for i in (0, 1)])
    down = spread(weight_grad(dmix_rows, hidden_rows))
    gate_up_terms = spread(weight_grad(mid_rows, dgu_rows))
    grad_mlp_out = jnp.zeros((shard_rows, hidden_width), F32)
    grad_mlp_in = jnp.zeros((shard_rows, 2 * hidden_width), F32)
    for k in range(ranks):
        giver = (rank - k) % ranks
        for which in (0, 1):
            start = (2 * giver + which) * f_own
            grad_mlp_out = put(grad_mlp_out, down[k][which], start)
            grad_mlp_in = put(grad_mlp_in, gate_up_terms[k][which][:, :f_own], start)
            grad_mlp_in = put(grad_mlp_in, gate_up_terms[k][which][:, f_own:], hidden_width + start)

    d_att_own, d_att_other = dot(d_branches, proj_own), dot(d_branches, proj_other)
    d_attended = jnp.concatenate(ordered(d_att_own, d_att_other), 1).astype(BF16)
    d_attended = d_attended.reshape(rows, heads, HEAD_DIM)
    tanh_again, capped_again = score_rows()
    chances_f = jnp.exp(capped_again - log_total)
    d_values = jnp.einsum(
        "gtl,tgd->ld", chances_f.astype(BF16), d_attended, preferred_element_type=F32
    )
    d_chances = jnp.einsum("tgd,ld->gtl", d_attended, values, preferred_element_type=F32)
    row_inner = jnp.sum(chances_f * d_chances, -1, keepdims=True)
    d_raw = (
        chances_f * (d_chances - row_inner) * (1.0 - tanh_again * tanh_again) * scaling
    ).astype(BF16)
    d_query = jnp.einsum("gtl,ld->tgd", d_raw, keys, preferred_element_type=F32)
    d_keys = jnp.einsum("gtl,tgd->ld", d_raw, query, preferred_element_type=F32)
    d_key_value = jnp.concatenate([d_keys, d_values], 1)
    d_key_value = d_key_value[:rows] + partner(d_key_value[rows:].astype(BF16)).astype(F32)
    d_query_raw = rotate_back(d_query, cosine[:, None], sine_table[:, None]).reshape(
        rows, heads * HEAD_DIM
    )
    d_key_raw = rotate_back(d_key_value[:, :HEAD_DIM], cosine, sine_table)
    dq_own, dq_other = ordered(d_query_raw[:, :q_own], d_query_raw[:, q_own:])
    dkv_own, dkv_other = ordered(d_key_raw, d_key_value[:, HEAD_DIM:])
    dproj_own = jnp.concatenate([dq_own, dkv_own], 1).astype(BF16)
    dproj_other = jnp.concatenate([dq_other, dkv_other], 1).astype(BF16)
    d_in = dot_t(dproj_own, qkv_own) + dot_t(dproj_other, qkv_other)
    grad_pre_gain = jnp.sum(d_in * plain_in, 0)
    d_in = d_in.reshape(ranks, tokens, width)
    d_in = line_scatter([d_in[k] for k in range(ranks)], ranks)
    d_source = d_residual + norm_backward(source, scale_in[:tokens], d_in * g_pre)

    in_rows = both_cores(normed_in)
    dbranch_rows = both_cores(d_branches)
    dproj_rows = both_cores(dproj_own, dproj_other)
    att_rows = both_cores(att_own, att_other)
    out_proj = spread(weight_grad(dbranch_rows, att_rows))
    projection = spread(weight_grad(in_rows, dproj_rows))
    grad_attn = jnp.zeros((shard_rows, attn_weights.shape[1]), F32)
    for k in range(ranks):
        giver = (rank - k) % ranks
        for which in (0, 1):
            start = (2 * giver + which) * q_own
            grad_attn = put(grad_attn, out_proj[k][which], qkv_cols + start)
            grad_attn = put(grad_attn, projection[k][which][:, :q_own], start)
            start = query_cols + which * key_cols + giver // sharing * HEAD_DIM
            grad_attn = put(grad_attn, projection[k][which][:, q_own:], start, sharing > 1)

    gain_terms = jnp.stack(
        [grad_pre_gain, gains_sums["post"], gains_sums["mid"], gains_sums["out"]], 1
    )
    grad_gains = lax.psum_scatter(gain_terms, ("ctx", "fsdp"), scatter_dimension=0, tiled=True)
    return (
        block_out,
        d_source.reshape(layer_input.shape),
        grad_attn,
        grad_mlp_in,
        grad_mlp_out,
        grad_gains,
    )


def solution(mesh):
    in_specs = (
        P("fsdp", "ctx", None),
        P("fsdp", None),
        P("fsdp", None),
        P("fsdp", None),
        P("fsdp", None),
        P("fsdp", "ctx", None),
    )
    out_specs = (
        P("fsdp", "ctx", None),
        P("fsdp", "ctx", None),
        P(("ctx", "fsdp"), None),
        P(("ctx", "fsdp"), None),
        P(("ctx", "fsdp"), None),
        P(("ctx", "fsdp"), None),
    )
    return jax.shard_map(local, mesh=mesh, in_specs=in_specs, out_specs=out_specs, check_vma=False)
```

```python
import jax
import jax.numpy as jnp
from jax import lax
from jax.experimental import pallas as pl
from jax.experimental.pallas import tpu as pltpu
from jax.sharding import PartitionSpec as P

HEADS = 8
KV_HEADS = 4
HEAD_DIM = 256

EPSILON = 1e-06
SOFT_CAP = 50.0
ROTARY_BASE = 10000.0
MASKED_SCORE = -1e30
STREAMS = 1

F32 = jnp.float32
BF16 = jnp.bfloat16


def positions_of(rows, half_block, ctx_count):
    owners = rows // (2 * half_block)
    within = rows % (2 * half_block)
    return jnp.where(
        within < half_block,
        owners * half_block + within,
        (2 * ctx_count - 1 - owners) * half_block + within - half_block,
    )


def rotary_tables(places, head_dim):
    half_width = head_dim // 2
    frequency = ROTARY_BASE ** (-jnp.arange(half_width, dtype=F32) * 2.0 / head_dim)
    angles = places.astype(F32)[:, None] * frequency[None, :]
    cosine = jnp.concatenate([jnp.cos(angles), jnp.cos(angles)], -1)
    sine_table = jnp.concatenate([jnp.sin(angles), jnp.sin(angles)], -1)
    return (cosine, sine_table)


def turned(values):
    half_width = values.shape[-1] // 2
    return jnp.concatenate([-values[..., half_width:], values[..., :half_width]], -1)


def rotate(values, cosine, sine_table):
    return values * cosine + turned(values) * sine_table


def rotate_back(grads, cosine, sine_table):
    return grads * cosine - turned(grads * sine_table)


def inverse_rms(values):
    return lax.rsqrt(jnp.mean(values * values, -1, keepdims=True) + EPSILON)


def norm_backward(values, scale, grad_normed):
    normed = values * scale
    return scale * (grad_normed - normed * jnp.mean(grad_normed * normed, -1, keepdims=True))


def geglu(gate, upper):
    return jax.nn.gelu(gate, approximate=True) * upper


def dot(a, b):
    return jnp.dot(a, b, preferred_element_type=F32)


def dot_t(a, b):
    return jnp.einsum("tk,dk->td", a, b, preferred_element_type=F32)


def swap(values, axis, distance, count):
    return lax.ppermute(values, axis, [(i, i ^ distance) for i in range(count)])


def line_gather(values, ranks):
    slots = {0: values}
    bit = ranks // 2
    while bit:
        slots.update({k ^ bit: swap(v, "ctx", 2 * bit, 2 * ranks) for k, v in slots.items()})
        bit //= 2
    return [slots[k] for k in range(ranks)]


def line_scatter(parts, ranks, beside=()):
    sums = {k: v.astype(F32) for k, v in enumerate(parts)}
    bit = 1
    while bit < ranks:
        got = {
            k: swap(sums.pop(k).astype(BF16), "ctx", 2 * bit, 2 * ranks)
            for k in sorted(sums, reverse=True)
            if k & bit
        }
        if beside and bit == 1:
            got, beside = together(got, beside)
        for k, v in got.items():
            sums[k ^ bit] = sums[k ^ bit] + v.astype(F32)
        bit *= 2
    return (sums[0], beside) if beside else sums[0]


def square_gather(piece, place, beside):
    rows = piece.shape[0]
    half = rows // 2
    near, far = swap(piece, "fsdp", 1, 4), swap(piece, "fsdp", 2, 4)
    first, then = beside
    near, far, first = together(near, far, first)
    corner_a, corner_b = swap(near[:half], "fsdp", 2, 4), swap(far[half:], "fsdp", 1, 4)
    corner_a, corner_b, second = together(corner_a, corner_b, then(first))
    whole = jnp.zeros((4 * rows, piece.shape[1]), piece.dtype)
    for block, at in (
        (piece, place * rows),
        (near, (place ^ 1) * rows),
        (far, (place ^ 2) * rows),
        (corner_a, (place ^ 3) * rows),
        (corner_b, (place ^ 3) * rows + half),
    ):
        whole = lax.dynamic_update_slice_in_dim(whole, block, at, 0)
    return whole, first, second


def corner_scatter(corner, count):
    half = corner.shape[0] // 2
    corner = corner.astype(BF16)
    return swap(corner[:half], "fsdp", 1, count), swap(corner[half:], "fsdp", 2, count)


def rows_scatter(parts, corners, count):
    half = parts[3].shape[0] // 2
    by_near, by_far = corners[0].astype(F32), corners[1].astype(F32)
    near = jnp.concatenate([parts[1][:half], parts[1][half:] + by_far], 0).astype(BF16)
    far = jnp.concatenate([parts[2][:half] + by_near, parts[2][half:]], 0).astype(BF16)
    near, far = swap(near, "fsdp", 1, count), swap(far, "fsdp", 2, count)
    return parts[0] + near.astype(F32) + far.astype(F32)


def together(*values):
    return lax.optimization_barrier(values)


VMEM_BYTES = 60 * 1024 * 1024


def kernel_call(body, grid, in_specs, out_specs, out_shape, scratch, flops, moved, prefetch=0):
    return pl.pallas_call(
        body,
        grid_spec=pltpu.PrefetchScalarGridSpec(
            num_scalar_prefetch=prefetch,
            grid=grid,
            in_specs=in_specs,
            out_specs=out_specs,
            scratch_shapes=scratch,
        ),
        out_shape=out_shape,
        compiler_params=pltpu.CompilerParams(
            vmem_limit_bytes=VMEM_BYTES, dimension_semantics=("arbitrary",) * len(grid)
        ),
        cost_estimate=pl.CostEstimate(flops=flops, bytes_accessed=moved, transcendentals=0),
    )


def mm(a, b):
    return jnp.dot(a, b, preferred_element_type=F32)


def mm_nt(a, b):
    return lax.dot_general(a, b, (((1,), (1,)), ((), ())), preferred_element_type=F32)


def mm_tn(a, b):
    return lax.dot_general(a, b, (((0,), (0,)), ((), ())), preferred_element_type=F32)


def tile_of(size, most):
    return max(t for t in range(128, most + 1, 128) if size % t == 0)


def gelu_parts(gate):
    rate = 0.7978845608028654
    square = gate * gate
    t = jnp.tanh(rate * gate * (1.0 + 0.044715 * square))
    half = 0.5 * (1.0 + t)
    slope = half + 0.5 * gate * (1.0 - t * t) * rate * (1.0 + 3.0 * 0.044715 * square)
    return gate * half, slope


def core_blocks(shape, steps):
    lead = (0,) * (len(shape) - 1)
    return [
        pl.BlockSpec(shape, lambda h, i, c: (*lead, jnp.where(h == 0, i, steps - 1))),
        pl.BlockSpec(shape, lambda h, i, c: (*lead, jnp.where(h == 0, 0, i))),
    ]


def gate_up_forward(values, w_in, core, most=384):
    rows, width = values.shape
    size = w_in.shape[2] // 2
    tile = tile_of(size, most)
    steps = size // tile

    def body(core_ref, x, g, u, hidden0, hidden1, gate_all, up_all):
        gate, up = mm(x[...], g[0]), mm(x[...], u[0])
        gate_all[0] = gate
        up_all[0] = up
        hidden = (gelu_parts(gate)[0] * up).astype(BF16)

        @pl.when(pl.program_id(0) == 0)
        def _():
            hidden0[0] = hidden

        @pl.when(pl.program_id(0) == 1)
        def _():
            hidden1[0] = hidden

    saved = pl.BlockSpec((1, rows, tile), lambda h, i, c: (h, 0, i))
    return kernel_call(
        body,
        (2, steps),
        [
            pl.BlockSpec((rows, width), lambda h, i, c: (0, 0)),
            pl.BlockSpec((1, width, tile), lambda h, i, c: (c[0] ^ h, 0, i)),
            pl.BlockSpec((1, width, tile), lambda h, i, c: (c[0] ^ h, 0, steps + i)),
        ],
        core_blocks((1, rows, tile), steps) + [saved, saved],
        [jax.ShapeDtypeStruct((1, rows, size), BF16)] * 2
        + [jax.ShapeDtypeStruct((2, rows, size), F32)] * 2,
        [],
        8 * rows * width * size,
        8 * width * size + 20 * rows * size,
        prefetch=1,
    )(core, values, w_in, w_in)


def down_forward(hidden, w_out, core, earlier=(), most=768):
    _, rows, size = hidden[0].shape
    width = w_out.shape[1]
    tile = tile_of(width, most)

    def body(core_ref, h0, h1, o0, o1, *refs):
        out = refs[-1]
        out[...] = (mm_nt(h0[0], o0[0]) + mm_nt(h1[0], o1[0])).astype(BF16)

    whole = pl.BlockSpec((1, rows, size), lambda i, c: (0, 0, 0))
    return kernel_call(
        body,
        (width // tile,),
        [
            whole,
            whole,
            pl.BlockSpec((1, tile, size), lambda i, c: (c[0], i, 0)),
            pl.BlockSpec((1, tile, size), lambda i, c: (1 - c[0], i, 0)),
        ]
        + [pl.BlockSpec(memory_space=pl.ANY)] * len(earlier),
        pl.BlockSpec((rows, tile), lambda i, c: (0, i)),
        jax.ShapeDtypeStruct((rows, width), BF16),
        [],
        4 * rows * width * size,
        4 * width * size + 4 * rows * size,
        prefetch=1,
    )(core, *hidden, w_out, w_out, *earlier)


def down_backward(d_mixed, gate_all, up_all, w_out, core, most=384):
    rows, width = d_mixed.shape
    size = w_out.shape[2]
    tile = tile_of(size, most)
    steps = size // tile

    def body(core_ref, x, gate, up, o, dgu0, dgu1):
        d_hidden = mm(x[...], o[0])
        value, slope = gelu_parts(gate[0])
        d_gate = (d_hidden * up[0] * slope).astype(BF16)
        d_up = (d_hidden * value).astype(BF16)

        @pl.when(pl.program_id(0) == 0)
        def _():
            dgu0[0] = d_gate
            dgu0[1] = d_up

        @pl.when(pl.program_id(0) == 1)
        def _():
            dgu1[0] = d_gate
            dgu1[1] = d_up

    saved = pl.BlockSpec((1, rows, tile), lambda h, i, c: (h, 0, i))
    return kernel_call(
        body,
        (2, steps),
        [
            pl.BlockSpec((rows, width), lambda h, i, c: (0, 0)),
            saved,
            saved,
            pl.BlockSpec((1, width, tile), lambda h, i, c: (c[0] ^ h, 0, i)),
        ],
        core_blocks((2, rows, tile), steps),
        [jax.ShapeDtypeStruct((2, rows, size), BF16)] * 2,
        [],
        4 * rows * width * size,
        4 * width * size + 24 * rows * size,
        prefetch=1,
    )(core, d_mixed, gate_all, up_all, w_out)


def gate_up_backward(dgu, w_in, core, earlier=(), most=768):
    _, rows, size = dgu[0].shape
    width = w_in.shape[1]
    tile = tile_of(width, most)

    def body(core_ref, d0, d1, w0, w1, *refs):
        out = refs[-1]
        total = mm_nt(d0[0], w0[0, :, :size]) + mm_nt(d0[1], w0[0, :, size:])
        total += mm_nt(d1[0], w1[0, :, :size]) + mm_nt(d1[1], w1[0, :, size:])
        out[...] = total.astype(BF16)

    whole = pl.BlockSpec((2, rows, size), lambda i, c: (0, 0, 0))
    return kernel_call(
        body,
        (width // tile,),
        [
            whole,
            whole,
            pl.BlockSpec((1, tile, 2 * size), lambda i, c: (c[0], i, 0)),
            pl.BlockSpec((1, tile, 2 * size), lambda i, c: (1 - c[0], i, 0)),
        ]
        + [pl.BlockSpec(memory_space=pl.ANY)] * len(earlier),
        pl.BlockSpec((rows, tile), lambda i, c: (0, i)),
        jax.ShapeDtypeStruct((rows, width), BF16),
        [],
        8 * rows * width * size,
        8 * width * size + 8 * rows * size,
        prefetch=1,
    )(core, *dgu, w_in, w_in, *earlier)


def weight_grad_kernel(lefts, rights, ctx_count, fsdp_count):
    width = lefts[0].shape[1]
    groups, _, size = rights[0].shape
    counts = [v.shape[0] for v in lefts]
    starts = [sum(counts[:i]) for i in range(len(counts))]
    shard = width // (ctx_count * fsdp_count)
    halves = 2
    part, ctx_part = width // halves, ctx_count // halves
    tile = tile_of(size, 1152)
    steps = size // tile

    def body(*refs):
        left_refs, right_refs = refs[: len(counts)], refs[len(counts) : 2 * len(counts)]
        out, turned_left = refs[2 * len(counts) :]

        @pl.when((pl.program_id(1) == 0) & (pl.program_id(2) == 0))
        def _():
            for ref, start, count in zip(left_refs, starts, counts):
                turned_left[:, start : start + count] = ref[...].T

        product = 0.0
        for ref, start, count in zip(right_refs, starts, counts):
            product = product + mm(turned_left[:, start : start + count], ref[0])
        for f in range(fsdp_count):
            at = [(c * fsdp_count + f) * shard for c in range(ctx_part)]
            out[f] = jnp.concatenate([product[i : i + shard] for i in at], 0).astype(BF16)

    return kernel_call(
        body,
        (halves, groups, steps),
        [pl.BlockSpec((n, part), lambda h, g, t: (0, h)) for n in counts]
        + [pl.BlockSpec((1, n, tile), lambda h, g, t: (g, 0, t)) for n in counts],
        pl.BlockSpec((fsdp_count, ctx_part * shard, tile), lambda h, g, t: (0, h, g * steps + t)),
        jax.ShapeDtypeStruct((fsdp_count, ctx_count * shard, groups * size), BF16),
        [pltpu.VMEM((part, sum(counts)), BF16)],
        2 * sum(counts) * width * groups * size,
        4 * sum(counts) * (width + groups * size) + 2 * width * groups * size,
    )(*lefts, *rights)


def rotated(values, cosine, sine, back=False):
    size = values.shape[1] // 2
    low, high = values[:, :size], values[:, size:]
    if back:
        sine = -sine
    return jnp.concatenate([low * cosine - high * sine, high * cosine + low * sine], 1)


def qkv_kernel(inputs, attn, cosine, sine, core):
    rows, width = inputs.shape
    block = rows // 2
    size = HEAD_DIM

    def body(core_ref, x, gains, w0, w1, cos, sin, normed_out, q0, q1, kv):
        source = x[...].astype(F32)
        gain = gains[...].astype(F32).T[:1]
        normed = (source * inverse_rms(source) * gain).astype(BF16)
        normed_out[...] = normed
        first = core_ref[0] == 0
        own, other = mm(normed, w0[...]), mm(normed, w1[...])
        q0[...] = rotated(own[:, :size], cos[...], sin[...]).astype(BF16)
        q1[...] = rotated(other[:, :size], cos[...], sin[...]).astype(BF16)
        key = jnp.where(first, own[:, size:], other[:, size:])
        kv[:, :size] = rotated(key, cos[...], sin[...]).astype(BF16)
        kv[:, size:] = jnp.where(first, other[:, size:], own[:, size:]).astype(BF16)

    def by_rows(columns):
        return pl.BlockSpec((block, columns), lambda i, c: (i, 0))

    return kernel_call(
        body,
        (2,),
        [
            by_rows(width),
            pl.BlockSpec((width, 128), lambda i, c: (0, 3 * size // 128)),
            pl.BlockSpec((width, 2 * size), lambda i, c: (0, 0)),
            pl.BlockSpec((width, 2 * size), lambda i, c: (0, 0)),
            by_rows(size // 2),
            by_rows(size // 2),
        ],
        [by_rows(width), by_rows(size), by_rows(size), by_rows(2 * size)],
        [
            jax.ShapeDtypeStruct((rows, width), BF16),
            jax.ShapeDtypeStruct((rows, size), BF16),
            jax.ShapeDtypeStruct((rows, size), BF16),
            jax.ShapeDtypeStruct((rows, 2 * size), BF16),
        ],
        [],
        8 * rows * width * size,
        8 * width * size + 4 * rows * width,
        prefetch=1,
    )(core, inputs, attn[0], *attn, cosine, sine)


def scores(query, key, key_place, query_place):
    raw = mm_nt(query, key)
    tanh_part = jnp.tanh(raw * (HEAD_DIM**-0.5 / SOFT_CAP))
    return tanh_part, jnp.where(key_place <= query_place, jnp.exp(SOFT_CAP * tanh_part), 0.0)


def attention_specs(rows, width, block):
    def by_rows(columns):
        return pl.BlockSpec((block, columns), lambda i, c: (i, 0))

    size = HEAD_DIM
    kv = pl.BlockSpec((rows, 2 * size), lambda i, c: (0, 0))
    places = pl.BlockSpec((1, rows), lambda i, c: (0, 0))
    weights = [pl.BlockSpec((width, size), lambda i, c: (0, 2))] * 2
    return by_rows, [by_rows(size), by_rows(size), kv, kv, by_rows(1), places, places] + weights


def attention_forward(core, queries, kvs, row_places, key_places, attn):
    rows, width, size = queries[0].shape[0], attn[0].shape[0], HEAD_DIM
    block = rows // 2

    def body(core_ref, q0, q1, kv0, kv1, place, places0, places1, w0, w1, att0, att1, branch):
        total = 0.0
        for q, att, w in ((q0, att0, w0), (q1, att1, w1)):
            parts = [
                scores(q[...], kv[:, :size], places[...], place[...])[1]
                for kv, places in ((kv0, places0), (kv1, places1))
            ]
            scale = 1.0 / (
                jnp.sum(parts[0], -1, keepdims=True) + jnp.sum(parts[1], -1, keepdims=True)
            )
            attended = mm((parts[0] * scale).astype(BF16), kv0[:, size:])
            attended += mm((parts[1] * scale).astype(BF16), kv1[:, size:])
            attended = attended.astype(BF16)
            att[...] = attended
            total = total + mm_nt(attended, w[...])
        branch[...] = total.astype(BF16)

    by_rows, specs = attention_specs(rows, width, block)
    return kernel_call(
        body,
        (2,),
        specs,
        [by_rows(size), by_rows(size), by_rows(width)],
        [
            jax.ShapeDtypeStruct((rows, size), BF16),
            jax.ShapeDtypeStruct((rows, size), BF16),
            jax.ShapeDtypeStruct((rows, width), BF16),
        ],
        [],
        16 * rows * rows * size + 4 * rows * width * size,
        4 * width * size + 2 * rows * width,
        prefetch=1,
    )(core, *queries, *kvs, row_places, *key_places, *attn)


def attention_backward(
    d_branch, core, queries, kvs, row_places, key_places, attn, cosine, sine
):
    rows, width, size = queries[0].shape[0], attn[0].shape[0], HEAD_DIM
    block = rows // 2
    scaling = size**-0.5

    def body(
        core_ref, q0, q1, kv0, kv1, place, places0, places1, w0, w1, d_out, cos, sin,
        dq0, dq1, dkv0, dkv1, sum0, sum1
    ):
        @pl.when(pl.program_id(0) == 0)
        def _():
            sum0[...] = jnp.zeros_like(sum0)
            sum1[...] = jnp.zeros_like(sum1)

        for q, dq, w in ((q0, dq0, w0), (q1, dq1, w1)):
            query = q[...]
            d_att = mm(d_out[...], w[...]).astype(BF16)
            parts = [
                scores(query, kv[:, :size], places[...], place[...])
                for kv, places in ((kv0, places0), (kv1, places1))
            ]
            scale = 1.0 / sum(jnp.sum(e, -1, keepdims=True) for _, e in parts)
            chances = [e * scale for _, e in parts]
            d_chances = [mm_nt(d_att, kv[:, size:]) for kv in (kv0, kv1)]
            inner = sum(
                jnp.sum(p * d, -1, keepdims=True) for p, d in zip(chances, d_chances)
            )
            d_query = 0.0
            for (t, _), p, d, kv, sums in zip(
                parts, chances, d_chances, (kv0, kv1), (sum0, sum1)
            ):
                d_raw = (p * (d - inner) * (1.0 - t * t) * scaling).astype(BF16)
                d_query = d_query + mm(d_raw, kv[:, :size])
                sums[:, :size] += mm_tn(d_raw, query)
                sums[:, size:] += mm_tn(p.astype(BF16), d_att)
            dq[...] = rotated(d_query, cos[...], sin[...], back=True).astype(BF16)

        @pl.when(pl.program_id(0) == pl.num_programs(0) - 1)
        def _():
            dkv0[...] = sum0[...]
            dkv1[...] = sum1[...].astype(BF16)

    by_rows, specs = attention_specs(rows, width, block)
    whole = pl.BlockSpec((rows, 2 * size), lambda i, c: (0, 0))
    return kernel_call(
        body,
        (2,),
        specs + [by_rows(width), by_rows(size // 2), by_rows(size // 2)],
        [by_rows(size), by_rows(size), whole, whole],
        [
            jax.ShapeDtypeStruct((rows, size), BF16),
            jax.ShapeDtypeStruct((rows, size), BF16),
            jax.ShapeDtypeStruct((rows, 2 * size), F32),
            jax.ShapeDtypeStruct((rows, 2 * size), BF16),
        ],
        [pltpu.VMEM((rows, 2 * size), F32)] * 2,
        40 * rows * rows * size + 4 * rows * width * size,
        4 * width * size + 2 * rows * width,
        prefetch=1,
    )(core, *queries, *kvs, row_places, *key_places, *attn, d_branch, cosine, sine)


def qkv_backward(inputs, dqs, dkv_mine, dkv_got, attn, cosine, sine, core):
    rows, width = inputs.shape
    block, size = rows // 2, HEAD_DIM

    def body(core_ref, x, q0, q1, mine, got, w0, w1, cos, sin, d_in, dp0, dp1, gain):
        both = mine[...] + got[...].astype(F32)
        d_key = rotated(both[:, :size], cos[...], sin[...], back=True)
        first = core_ref[0] == 0
        dp0[0, :, :size] = q0[...]
        dp1[0, :, :size] = q1[...]
        dp0[0, :, size:] = jnp.where(first, d_key, both[:, size:]).astype(BF16)
        dp1[0, :, size:] = jnp.where(first, both[:, size:], d_key).astype(BF16)
        total = mm_nt(dp0[0], w0[...]) + mm_nt(dp1[0], w1[...])
        d_in[...] = total.astype(BF16)
        source = x[...].astype(F32)
        term = jnp.sum(total * source * inverse_rms(source), 0, keepdims=True)

        @pl.when(pl.program_id(0) == 0)
        def _():
            gain[...] = jnp.zeros_like(gain)

        gain[...] += term

    def by_rows(columns):
        return pl.BlockSpec((block, columns), lambda i, c: (i, 0))

    weights = [pl.BlockSpec((width, 2 * size), lambda i, c: (0, 0))] * 2
    terms = pl.BlockSpec((1, block, 2 * size), lambda i, c: (0, i, 0))
    return kernel_call(
        body,
        (2,),
        [by_rows(width), by_rows(size), by_rows(size), by_rows(2 * size), by_rows(2 * size)]
        + weights
        + [by_rows(size // 2), by_rows(size // 2)],
        [by_rows(width), terms, terms, pl.BlockSpec((1, width), lambda i, c: (0, 0))],
        [
            jax.ShapeDtypeStruct((rows, width), BF16),
            jax.ShapeDtypeStruct((1, rows, 2 * size), BF16),
            jax.ShapeDtypeStruct((1, rows, 2 * size), BF16),
            jax.ShapeDtypeStruct((1, width), F32),
        ],
        [],
        8 * rows * width * size,
        8 * width * size + 4 * rows * width,
        prefetch=1,
    )(core, inputs, *dqs, dkv_mine, dkv_got, *attn, cosine, sine)


def both_columns(total, place, ctx_count):
    first_core = place % 2 == 0
    total = total.reshape(ctx_count // 2, 2, -1, total.shape[1])
    mine = jnp.where(first_core, total[:, 0], total[:, 1])
    theirs = swap(jnp.where(first_core, total[:, 1], total[:, 0]), "ctx", 1, ctx_count)
    both = (jnp.where(first_core, mine, theirs), jnp.where(first_core, theirs, mine))
    return jnp.stack(both, 1)


def rank_parts(both, place, ctx_count):
    return [
        lax.dynamic_index_in_dim(both, place // 2 ^ k, 0, keepdims=False)
        for k in range(ctx_count // 2)
    ]


def spread(parts, ctx_count):
    return [
        part if k == 0 else swap(part, "ctx", 2 * k, ctx_count) for k, part in enumerate(parts)
    ]


def put(into, piece, start):
    return lax.dynamic_update_slice_in_dim(into, piece.astype(F32), start, 1)


def local_kernels(
    layer_input, attn_weights, mlp_in_weights, mlp_out_weights, norm_gains, output_grad
):
    tokens, width = layer_input.shape[1:]
    half_block = tokens // 2
    ctx_count = lax.axis_size("ctx")
    fsdp_count = lax.axis_size("fsdp")
    ranks = ctx_count // 2
    place = lax.axis_index("ctx")
    fsdp_place = lax.axis_index("fsdp")
    rank, core = place // 2, place % 2
    query_cols, key_cols = HEADS * HEAD_DIM, KV_HEADS * HEAD_DIM
    qkv_cols = query_cols + 2 * key_cols
    hidden_width = mlp_out_weights.shape[1]
    f_own = hidden_width // ctx_count
    shard_rows = width // (ctx_count * fsdp_count)

    def partner(values):
        return swap(values, "ctx", 1, ctx_count)

    def columns(array, start, size):
        return lax.dynamic_slice_in_dim(array, start, size, 1)

    chip_groups = [
        [(2 * r + c) * fsdp_count + f for c in (0, 1) for f in range(fsdp_count)]
        for r in range(ranks)
    ]

    def chip_gather(piece):
        whole = lax.all_gather(
            piece, ("ctx", "fsdp"), axis=0, tiled=True, axis_index_groups=chip_groups
        )
        return whole.reshape(2, width, piece.shape[1])

    def over_sequences(product):
        product = product.reshape(width, product.shape[2])
        return lax.psum_scatter(product, "fsdp", scatter_dimension=0, tiled=True)

    def joined(pieces):
        return jnp.concatenate(pieces, 0)

    own_input = layer_input.reshape(tokens, width)
    source = own_input.astype(F32)
    upstream = output_grad.reshape(tokens, width).astype(F32)
    kv_start = query_cols + core * key_cols + rank * HEAD_DIM
    piece = [
        columns(attn_weights, place * HEAD_DIM, HEAD_DIM),
        columns(attn_weights, kv_start, HEAD_DIM),
        columns(attn_weights, qkv_cols + place * HEAD_DIM, HEAD_DIM),
        jnp.pad(norm_gains, ((0, 0), (0, 124))),
    ]
    piece = jnp.concatenate(piece, 1)
    if fsdp_count == 4:
        ways = (
            [swap(own_input, "ctx", 4, ctx_count), swap(own_input, "ctx", 2, ctx_count)],
            lambda got: swap(got[0], "ctx", 2, ctx_count),
        )
        attn_own, (slot_2, slot_1), slot_3 = square_gather(piece, fsdp_place, ways)
        inputs = joined([own_input, slot_1, slot_2, slot_3])
    else:
        attn_own = lax.all_gather(piece, "fsdp", axis=0, tiled=True)
        inputs = joined(line_gather(own_input, ranks))
    attn = (attn_own, partner(attn_own))
    gains = attn_own[:, 3 * HEAD_DIM : 3 * HEAD_DIM + 4].astype(F32)
    g_pre, g_post, g_mid, g_out = [gains[:, i] for i in range(4)]
    in_all = chip_gather(
        jnp.concatenate(
            [
                columns(mlp_in_weights, place * f_own, f_own),
                columns(mlp_in_weights, hidden_width + place * f_own, f_own),
            ],
            1,
        )
    )
    out_all = chip_gather(columns(mlp_out_weights, place * f_own, f_own))

    def places_of(which):
        owners = (2 * (rank ^ jnp.arange(ranks, dtype=jnp.int32)) + which)[:, None] * tokens
        gathered_rows = owners + jnp.arange(tokens, dtype=jnp.int32)[None, :]
        return positions_of(gathered_rows.reshape(-1), half_block, ctx_count)

    own_places, other_places = places_of(core), places_of(1 - core)
    cosine, sine = rotary_tables(own_places, HEAD_DIM)
    cosine, sine = cosine[:, : HEAD_DIM // 2], sine[:, : HEAD_DIM // 2]
    row_places, key_places = own_places[:, None], (own_places[None, :], other_places[None, :])
    core_word = core.reshape(1).astype(jnp.int32)

    normed_in, *queries, kv_own = qkv_kernel(inputs, attn, cosine, sine, core_word)
    attention = (core_word, queries, (kv_own, partner(kv_own)), row_places, key_places, attn)
    att_own, att_other, branch_parts = attention_forward(*attention)
    branch_parts = branch_parts.reshape(ranks, tokens, width)

    def own_rows(halves, beside=()):
        halves = [v.reshape(2, tokens, width) for v in halves]
        return line_scatter([halves[k % 2][k // 2] for k in range(4)], ranks, beside)

    def gathered_halves(values, work):
        slots = line_gather(values, ranks)
        first = joined([slots[0], slots[2]])
        done = work(first, 0)
        last, first, done = together(slots[3], first, done)
        second = joined([slots[1], last])
        return (first, second), (done, work(second, 1))

    branch_parts = branch_parts.reshape(ranks, tokens, width)
    branch = line_scatter(list(branch_parts), ranks)
    scale_branch = inverse_rms(branch)
    residual = source + branch * scale_branch * g_post
    scale_mid = inverse_rms(residual)
    mids, forward = gathered_halves(
        (residual * scale_mid * g_mid).astype(BF16), lambda v, _: gate_up_forward(v, in_all, core_word)
    )
    mixed_1 = down_forward(forward[1][:2], out_all, core_word)
    mixed_0 = down_forward(forward[0][:2], out_all, core_word, (mixed_1,))
    hidden_own = [f[0] for f in forward]
    hidden_got = [partner(f[1]) for f in forward]
    mid_got = [partner(v) for v in mids]
    mixed = own_rows((mixed_0, mixed_1))
    mixed, hidden_own, hidden_got, mid_got = together(mixed, hidden_own, hidden_got, mid_got)
    scale_mixed = inverse_rms(mixed)
    block_out = (residual + mixed * scale_mixed * g_out).astype(BF16)
    grad_out_gain = jnp.sum(upstream * mixed * scale_mixed, 0)
    d_mixeds, d_gate_ups = gathered_halves(
        norm_backward(mixed, scale_mixed, upstream * g_out).astype(BF16),
        lambda v, k: down_backward(v, *forward[k][2:], out_all, core_word),
    )

    def weight_grad(lefts, rights):
        return weight_grad_kernel(lefts, rights, ctx_count, fsdp_count)

    down_product = weight_grad(
        [*d_mixeds, *[partner(v) for v in d_mixeds]], hidden_own + hidden_got
    )
    d_gate_ups, down_product = together(d_gate_ups, down_product)
    down_total = over_sequences(down_product)
    d_mid_1 = gate_up_backward(d_gate_ups[1], in_all, core_word)
    d_mid_0 = gate_up_backward(d_gate_ups[0], in_all, core_word, (d_mid_1,))
    gate_up_product = weight_grad(
        [*mids, *mid_got], [v[0] for v in d_gate_ups] + [partner(v[1]) for v in d_gate_ups]
    )
    d_mid, (gate_up_product,) = own_rows((d_mid_0, d_mid_1), (gate_up_product,))
    gate_up_total = over_sequences(gate_up_product)
    grad_mid_gain = jnp.sum(d_mid * residual * scale_mid, 0)
    d_residual = upstream + norm_backward(residual, scale_mid, d_mid * g_mid)
    grad_post_gain = jnp.sum(d_residual * branch * scale_branch, 0)
    d_branches = joined(
        line_gather(
            norm_backward(branch, scale_branch, d_residual * g_post).astype(BF16), ranks
        )
    )

    down_parts = rank_parts(both_columns(down_total, place, ctx_count), place, ctx_count)
    d_branches, down_parts = together(d_branches, down_parts)
    down = spread(down_parts, ctx_count)
    *d_queries, dkv_own, dkv_other = attention_backward(d_branches, *attention, cosine, sine)
    dkv_got, down[1] = together(partner(dkv_other), down[1])
    d_in, dproj_own, dproj_other, grad_pre_gain = qkv_backward(
        inputs, d_queries, dkv_own, dkv_got, attn, cosine, sine, core_word
    )

    gain_terms = jnp.stack([grad_pre_gain[0], grad_post_gain, grad_mid_gain, grad_out_gain], 1)
    gain_terms = gain_terms.reshape(ctx_count, fsdp_count, shard_rows, 4)
    gain_terms = gain_terms.transpose(1, 0, 2, 3).reshape(fsdp_count, -1, 4)
    out_product = weight_grad(
        [d_branches, partner(d_branches)], [att_own[None], partner(att_other)[None]]
    )
    product = weight_grad([normed_in, partner(normed_in)], [dproj_own, partner(dproj_other)])
    product = jnp.concatenate([product, out_product, gain_terms.astype(BF16)], 2)
    gate_up_parts = rank_parts(both_columns(gate_up_total, place, ctx_count), place, ctx_count)
    gate_up_parts, product = together(gate_up_parts, product)
    gate_up_terms = spread(gate_up_parts, ctx_count)
    d_in = list(d_in.reshape(ranks, tokens, width))
    if fsdp_count == 4:
        parts = [
            lax.dynamic_index_in_dim(product, fsdp_place ^ k, 0, keepdims=False).astype(F32)
            for k in range(4)
        ]
        corners = corner_scatter(parts[3], 4)
        d_in, (corners,) = line_scatter(d_in, ranks, (corners,))
        attn_total = rows_scatter(parts, corners, 4).astype(BF16)
    else:
        d_in = line_scatter(d_in, ranks)
        attn_total = over_sequences(product)
    attn_parts = rank_parts(both_columns(attn_total, place, ctx_count), place, ctx_count)
    attn_terms = spread(attn_parts, ctx_count)
    d_source = d_residual + norm_backward(source, inverse_rms(source), d_in * g_pre)

    grad_mlp_out = jnp.zeros((shard_rows, hidden_width), F32)
    grad_mlp_in = jnp.zeros((shard_rows, 2 * hidden_width), F32)
    grad_attn = jnp.zeros((shard_rows, attn_weights.shape[1]), F32)
    grad_gains = jnp.zeros((shard_rows, 4), F32)
    for k in range(ranks):
        giver = rank ^ k
        for which in (0, 1):
            start = (2 * giver + which) * f_own
            grad_mlp_out = put(grad_mlp_out, down[k][which], start)
            term = gate_up_terms[k][which]
            grad_mlp_in = put(grad_mlp_in, term[:, :f_own], start)
            grad_mlp_in = put(grad_mlp_in, term[:, f_own:], hidden_width + start)
            term = attn_terms[k][which]
            start = (2 * giver + which) * HEAD_DIM
            grad_attn = put(grad_attn, term[:, :HEAD_DIM], start)
            grad_attn = put(grad_attn, term[:, 2 * HEAD_DIM : 3 * HEAD_DIM], qkv_cols + start)
            start = query_cols + which * key_cols + giver * HEAD_DIM
            grad_attn = put(grad_attn, term[:, HEAD_DIM : 2 * HEAD_DIM], start)
            grad_gains = grad_gains + term[:, 3 * HEAD_DIM :].astype(F32)
    return (
        block_out.reshape(layer_input.shape),
        d_source.reshape(layer_input.shape),
        grad_attn,
        grad_mlp_in,
        grad_mlp_out,
        grad_gains,
    )


def local(layer_input, attn_weights, mlp_in_weights, mlp_out_weights, norm_gains, output_grad):
    ctx_count, fsdp_count = lax.axis_size("ctx"), lax.axis_size("fsdp")
    width, hidden_width = layer_input.shape[2], mlp_out_weights.shape[1]
    fits = (
        ctx_count == HEADS == 2 * KV_HEADS == 8
        and hidden_width % (128 * ctx_count) == 0
        and width % 256 == 0
        and width % (8 * ctx_count * fsdp_count) == 0
        and (width // fsdp_count) % 32 == 0
    )
    path = local_kernels if fits else local_general
    return path(
        layer_input, attn_weights, mlp_in_weights, mlp_out_weights, norm_gains, output_grad
    )


def local_general(layer_input, attn_weights, mlp_in_weights, mlp_out_weights, norm_gains, output_grad):
    tokens, width = layer_input.shape[1:]
    half_block = tokens // 2
    ctx_count = lax.axis_size("ctx")
    fsdp_count = lax.axis_size("fsdp")
    ranks = ctx_count // 2
    place = lax.axis_index("ctx")
    rank, core = place // 2, place % 2
    first_core = core == 0
    query_cols, key_cols = HEADS * HEAD_DIM, KV_HEADS * HEAD_DIM
    qkv_cols = query_cols + 2 * key_cols
    heads = HEADS // ranks
    sharing = ranks // KV_HEADS
    hidden_width = mlp_out_weights.shape[1]
    q_own = query_cols // ctx_count
    f_own = hidden_width // ctx_count
    shard_rows = width // (ctx_count * fsdp_count)
    scaling = HEAD_DIM**-0.5

    def partner(values):
        return swap(values, "ctx", 1, ctx_count)

    def columns(array, start, size):
        return lax.dynamic_slice_in_dim(array, start, size, 1)


    kv_start = query_cols + core * key_cols + rank // sharing * HEAD_DIM
    attn_piece = (
        columns(attn_weights, place * q_own, q_own),
        columns(attn_weights, kv_start, HEAD_DIM),
        columns(attn_weights, qkv_cols + place * q_own, q_own),
    )
    attn_own = lax.all_gather(jnp.concatenate(attn_piece, 1), "fsdp", axis=0, tiled=True)
    in_piece = (
        columns(mlp_in_weights, place * f_own, f_own),
        columns(mlp_in_weights, hidden_width + place * f_own, f_own),
    )
    in_piece = jnp.concatenate(in_piece, 1)
    out_piece = columns(mlp_out_weights, place * f_own, f_own)
    in_own = lax.all_gather(in_piece, "fsdp", axis=0, tiled=True)
    out_own = lax.all_gather(out_piece, "fsdp", axis=0, tiled=True)
    gains = lax.all_gather(norm_gains, "fsdp", axis=0, tiled=True).astype(F32)
    g_pre, g_post, g_mid, g_out = [gains[:, i] for i in range(4)]
    attn_other = partner(attn_own)
    qkv_own, proj_own = attn_own[:, : q_own + HEAD_DIM], attn_own[:, q_own + HEAD_DIM :]
    qkv_other, proj_other = attn_other[:, : q_own + HEAD_DIM], attn_other[:, q_own + HEAD_DIM :]

    own_input = layer_input.reshape(tokens, width)
    source = own_input.astype(F32)
    upstream = output_grad.reshape(tokens, width).astype(F32)
    inputs = jnp.concatenate(line_gather(own_input, ranks), 0).astype(F32)
    scale_in = inverse_rms(inputs)
    plain_in = inputs * scale_in
    normed_in = (plain_in * g_pre).astype(BF16)

    def places_of(which):
        slots = rank ^ jnp.arange(ranks, dtype=jnp.int32)
        owners = (2 * slots + which)[:, None] * tokens
        rows = owners + jnp.arange(tokens, dtype=jnp.int32)[None, :]
        return positions_of(rows.reshape(-1), half_block, ctx_count)

    own_places, other_places = places_of(core), places_of(1 - core)
    cosine, sine_table = rotary_tables(own_places, HEAD_DIM)
    all_places = jnp.concatenate([own_places, other_places], 0)
    allowed = all_places[None, :] <= own_places[:, None]
    rows = ranks * tokens

    def ordered(mine, theirs):
        return jnp.where(first_core, mine, theirs), jnp.where(first_core, theirs, mine)

    proj_a, proj_b = dot(normed_in, qkv_own), dot(normed_in, qkv_other)
    query_raw = jnp.concatenate(ordered(proj_a[:, :q_own], proj_b[:, :q_own]), 1)
    key_raw, value_raw = ordered(proj_a[:, q_own:], proj_b[:, q_own:])
    query = rotate(
        query_raw.reshape(rows, heads, HEAD_DIM), cosine[:, None], sine_table[:, None]
    ).astype(BF16)
    key_own = rotate(key_raw, cosine, sine_table).astype(BF16)
    value_own = value_raw.astype(BF16)
    key_value = jnp.concatenate([key_own, value_own], 1)
    key_value = jnp.concatenate([key_value, partner(key_value)], 0)
    keys, values = key_value[:, :HEAD_DIM], key_value[:, HEAD_DIM:]

    def score_rows():
        raw_scores = jnp.einsum("tgd,ld->gtl", query, keys, preferred_element_type=F32)
        tanh_part = jnp.tanh(raw_scores * scaling / SOFT_CAP)
        return tanh_part, jnp.where(allowed, SOFT_CAP * tanh_part, MASKED_SCORE)

    tanh_part, capped = score_rows()
    row_max = jnp.max(capped, -1, keepdims=True)
    weights = jnp.exp(capped - row_max)
    row_total = jnp.sum(weights, -1, keepdims=True)
    log_total = row_max + jnp.log(row_total)
    chances = (weights / row_total).astype(BF16)
    attended = jnp.einsum("gtl,ld->tgd", chances, values, preferred_element_type=F32)
    attended = attended.reshape(rows, heads * HEAD_DIM).astype(BF16)
    att_own, att_other = ordered(attended[:, :q_own], attended[:, q_own:])
    branch_parts = (dot_t(att_own, proj_own) + dot_t(att_other, proj_other)).reshape(
        ranks, tokens, width
    )

    span = tokens // STREAMS
    cuts = [slice(s * span, (s + 1) * span) for s in range(STREAMS)]

    def own_rows(parts):
        return line_scatter(list(parts.reshape(ranks, -1, width)), ranks)

    def all_rows(values):
        return jnp.concatenate(line_gather(values, ranks), 0)

    branch = [own_rows(branch_parts[:, cut]) for cut in cuts]
    halves = ((in_own, out_own), (partner(in_own), partner(out_own)))
    scale_branch = [inverse_rms(v) for v in branch]
    residual = [source[cut] + v * w * g_post for cut, v, w in zip(cuts, branch, scale_branch)]
    scale_mid = [inverse_rms(v) for v in residual]
    mids = [all_rows((v * w * g_mid).astype(BF16)) for v, w in zip(residual, scale_mid)]
    hiddens, backs, mixed = [], [], []
    for values_in in mids:
        hidden_of, back_of, total = [], [], 0.0
        for w_in, w_out in halves:
            gate_up = dot(values_in, w_in)
            hidden, back = jax.vjp(geglu, gate_up[:, :f_own], gate_up[:, f_own:])
            hidden_of.append(hidden.astype(BF16))
            back_of.append(back)
            total = total + dot_t(hidden_of[-1], w_out)
        hiddens.append(hidden_of)
        backs.append(back_of)
        mixed.append(own_rows(total))
    scale_mixed = [inverse_rms(v) for v in mixed]
    block_out = [
        (r + v * w * g_out).astype(BF16) for r, v, w in zip(residual, mixed, scale_mixed)
    ]
    ups = [upstream[cut] for cut in cuts]
    grad_out_gain = sum(jnp.sum(u * v * w, 0) for u, v, w in zip(ups, mixed, scale_mixed))
    d_mixeds = [
        all_rows(norm_backward(v, w, u * g_out).astype(BF16))
        for u, v, w in zip(ups, mixed, scale_mixed)
    ]

    def both_cores(mine, others=None):
        return jnp.concatenate([mine, partner(mine if others is None else others)], 0)

    def joined(pieces):
        return jnp.concatenate(pieces, 0)

    def grouped(left):
        left = left.reshape(left.shape[0], ctx_count, fsdp_count, shard_rows)
        return left.transpose(0, 2, 1, 3).reshape(left.shape[0], fsdp_count, ctx_count * shard_rows)

    def weight_grad(left, right):
        product = jnp.einsum("tfr,tn->frn", grouped(left), right, preferred_element_type=F32)
        return product.reshape(width, right.shape[1]).astype(BF16)

    def over_sequences(product):
        total = lax.psum_scatter(product, "fsdp", scatter_dimension=0, tiled=True)
        return total.reshape(ranks, 2, shard_rows, product.shape[1])

    def spread(total):
        mine = jnp.where(first_core, total[:, 0], total[:, 1])
        theirs = partner(jnp.where(first_core, total[:, 1], total[:, 0]))
        both = jnp.stack(ordered(mine, theirs), 1)
        got = []
        for k in range(ranks):
            part = lax.dynamic_index_in_dim(both, rank ^ k, 0, keepdims=False)
            got.append(part if k == 0 else swap(part, "ctx", 2 * k, ctx_count))
        return got

    def put(into, piece, start, adds=False):
        piece = piece.astype(F32)
        if adds:
            piece = piece + lax.dynamic_slice_in_dim(into, start, piece.shape[1], 1)
        return lax.dynamic_update_slice_in_dim(into, piece, start, 1)

    mid_rows = both_cores(joined(mids))
    hidden_rows = both_cores(joined([h[0] for h in hiddens]), joined([h[1] for h in hiddens]))
    down_product = weight_grad(both_cores(joined(d_mixeds)), hidden_rows)
    d_mid, d_gate_ups = [], []
    for values_in, back_of in zip(d_mixeds, backs):
        total, d_gate_up_of = 0.0, []
        for (w_in, w_out), back in zip(halves, back_of):
            d_gate_up = jnp.concatenate(back(dot(values_in, w_out)), 1).astype(BF16)
            d_gate_up_of.append(d_gate_up)
            total = total + dot_t(d_gate_up, w_in)
        d_gate_ups.append(d_gate_up_of)
        d_mid.append(own_rows(total))
    down_total = over_sequences(down_product)
    dgu_rows = both_cores(joined([d[0] for d in d_gate_ups]), joined([d[1] for d in d_gate_ups]))
    gate_up_product = weight_grad(mid_rows, dgu_rows)
    gate_up_total = over_sequences(gate_up_product)

    grad_mid_gain = sum(jnp.sum(d * v * w, 0) for d, v, w in zip(d_mid, residual, scale_mid))
    d_residual = [
        u + norm_backward(v, w, d * g_mid) for u, v, w, d in zip(ups, residual, scale_mid, d_mid)
    ]
    grad_post_gain = sum(
        jnp.sum(d * v * w, 0) for d, v, w in zip(d_residual, branch, scale_branch)
    )
    d_branches = [
        line_gather(norm_backward(v, w, d * g_post).astype(BF16), ranks)
        for d, v, w in zip(d_residual, branch, scale_branch)
    ]
    d_branches = joined([d[k] for k in range(ranks) for d in d_branches])
    d_residual = joined(d_residual)

    down = spread(down_total)
    d_att_own, d_att_other = dot(d_branches, proj_own), dot(d_branches, proj_other)
    d_attended = jnp.concatenate(ordered(d_att_own, d_att_other), 1).astype(BF16)
    d_attended = d_attended.reshape(rows, heads, HEAD_DIM)
    tanh_again, capped_again = score_rows()
    chances_f = jnp.exp(capped_again - log_total)
    d_values = jnp.einsum(
        "gtl,tgd->ld", chances_f.astype(BF16), d_attended, preferred_element_type=F32
    )
    d_chances = jnp.einsum("tgd,ld->gtl", d_attended, values, preferred_element_type=F32)
    row_inner = jnp.sum(chances_f * d_chances, -1, keepdims=True)
    d_raw = (
        chances_f * (d_chances - row_inner) * (1.0 - tanh_again * tanh_again) * scaling
    ).astype(BF16)
    d_query = jnp.einsum("gtl,ld->tgd", d_raw, keys, preferred_element_type=F32)
    d_keys = jnp.einsum("gtl,tgd->ld", d_raw, query, preferred_element_type=F32)
    d_key_value = jnp.concatenate([d_keys, d_values], 1)
    d_key_value = d_key_value[:rows] + partner(d_key_value[rows:].astype(BF16)).astype(F32)
    d_query_raw = rotate_back(d_query, cosine[:, None], sine_table[:, None]).reshape(
        rows, heads * HEAD_DIM
    )
    d_key_raw = rotate_back(d_key_value[:, :HEAD_DIM], cosine, sine_table)
    dq_own, dq_other = ordered(d_query_raw[:, :q_own], d_query_raw[:, q_own:])
    dkv_own, dkv_other = ordered(d_key_raw, d_key_value[:, HEAD_DIM:])
    dproj_own = jnp.concatenate([dq_own, dkv_own], 1).astype(BF16)
    dproj_other = jnp.concatenate([dq_other, dkv_other], 1).astype(BF16)
    d_in = dot_t(dproj_own, qkv_own) + dot_t(dproj_other, qkv_other)
    grad_pre_gain = jnp.sum(d_in * plain_in, 0)
    d_in = own_rows(d_in)
    d_source = d_residual + norm_backward(source, scale_in[:tokens], d_in * g_pre)

    gate_up_terms = spread(gate_up_total)
    gain_terms = jnp.stack([grad_pre_gain, grad_post_gain, grad_mid_gain, grad_out_gain], 1)
    gain_terms = gain_terms.reshape(ctx_count, fsdp_count, shard_rows, 4)
    gain_terms = gain_terms.transpose(1, 0, 2, 3).reshape(fsdp_count, -1, 4)
    lefts = (grouped(both_cores(normed_in)), grouped(both_cores(d_branches)))
    rights = (both_cores(dproj_own, dproj_other), both_cores(att_own, att_other))

    def attn_part(index):
        at = [lax.dynamic_index_in_dim(v, index, 1, keepdims=False) for v in lefts]
        gain_rows = lax.dynamic_index_in_dim(gain_terms, index, 0, keepdims=False)
        pieces = [
            jnp.einsum("tr,tn->rn", v, right, preferred_element_type=F32)
            for v, right in zip(at, rights)
        ]
        return jnp.concatenate(pieces + [gain_rows], 1)

    attn_total = over_sequences(joined([attn_part(i).astype(BF16) for i in range(fsdp_count)]))
    attn_terms = spread(attn_total)

    grad_mlp_out = jnp.zeros((shard_rows, hidden_width), F32)
    grad_mlp_in = jnp.zeros((shard_rows, 2 * hidden_width), F32)
    grad_attn = jnp.zeros((shard_rows, attn_weights.shape[1]), F32)
    grad_gains = jnp.zeros((shard_rows, 4), F32)
    kv_end, out_end = q_own + HEAD_DIM, 2 * q_own + HEAD_DIM
    for k in range(ranks):
        giver = rank ^ k
        for which in (0, 1):
            start = (2 * giver + which) * f_own
            grad_mlp_out = put(grad_mlp_out, down[k][which], start)
            term = gate_up_terms[k][which]
            grad_mlp_in = put(grad_mlp_in, term[:, :f_own], start)
            grad_mlp_in = put(grad_mlp_in, term[:, f_own:], hidden_width + start)
            term = attn_terms[k][which]
            start = (2 * giver + which) * q_own
            grad_attn = put(grad_attn, term[:, :q_own], start)
            grad_attn = put(grad_attn, term[:, kv_end:out_end], qkv_cols + start)
            start = query_cols + which * key_cols + giver // sharing * HEAD_DIM
            grad_attn = put(grad_attn, term[:, q_own:kv_end], start, sharing > 1)
            grad_gains = grad_gains + term[:, out_end:].astype(F32)
    return (
        joined(block_out).reshape(layer_input.shape),
        d_source.reshape(layer_input.shape),
        grad_attn,
        grad_mlp_in,
        grad_mlp_out,
        grad_gains,
    )


def solution(mesh):
    in_specs = (
        P("fsdp", "ctx", None),
        P("fsdp", None),
        P("fsdp", None),
        P("fsdp", None),
        P("fsdp", None),
        P("fsdp", "ctx", None),
    )
    out_specs = (
        P("fsdp", "ctx", None),
        P("fsdp", "ctx", None),
        P(("ctx", "fsdp"), None),
        P(("ctx", "fsdp"), None),
        P(("ctx", "fsdp"), None),
        P(("ctx", "fsdp"), None),
    )
    return jax.shard_map(local, mesh=mesh, in_specs=in_specs, out_specs=out_specs, check_vma=False)
```

```python
import jax
import jax.numpy as jnp
from jax import lax
from jax.experimental import pallas as pl
from jax.experimental.pallas import tpu as pltpu
from jax.sharding import PartitionSpec as P

HEADS = 8
KV_HEADS = 4
HEAD_DIM = 256

EPSILON = 1e-06
SOFT_CAP = 50.0
ROTARY_BASE = 10000.0
MASKED_SCORE = -1e30
STREAMS = 1

F32 = jnp.float32
BF16 = jnp.bfloat16


def positions_of(rows, half_block, ctx_count):
    owners = rows // (2 * half_block)
    within = rows % (2 * half_block)
    return jnp.where(
        within < half_block,
        owners * half_block + within,
        (2 * ctx_count - 1 - owners) * half_block + within - half_block,
    )


def rotary_tables(places, head_dim):
    half_width = head_dim // 2
    frequency = ROTARY_BASE ** (-jnp.arange(half_width, dtype=F32) * 2.0 / head_dim)
    angles = places.astype(F32)[:, None] * frequency[None, :]
    cosine = jnp.concatenate([jnp.cos(angles), jnp.cos(angles)], -1)
    sine_table = jnp.concatenate([jnp.sin(angles), jnp.sin(angles)], -1)
    return (cosine, sine_table)


def turned(values):
    half_width = values.shape[-1] // 2
    return jnp.concatenate([-values[..., half_width:], values[..., :half_width]], -1)


def rotate(values, cosine, sine_table):
    return values * cosine + turned(values) * sine_table


def rotate_back(grads, cosine, sine_table):
    return grads * cosine - turned(grads * sine_table)


def inverse_rms(values):
    return lax.rsqrt(jnp.mean(values * values, -1, keepdims=True) + EPSILON)


def norm_backward(values, scale, grad_normed):
    normed = values * scale
    return scale * (grad_normed - normed * jnp.mean(grad_normed * normed, -1, keepdims=True))


def geglu(gate, upper):
    return jax.nn.gelu(gate, approximate=True) * upper


def dot(a, b):
    return jnp.dot(a, b, preferred_element_type=F32)


def dot_t(a, b):
    return jnp.einsum("tk,dk->td", a, b, preferred_element_type=F32)


def swap(values, axis, distance, count):
    return lax.ppermute(values, axis, [(i, i ^ distance) for i in range(count)])


def line_gather(values, ranks):
    slots = {0: values}
    bit = ranks // 2
    while bit:
        slots.update({k ^ bit: swap(v, "ctx", 2 * bit, 2 * ranks) for k, v in slots.items()})
        bit //= 2
    return [slots[k] for k in range(ranks)]


def line_scatter(parts, ranks):
    sums = {k: v.astype(F32) for k, v in enumerate(parts)}
    bit = 1
    while bit < ranks:
        for k in sorted(sums, reverse=True):
            if k & bit:
                got = swap(sums.pop(k).astype(BF16), "ctx", 2 * bit, 2 * ranks)
                sums[k ^ bit] = sums[k ^ bit] + got.astype(F32)
        bit *= 2
    return sums[0]


def four_scatter(parts, ctx_count, with_first=(), with_far=()):
    by_near = swap(parts[3].astype(BF16), "ctx", 2, ctx_count)
    near, far, by_near, with_first = together(parts[1], parts[2], by_near, with_first)
    far = (far.astype(F32) + by_near.astype(F32)).astype(BF16)
    far = swap(far, "ctx", 4, ctx_count)
    near = swap(near.astype(BF16), "ctx", 2, ctx_count)
    near, far, with_far = together(near, far, with_far)
    return (parts[0], near, far), with_first, with_far


def sum_of(terms):
    return sum(v.astype(F32) for v in terms)


def square_gather(piece, place, beside):
    rows = piece.shape[0]
    half = rows // 2
    near, far = swap(piece, "fsdp", 1, 4), swap(piece, "fsdp", 2, 4)
    first, then = beside
    near, far, first = together(near, far, first)
    corner_a, corner_b = swap(near[:half], "fsdp", 2, 4), swap(far[half:], "fsdp", 1, 4)
    corner_a, corner_b, second = together(corner_a, corner_b, then(first))
    whole = jnp.zeros((4 * rows, piece.shape[1]), piece.dtype)
    for block, at in (
        (piece, place * rows),
        (near, (place ^ 1) * rows),
        (far, (place ^ 2) * rows),
        (corner_a, (place ^ 3) * rows),
        (corner_b, (place ^ 3) * rows + half),
    ):
        whole = lax.dynamic_update_slice_in_dim(whole, block, at, 0)
    return whole, first, second


def corner_scatter(corner, count):
    half = corner.shape[0] // 2
    corner = corner.astype(BF16)
    return swap(corner[:half], "fsdp", 1, count), swap(corner[half:], "fsdp", 2, count)


def rows_scatter(parts, corners, count):
    half = parts[3].shape[0] // 2
    by_near, by_far = corners[0].astype(F32), corners[1].astype(F32)
    near = jnp.concatenate([parts[1][:half], parts[1][half:] + by_far], 0).astype(BF16)
    far = jnp.concatenate([parts[2][:half] + by_near, parts[2][half:]], 0).astype(BF16)
    near, far = swap(near, "fsdp", 1, count), swap(far, "fsdp", 2, count)
    return parts[0] + near.astype(F32) + far.astype(F32)


def together(*values):
    return lax.optimization_barrier(values)


VMEM_BYTES = 60 * 1024 * 1024


def kernel_call(body, grid, in_specs, out_specs, out_shape, scratch, flops, moved, prefetch=0):
    return pl.pallas_call(
        body,
        grid_spec=pltpu.PrefetchScalarGridSpec(
            num_scalar_prefetch=prefetch,
            grid=grid,
            in_specs=in_specs,
            out_specs=out_specs,
            scratch_shapes=scratch,
        ),
        out_shape=out_shape,
        compiler_params=pltpu.CompilerParams(
            vmem_limit_bytes=VMEM_BYTES, dimension_semantics=("arbitrary",) * len(grid)
        ),
        cost_estimate=pl.CostEstimate(flops=flops, bytes_accessed=moved, transcendentals=0),
    )


def mm(a, b):
    return jnp.dot(a, b, preferred_element_type=F32)


def mm_nt(a, b):
    return lax.dot_general(a, b, (((1,), (1,)), ((), ())), preferred_element_type=F32)


def mm_tn(a, b):
    return lax.dot_general(a, b, (((0,), (0,)), ((), ())), preferred_element_type=F32)


def tile_of(size, most):
    return max(t for t in range(128, most + 1, 128) if size % t == 0)


def gelu_parts(gate):
    rate = 0.7978845608028654
    square = gate * gate
    t = jnp.tanh(rate * gate * (1.0 + 0.044715 * square))
    half = 0.5 * (1.0 + t)
    slope = half + 0.5 * gate * (1.0 - t * t) * rate * (1.0 + 3.0 * 0.044715 * square)
    return gate * half, slope


def core_blocks(shape, steps):
    lead = (0,) * (len(shape) - 1)
    return [
        pl.BlockSpec(shape, lambda h, i, c: (*lead, jnp.where(h == 0, i, steps - 1))),
        pl.BlockSpec(shape, lambda h, i, c: (*lead, jnp.where(h == 0, 0, i))),
    ]


def gate_up_forward(values, w_in, core, most=384):
    rows, width = values.shape
    size = w_in.shape[2] // 2
    tile = tile_of(size, most)
    steps = size // tile

    def body(core_ref, x, g, u, hidden0, hidden1, gate_all, up_all):
        gate, up = mm(x[...], g[0]), mm(x[...], u[0])
        gate_all[0] = gate
        up_all[0] = up
        hidden = (gelu_parts(gate)[0] * up).astype(BF16)

        @pl.when(pl.program_id(0) == 0)
        def _():
            hidden0[0] = hidden

        @pl.when(pl.program_id(0) == 1)
        def _():
            hidden1[0] = hidden

    saved = pl.BlockSpec((1, rows, tile), lambda h, i, c: (h, 0, i))
    return kernel_call(
        body,
        (2, steps),
        [
            pl.BlockSpec((rows, width), lambda h, i, c: (0, 0)),
            pl.BlockSpec((1, width, tile), lambda h, i, c: (c[0] ^ h, 0, i)),
            pl.BlockSpec((1, width, tile), lambda h, i, c: (c[0] ^ h, 0, steps + i)),
        ],
        core_blocks((1, rows, tile), steps) + [saved, saved],
        [jax.ShapeDtypeStruct((1, rows, size), BF16)] * 2
        + [jax.ShapeDtypeStruct((2, rows, size), F32)] * 2,
        [],
        8 * rows * width * size,
        8 * width * size + 20 * rows * size,
        prefetch=1,
    )(core, values, w_in, w_in)


def down_forward(hidden, w_out, core, earlier=(), most=768):
    _, rows, size = hidden[0].shape
    width = w_out.shape[1]
    tile = tile_of(width, most)

    def body(core_ref, h0, h1, o0, o1, *refs):
        out = refs[-1]
        out[...] = (mm_nt(h0[0], o0[0]) + mm_nt(h1[0], o1[0])).astype(BF16)

    whole = pl.BlockSpec((1, rows, size), lambda i, c: (0, 0, 0))
    return kernel_call(
        body,
        (width // tile,),
        [
            whole,
            whole,
            pl.BlockSpec((1, tile, size), lambda i, c: (c[0], i, 0)),
            pl.BlockSpec((1, tile, size), lambda i, c: (1 - c[0], i, 0)),
        ]
        + [pl.BlockSpec(memory_space=pl.ANY)] * len(earlier),
        pl.BlockSpec((rows, tile), lambda i, c: (0, i)),
        jax.ShapeDtypeStruct((rows, width), BF16),
        [],
        4 * rows * width * size,
        4 * width * size + 4 * rows * size,
        prefetch=1,
    )(core, *hidden, w_out, w_out, *earlier)


def down_backward(d_mixed, gate_all, up_all, w_out, core, most=384):
    rows, width = d_mixed.shape
    size = w_out.shape[2]
    tile = tile_of(size, most)
    steps = size // tile

    def body(core_ref, x, gate, up, o, dgu0, dgu1):
        d_hidden = mm(x[...], o[0])
        value, slope = gelu_parts(gate[0])
        d_gate = (d_hidden * up[0] * slope).astype(BF16)
        d_up = (d_hidden * value).astype(BF16)

        @pl.when(pl.program_id(0) == 0)
        def _():
            dgu0[0] = d_gate
            dgu0[1] = d_up

        @pl.when(pl.program_id(0) == 1)
        def _():
            dgu1[0] = d_gate
            dgu1[1] = d_up

    saved = pl.BlockSpec((1, rows, tile), lambda h, i, c: (h, 0, i))
    return kernel_call(
        body,
        (2, steps),
        [
            pl.BlockSpec((rows, width), lambda h, i, c: (0, 0)),
            saved,
            saved,
            pl.BlockSpec((1, width, tile), lambda h, i, c: (c[0] ^ h, 0, i)),
        ],
        core_blocks((2, rows, tile), steps),
        [jax.ShapeDtypeStruct((2, rows, size), BF16)] * 2,
        [],
        4 * rows * width * size,
        4 * width * size + 24 * rows * size,
        prefetch=1,
    )(core, d_mixed, gate_all, up_all, w_out)


def gate_up_backward(dgu, w_in, core, earlier=(), most=768):
    _, rows, size = dgu[0].shape
    width = w_in.shape[1]
    tile = tile_of(width, most)

    def body(core_ref, d0, d1, w0, w1, *refs):
        out = refs[-1]
        total = mm_nt(d0[0], w0[0, :, :size]) + mm_nt(d0[1], w0[0, :, size:])
        total += mm_nt(d1[0], w1[0, :, :size]) + mm_nt(d1[1], w1[0, :, size:])
        out[...] = total.astype(BF16)

    whole = pl.BlockSpec((2, rows, size), lambda i, c: (0, 0, 0))
    return kernel_call(
        body,
        (width // tile,),
        [
            whole,
            whole,
            pl.BlockSpec((1, tile, 2 * size), lambda i, c: (c[0], i, 0)),
            pl.BlockSpec((1, tile, 2 * size), lambda i, c: (1 - c[0], i, 0)),
        ]
        + [pl.BlockSpec(memory_space=pl.ANY)] * len(earlier),
        pl.BlockSpec((rows, tile), lambda i, c: (0, i)),
        jax.ShapeDtypeStruct((rows, width), BF16),
        [],
        8 * rows * width * size,
        8 * width * size + 8 * rows * size,
        prefetch=1,
    )(core, *dgu, w_in, w_in, *earlier)


def weight_grad_kernel(lefts, rights, ctx_count, fsdp_count, earlier=()):
    width = lefts[0].shape[1]
    groups, _, size = rights[0].shape
    counts = [v.shape[0] for v in lefts]
    starts = [sum(counts[:i]) for i in range(len(counts))]
    shard = width // (ctx_count * fsdp_count)
    halves = 2
    part, ctx_part = width // halves, ctx_count // halves
    tile = tile_of(size, 1152)
    steps = size // tile

    def body(*refs):
        left_refs, right_refs = refs[: len(counts)], refs[len(counts) : 2 * len(counts)]
        out, turned_left = refs[-2:]

        @pl.when((pl.program_id(1) == 0) & (pl.program_id(2) == 0))
        def _():
            for ref, start, count in zip(left_refs, starts, counts):
                turned_left[:, start : start + count] = ref[...].T

        product = 0.0
        for ref, start, count in zip(right_refs, starts, counts):
            product = product + mm(turned_left[:, start : start + count], ref[0])
        for f in range(fsdp_count):
            at = [(c * fsdp_count + f) * shard for c in range(ctx_part)]
            out[f] = jnp.concatenate([product[i : i + shard] for i in at], 0).astype(BF16)

    return kernel_call(
        body,
        (halves, groups, steps),
        [pl.BlockSpec((n, part), lambda h, g, t: (0, h)) for n in counts]
        + [pl.BlockSpec((1, n, tile), lambda h, g, t: (g, 0, t)) for n in counts]
        + [pl.BlockSpec(memory_space=pl.ANY)] * len(earlier),
        pl.BlockSpec((fsdp_count, ctx_part * shard, tile), lambda h, g, t: (0, h, g * steps + t)),
        jax.ShapeDtypeStruct((fsdp_count, ctx_count * shard, groups * size), BF16),
        [pltpu.VMEM((part, sum(counts)), BF16)],
        2 * sum(counts) * width * groups * size,
        4 * sum(counts) * (width + groups * size) + 2 * width * groups * size,
    )(*lefts, *rights, *earlier)


def rotated(values, cosine, sine, back=False):
    size = values.shape[1] // 2
    low, high = values[:, :size], values[:, size:]
    if back:
        sine = -sine
    return jnp.concatenate([low * cosine - high * sine, high * cosine + low * sine], 1)


def qkv_kernel(inputs, g_pre, attn, cosine, sine, core):
    rows, width = inputs.shape
    block = rows // 2
    size = HEAD_DIM

    def body(core_ref, x, gain, w0, w1, cos, sin, normed_out, q0, q1, kv):
        source = x[...].astype(F32)
        normed = (source * inverse_rms(source) * gain[...]).astype(BF16)
        normed_out[...] = normed
        first = core_ref[0] == 0
        own, other = mm(normed, w0[...]), mm(normed, w1[...])
        q0[...] = rotated(own[:, :size], cos[...], sin[...]).astype(BF16)
        q1[...] = rotated(other[:, :size], cos[...], sin[...]).astype(BF16)
        key = jnp.where(first, own[:, size:], other[:, size:])
        kv[:, :size] = rotated(key, cos[...], sin[...]).astype(BF16)
        kv[:, size:] = jnp.where(first, other[:, size:], own[:, size:]).astype(BF16)

    def by_rows(columns):
        return pl.BlockSpec((block, columns), lambda i, c: (i, 0))

    return kernel_call(
        body,
        (2,),
        [
            by_rows(width),
            pl.BlockSpec((1, width), lambda i, c: (0, 0)),
            pl.BlockSpec((width, 2 * size), lambda i, c: (0, 0)),
            pl.BlockSpec((width, 2 * size), lambda i, c: (0, 0)),
            by_rows(size // 2),
            by_rows(size // 2),
        ],
        [by_rows(width), by_rows(size), by_rows(size), by_rows(2 * size)],
        [
            jax.ShapeDtypeStruct((rows, width), BF16),
            jax.ShapeDtypeStruct((rows, size), BF16),
            jax.ShapeDtypeStruct((rows, size), BF16),
            jax.ShapeDtypeStruct((rows, 2 * size), BF16),
        ],
        [],
        8 * rows * width * size,
        8 * width * size + 4 * rows * width,
        prefetch=1,
    )(core, inputs, g_pre, *attn, cosine, sine)


def scores(query, key, key_place, query_place):
    raw = mm_nt(query, key)
    tanh_part = jnp.tanh(raw * (HEAD_DIM**-0.5 / SOFT_CAP))
    return tanh_part, jnp.where(key_place <= query_place, jnp.exp(SOFT_CAP * tanh_part), 0.0)


def attention_specs(rows, width, block):
    def by_rows(columns):
        return pl.BlockSpec((block, columns), lambda i, c: (i, 0))

    size = HEAD_DIM
    kv = pl.BlockSpec((rows, 2 * size), lambda i, c: (0, 0))
    places = pl.BlockSpec((1, rows), lambda i, c: (0, 0))
    weights = [pl.BlockSpec((width, size), lambda i, c: (0, 2))] * 2
    return by_rows, [by_rows(size), by_rows(size), kv, kv, by_rows(1), places, places] + weights


def attention_forward(core, queries, kvs, row_places, key_places, attn):
    rows, width, size = queries[0].shape[0], attn[0].shape[0], HEAD_DIM
    block = rows // 2

    def body(core_ref, q0, q1, kv0, kv1, place, places0, places1, w0, w1, att0, att1, branch):
        total = 0.0
        for q, att, w in ((q0, att0, w0), (q1, att1, w1)):
            parts = [
                scores(q[...], kv[:, :size], places[...], place[...])[1]
                for kv, places in ((kv0, places0), (kv1, places1))
            ]
            scale = 1.0 / (
                jnp.sum(parts[0], -1, keepdims=True) + jnp.sum(parts[1], -1, keepdims=True)
            )
            attended = mm((parts[0] * scale).astype(BF16), kv0[:, size:])
            attended += mm((parts[1] * scale).astype(BF16), kv1[:, size:])
            attended = attended.astype(BF16)
            att[...] = attended
            total = total + mm_nt(attended, w[...])
        branch[...] = total.astype(BF16)

    by_rows, specs = attention_specs(rows, width, block)
    return kernel_call(
        body,
        (2,),
        specs,
        [by_rows(size), by_rows(size), by_rows(width)],
        [
            jax.ShapeDtypeStruct((rows, size), BF16),
            jax.ShapeDtypeStruct((rows, size), BF16),
            jax.ShapeDtypeStruct((rows, width), BF16),
        ],
        [],
        16 * rows * rows * size + 4 * rows * width * size,
        4 * width * size + 2 * rows * width,
        prefetch=1,
    )(core, *queries, *kvs, row_places, *key_places, *attn)


def attention_backward(
    d_branch, core, queries, kvs, row_places, key_places, attn, cosine, sine
):
    rows, width, size = queries[0].shape[0], attn[0].shape[0], HEAD_DIM
    block = rows // 2
    scaling = size**-0.5

    def body(
        core_ref, q0, q1, kv0, kv1, place, places0, places1, w0, w1, d_out, cos, sin,
        dq0, dq1, dkv0, dkv1, sum0, sum1
    ):
        @pl.when(pl.program_id(0) == 0)
        def _():
            sum0[...] = jnp.zeros_like(sum0)
            sum1[...] = jnp.zeros_like(sum1)

        for q, dq, w in ((q0, dq0, w0), (q1, dq1, w1)):
            query = q[...]
            d_att = mm(d_out[...], w[...]).astype(BF16)
            parts = [
                scores(query, kv[:, :size], places[...], place[...])
                for kv, places in ((kv0, places0), (kv1, places1))
            ]
            scale = 1.0 / sum(jnp.sum(e, -1, keepdims=True) for _, e in parts)
            chances = [e * scale for _, e in parts]
            d_chances = [mm_nt(d_att, kv[:, size:]) for kv in (kv0, kv1)]
            inner = sum(
                jnp.sum(p * d, -1, keepdims=True) for p, d in zip(chances, d_chances)
            )
            d_query = 0.0
            for (t, _), p, d, kv, sums in zip(
                parts, chances, d_chances, (kv0, kv1), (sum0, sum1)
            ):
                d_raw = (p * (d - inner) * (1.0 - t * t) * scaling).astype(BF16)
                d_query = d_query + mm(d_raw, kv[:, :size])
                sums[:, :size] += mm_tn(d_raw, query)
                sums[:, size:] += mm_tn(p.astype(BF16), d_att)
            dq[...] = rotated(d_query, cos[...], sin[...], back=True).astype(BF16)

        @pl.when(pl.program_id(0) == pl.num_programs(0) - 1)
        def _():
            dkv0[...] = sum0[...]
            dkv1[...] = sum1[...].astype(BF16)

    by_rows, specs = attention_specs(rows, width, block)
    whole = pl.BlockSpec((rows, 2 * size), lambda i, c: (0, 0))
    return kernel_call(
        body,
        (2,),
        specs + [by_rows(width), by_rows(size // 2), by_rows(size // 2)],
        [by_rows(size), by_rows(size), whole, whole],
        [
            jax.ShapeDtypeStruct((rows, size), BF16),
            jax.ShapeDtypeStruct((rows, size), BF16),
            jax.ShapeDtypeStruct((rows, 2 * size), F32),
            jax.ShapeDtypeStruct((rows, 2 * size), BF16),
        ],
        [pltpu.VMEM((rows, 2 * size), F32)] * 2,
        40 * rows * rows * size + 4 * rows * width * size,
        4 * width * size + 2 * rows * width,
        prefetch=1,
    )(core, *queries, *kvs, row_places, *key_places, *attn, d_branch, cosine, sine)


def qkv_backward(inputs, dqs, dkv_mine, dkv_got, attn, cosine, sine, core):
    rows, width = inputs.shape
    block, size = rows // 2, HEAD_DIM

    def body(core_ref, x, q0, q1, mine, got, w0, w1, cos, sin, d_in, dp0, dp1, gain):
        both = mine[...] + got[...].astype(F32)
        d_key = rotated(both[:, :size], cos[...], sin[...], back=True)
        first = core_ref[0] == 0
        dp0[0, :, :size] = q0[...]
        dp1[0, :, :size] = q1[...]
        dp0[0, :, size:] = jnp.where(first, d_key, both[:, size:]).astype(BF16)
        dp1[0, :, size:] = jnp.where(first, both[:, size:], d_key).astype(BF16)
        total = mm_nt(dp0[0], w0[...]) + mm_nt(dp1[0], w1[...])
        d_in[...] = total.astype(BF16)
        source = x[...].astype(F32)
        term = jnp.sum(total * source * inverse_rms(source), 0, keepdims=True)

        @pl.when(pl.program_id(0) == 0)
        def _():
            gain[...] = jnp.zeros_like(gain)

        gain[...] += term

    def by_rows(columns):
        return pl.BlockSpec((block, columns), lambda i, c: (i, 0))

    weights = [pl.BlockSpec((width, 2 * size), lambda i, c: (0, 0))] * 2
    terms = pl.BlockSpec((1, block, 2 * size), lambda i, c: (0, i, 0))
    return kernel_call(
        body,
        (2,),
        [by_rows(width), by_rows(size), by_rows(size), by_rows(2 * size), by_rows(2 * size)]
        + weights
        + [by_rows(size // 2), by_rows(size // 2)],
        [by_rows(width), terms, terms, pl.BlockSpec((1, width), lambda i, c: (0, 0))],
        [
            jax.ShapeDtypeStruct((rows, width), BF16),
            jax.ShapeDtypeStruct((1, rows, 2 * size), BF16),
            jax.ShapeDtypeStruct((1, rows, 2 * size), BF16),
            jax.ShapeDtypeStruct((1, width), F32),
        ],
        [],
        8 * rows * width * size,
        8 * width * size + 4 * rows * width,
        prefetch=1,
    )(core, inputs, *dqs, dkv_mine, dkv_got, *attn, cosine, sine)


def to_owners(total, ctx_count):
    total = total.reshape(ctx_count, -1, total.shape[1])
    return lax.all_to_all(total, "ctx", split_axis=0, concat_axis=0, tiled=True)


def side_by_side(terms):
    return terms.astype(F32).transpose(1, 0, 2).reshape(terms.shape[1], -1)


def attention_outputs(terms, columns):
    count, rows, _ = terms.shape
    size = HEAD_DIM

    def body(t, grad, gains):
        total = 0.0
        for c in range(count):
            part = t[c].astype(F32)
            kv = count * size + (c % 2) * (count // 2) * size + c // 2 * size
            grad[:, c * size : (c + 1) * size] = part[:, :size]
            grad[:, kv : kv + size] = part[:, size : 2 * size]
            out = columns - (count - c) * size
            grad[:, out : out + size] = part[:, 2 * size : 3 * size]
            total = total + part[:, 3 * size :]
        gains[...] = total

    return pl.pallas_call(
        body,
        out_shape=[
            jax.ShapeDtypeStruct((rows, columns), F32),
            jax.ShapeDtypeStruct((rows, terms.shape[2] - 3 * size), F32),
        ],
        compiler_params=pltpu.CompilerParams(vmem_limit_bytes=VMEM_BYTES),
    )(terms)


def local_kernels(
    layer_input, attn_weights, mlp_in_weights, mlp_out_weights, norm_gains, output_grad
):
    tokens, width = layer_input.shape[1:]
    half_block = tokens // 2
    ctx_count = lax.axis_size("ctx")
    fsdp_count = lax.axis_size("fsdp")
    ranks = ctx_count // 2
    place = lax.axis_index("ctx")
    fsdp_place = lax.axis_index("fsdp")
    rank, core = place // 2, place % 2
    query_cols, key_cols = HEADS * HEAD_DIM, KV_HEADS * HEAD_DIM
    qkv_cols = query_cols + 2 * key_cols
    hidden_width = mlp_out_weights.shape[1]
    f_own = hidden_width // ctx_count
    shard_rows = width // (ctx_count * fsdp_count)

    def partner(values):
        return swap(values, "ctx", 1, ctx_count)

    def columns(array, start, size):
        return lax.dynamic_slice_in_dim(array, start, size, 1)

    chip_groups = [
        [(2 * r + c) * fsdp_count + f for c in (0, 1) for f in range(fsdp_count)]
        for r in range(ranks)
    ]

    def chip_gather(piece):
        whole = lax.all_gather(
            piece, ("ctx", "fsdp"), axis=0, tiled=True, axis_index_groups=chip_groups
        )
        return whole.reshape(2, width, piece.shape[1])

    def over_sequences(product):
        product = product.reshape(width, product.shape[2])
        return lax.psum_scatter(product, "fsdp", scatter_dimension=0, tiled=True)

    def joined(pieces):
        return jnp.concatenate(pieces, 0)

    own_input = layer_input.reshape(tokens, width)
    source = own_input.astype(F32)
    upstream = output_grad.reshape(tokens, width).astype(F32)
    kv_start = query_cols + core * key_cols + rank * HEAD_DIM
    piece = [
        columns(attn_weights, place * HEAD_DIM, HEAD_DIM),
        columns(attn_weights, kv_start, HEAD_DIM),
        columns(attn_weights, qkv_cols + place * HEAD_DIM, HEAD_DIM),
    ]
    piece, place_in = together(jnp.concatenate(piece, 1), place)
    own_gains = norm_gains.T
    if fsdp_count == 4:
        ways = [swap(own_input, "ctx", 4, ctx_count), swap(own_input, "ctx", 2, ctx_count)]

        def onward(got):
            return swap(got[0], "ctx", 2, ctx_count), [swap(own_gains, "fsdp", k, 4) for k in (1, 2, 3)]

        attn_own, (slot_2, slot_1), (slot_3, gains_got) = square_gather(
            piece, fsdp_place, (ways, onward)
        )
        gains = jnp.zeros((4, width), BF16)
        for k, block in enumerate([own_gains, *gains_got]):
            start = (fsdp_place ^ k) * own_gains.shape[1]
            gains = lax.dynamic_update_slice_in_dim(gains, block, start, 1)
        gains = gains.astype(F32)
        inputs = joined([own_input, slot_1, slot_2, slot_3])
    else:
        attn_own = lax.all_gather(piece, "fsdp", axis=0, tiled=True)
        inputs = joined(line_gather(own_input, ranks))
        gains = lax.all_gather(own_gains, "fsdp", axis=1, tiled=True).astype(F32)
    attn = (attn_own, partner(attn_own))
    g_pre, g_post, g_mid, g_out = [gains[i] for i in range(4)]
    in_all = chip_gather(
        jnp.concatenate(
            [
                columns(mlp_in_weights, place_in * f_own, f_own),
                columns(mlp_in_weights, hidden_width + place_in * f_own, f_own),
            ],
            1,
        )
    )
    out_all = chip_gather(columns(mlp_out_weights, place_in * f_own, f_own))

    def places_of(which):
        owners = (2 * (rank ^ jnp.arange(ranks, dtype=jnp.int32)) + which)[:, None] * tokens
        gathered_rows = owners + jnp.arange(tokens, dtype=jnp.int32)[None, :]
        return positions_of(gathered_rows.reshape(-1), half_block, ctx_count)

    own_places, other_places = places_of(core), places_of(1 - core)
    cosine, sine = rotary_tables(own_places, HEAD_DIM)
    cosine, sine = cosine[:, : HEAD_DIM // 2], sine[:, : HEAD_DIM // 2]
    row_places, key_places = own_places[:, None], (own_places[None, :], other_places[None, :])
    core_word = core.reshape(1).astype(jnp.int32)

    normed_in, *queries, kv_own = qkv_kernel(
        inputs, gains[:1], attn, cosine, sine, core_word
    )
    attention = (core_word, queries, (kv_own, partner(kv_own)), row_places, key_places, attn)
    att_own, att_other, branch_parts = attention_forward(*attention)
    branch_parts = branch_parts.reshape(ranks, tokens, width)

    def own_rows(halves, with_first=(), with_far=()):
        halves = [v.reshape(2, tokens, width) for v in halves]
        parts = [halves[k % 2][k // 2] for k in range(4)]
        terms, with_first, with_far = four_scatter(parts, ctx_count, with_first, with_far)
        return sum_of(terms), with_first, with_far

    def gathered_halves(values, work):
        slots = line_gather(values, ranks)
        first = joined([slots[0], slots[2]])
        done = work(first, 0)
        last, first, done = together(slots[3], first, done)
        second = joined([slots[1], last])
        return (first, second), (done, work(second, 1))

    branch = sum_of(four_scatter(branch_parts.reshape(ranks, tokens, width), ctx_count)[0])
    scale_branch = inverse_rms(branch)
    residual = source + branch * scale_branch * g_post
    scale_mid = inverse_rms(residual)
    mids, forward = gathered_halves(
        (residual * scale_mid * g_mid).astype(BF16), lambda v, _: gate_up_forward(v, in_all, core_word)
    )
    mixed_1 = down_forward(forward[1][:2], out_all, core_word)
    mixed_0 = down_forward(forward[0][:2], out_all, core_word, (mixed_1,))
    hidden_own = [f[0] for f in forward]
    hidden_got = [partner(f[1]) for f in forward]
    mid_got = [partner(v) for v in mids]
    mixed = own_rows((mixed_0, mixed_1))[0]
    mixed, hidden_own, hidden_got, mid_got = together(mixed, hidden_own, hidden_got, mid_got)
    scale_mixed = inverse_rms(mixed)
    block_out = (residual + mixed * scale_mixed * g_out).astype(BF16)
    grad_out_gain = jnp.sum(upstream * mixed * scale_mixed, 0)
    d_mixeds, d_gate_ups = gathered_halves(
        norm_backward(mixed, scale_mixed, upstream * g_out).astype(BF16),
        lambda v, k: down_backward(v, *forward[k][2:], out_all, core_word),
    )

    def weight_grad(lefts, rights, *earlier):
        return weight_grad_kernel(lefts, rights, ctx_count, fsdp_count, earlier)

    down_product = weight_grad(
        [*d_mixeds, *[partner(v) for v in d_mixeds]], hidden_own + hidden_got
    )
    d_gate_ups, down_product = together(d_gate_ups, down_product)
    down_total = over_sequences(down_product)
    d_mid_1 = gate_up_backward(d_gate_ups[1], in_all, core_word)
    d_mid_0 = gate_up_backward(d_gate_ups[0], in_all, core_word, (d_mid_1,))
    gate_up_product = weight_grad(
        [*mids, *mid_got],
        [v[0] for v in d_gate_ups] + [partner(v[1]) for v in d_gate_ups],
        d_mid_0,
    )
    d_mid, _, (gate_up_product,) = own_rows((d_mid_0, d_mid_1), (), (gate_up_product,))
    gate_up_total = over_sequences(gate_up_product)
    grad_mid_gain = jnp.sum(d_mid * residual * scale_mid, 0)
    d_residual = upstream + norm_backward(residual, scale_mid, d_mid * g_mid)
    grad_post_gain = jnp.sum(d_residual * branch * scale_branch, 0)
    d_branches = joined(
        line_gather(
            norm_backward(branch, scale_branch, d_residual * g_post).astype(BF16), ranks
        )
    )

    d_branches, down_total = together(d_branches, down_total)
    down = to_owners(down_total, ctx_count)
    *d_queries, dkv_own, dkv_other = attention_backward(d_branches, *attention, cosine, sine)
    d_in, dproj_own, dproj_other, grad_pre_gain = qkv_backward(
        inputs, d_queries, dkv_own, partner(dkv_other), attn, cosine, sine, core_word
    )

    gain_terms = jnp.stack([grad_pre_gain[0], grad_post_gain, grad_mid_gain, grad_out_gain], 1)
    gain_terms = gain_terms.reshape(ctx_count, fsdp_count, shard_rows, 4)
    gain_terms = gain_terms.transpose(1, 0, 2, 3).reshape(fsdp_count, -1, 4)
    out_product = weight_grad(
        [d_branches, partner(d_branches)], [att_own[None], partner(att_other)[None]]
    )
    product = weight_grad([normed_in, partner(normed_in)], [dproj_own, partner(dproj_other)])
    product = jnp.concatenate([product, out_product, gain_terms.astype(BF16)], 2)
    d_in = d_in.reshape(ranks, tokens, width)
    d_in, (down, product), (gate_up_total,) = four_scatter(
        d_in, ctx_count, (down, product), (gate_up_total,)
    )
    gate_up_terms = to_owners(gate_up_total, ctx_count)
    if fsdp_count == 4:
        parts = [
            lax.dynamic_index_in_dim(product, fsdp_place ^ k, 0, keepdims=False).astype(F32)
            for k in range(4)
        ]
        corners = corner_scatter(parts[3], 4)
        attn_total = rows_scatter(parts, corners, 4).astype(BF16)
    else:
        attn_total = over_sequences(product)
    gate_up_terms, attn_total = together(gate_up_terms, attn_total)
    attn_terms = to_owners(attn_total, ctx_count)
    d_in, attn_terms = together(d_in, attn_terms)
    d_in = sum_of(d_in)
    d_source = d_residual + norm_backward(source, inverse_rms(source), d_in * g_pre)

    grad_mlp_out = side_by_side(down)
    grad_mlp_in = jnp.concatenate(
        [side_by_side(gate_up_terms[:, :, :f_own]), side_by_side(gate_up_terms[:, :, f_own:])], 1
    )
    grad_attn, grad_gains = attention_outputs(attn_terms, attn_weights.shape[1])
    return (
        block_out.reshape(layer_input.shape),
        d_source.reshape(layer_input.shape),
        grad_attn,
        grad_mlp_in,
        grad_mlp_out,
        grad_gains,
    )


def local(layer_input, attn_weights, mlp_in_weights, mlp_out_weights, norm_gains, output_grad):
    ctx_count, fsdp_count = lax.axis_size("ctx"), lax.axis_size("fsdp")
    width, hidden_width = layer_input.shape[2], mlp_out_weights.shape[1]
    fits = (
        ctx_count == HEADS == 2 * KV_HEADS == 8
        and hidden_width % (128 * ctx_count) == 0
        and width % 256 == 0
        and width % (8 * ctx_count * fsdp_count) == 0
        and (width // fsdp_count) % 32 == 0
    )
    path = local_kernels if fits else local_general
    return path(
        layer_input, attn_weights, mlp_in_weights, mlp_out_weights, norm_gains, output_grad
    )


def local_general(layer_input, attn_weights, mlp_in_weights, mlp_out_weights, norm_gains, output_grad):
    tokens, width = layer_input.shape[1:]
    half_block = tokens // 2
    ctx_count = lax.axis_size("ctx")
    fsdp_count = lax.axis_size("fsdp")
    ranks = ctx_count // 2
    place = lax.axis_index("ctx")
    rank, core = place // 2, place % 2
    first_core = core == 0
    query_cols, key_cols = HEADS * HEAD_DIM, KV_HEADS * HEAD_DIM
    qkv_cols = query_cols + 2 * key_cols
    heads = HEADS // ranks
    sharing = ranks // KV_HEADS
    hidden_width = mlp_out_weights.shape[1]
    q_own = query_cols // ctx_count
    f_own = hidden_width // ctx_count
    shard_rows = width // (ctx_count * fsdp_count)
    scaling = HEAD_DIM**-0.5

    def partner(values):
        return swap(values, "ctx", 1, ctx_count)

    def columns(array, start, size):
        return lax.dynamic_slice_in_dim(array, start, size, 1)


    kv_start = query_cols + core * key_cols + rank // sharing * HEAD_DIM
    attn_piece = (
        columns(attn_weights, place * q_own, q_own),
        columns(attn_weights, kv_start, HEAD_DIM),
        columns(attn_weights, qkv_cols + place * q_own, q_own),
    )
    attn_own = lax.all_gather(jnp.concatenate(attn_piece, 1), "fsdp", axis=0, tiled=True)
    in_piece = (
        columns(mlp_in_weights, place * f_own, f_own),
        columns(mlp_in_weights, hidden_width + place * f_own, f_own),
    )
    in_piece = jnp.concatenate(in_piece, 1)
    out_piece = columns(mlp_out_weights, place * f_own, f_own)
    in_own = lax.all_gather(in_piece, "fsdp", axis=0, tiled=True)
    out_own = lax.all_gather(out_piece, "fsdp", axis=0, tiled=True)
    gains = lax.all_gather(norm_gains, "fsdp", axis=0, tiled=True).astype(F32)
    g_pre, g_post, g_mid, g_out = [gains[:, i] for i in range(4)]
    attn_other = partner(attn_own)
    qkv_own, proj_own = attn_own[:, : q_own + HEAD_DIM], attn_own[:, q_own + HEAD_DIM :]
    qkv_other, proj_other = attn_other[:, : q_own + HEAD_DIM], attn_other[:, q_own + HEAD_DIM :]

    own_input = layer_input.reshape(tokens, width)
    source = own_input.astype(F32)
    upstream = output_grad.reshape(tokens, width).astype(F32)
    inputs = jnp.concatenate(line_gather(own_input, ranks), 0).astype(F32)
    scale_in = inverse_rms(inputs)
    plain_in = inputs * scale_in
    normed_in = (plain_in * g_pre).astype(BF16)

    def places_of(which):
        slots = rank ^ jnp.arange(ranks, dtype=jnp.int32)
        owners = (2 * slots + which)[:, None] * tokens
        rows = owners + jnp.arange(tokens, dtype=jnp.int32)[None, :]
        return positions_of(rows.reshape(-1), half_block, ctx_count)

    own_places, other_places = places_of(core), places_of(1 - core)
    cosine, sine_table = rotary_tables(own_places, HEAD_DIM)
    all_places = jnp.concatenate([own_places, other_places], 0)
    allowed = all_places[None, :] <= own_places[:, None]
    rows = ranks * tokens

    def ordered(mine, theirs):
        return jnp.where(first_core, mine, theirs), jnp.where(first_core, theirs, mine)

    proj_a, proj_b = dot(normed_in, qkv_own), dot(normed_in, qkv_other)
    query_raw = jnp.concatenate(ordered(proj_a[:, :q_own], proj_b[:, :q_own]), 1)
    key_raw, value_raw = ordered(proj_a[:, q_own:], proj_b[:, q_own:])
    query = rotate(
        query_raw.reshape(rows, heads, HEAD_DIM), cosine[:, None], sine_table[:, None]
    ).astype(BF16)
    key_own = rotate(key_raw, cosine, sine_table).astype(BF16)
    value_own = value_raw.astype(BF16)
    key_value = jnp.concatenate([key_own, value_own], 1)
    key_value = jnp.concatenate([key_value, partner(key_value)], 0)
    keys, values = key_value[:, :HEAD_DIM], key_value[:, HEAD_DIM:]

    def score_rows():
        raw_scores = jnp.einsum("tgd,ld->gtl", query, keys, preferred_element_type=F32)
        tanh_part = jnp.tanh(raw_scores * scaling / SOFT_CAP)
        return tanh_part, jnp.where(allowed, SOFT_CAP * tanh_part, MASKED_SCORE)

    tanh_part, capped = score_rows()
    row_max = jnp.max(capped, -1, keepdims=True)
    weights = jnp.exp(capped - row_max)
    row_total = jnp.sum(weights, -1, keepdims=True)
    log_total = row_max + jnp.log(row_total)
    chances = (weights / row_total).astype(BF16)
    attended = jnp.einsum("gtl,ld->tgd", chances, values, preferred_element_type=F32)
    attended = attended.reshape(rows, heads * HEAD_DIM).astype(BF16)
    att_own, att_other = ordered(attended[:, :q_own], attended[:, q_own:])
    branch_parts = (dot_t(att_own, proj_own) + dot_t(att_other, proj_other)).reshape(
        ranks, tokens, width
    )

    span = tokens // STREAMS
    cuts = [slice(s * span, (s + 1) * span) for s in range(STREAMS)]

    def own_rows(parts):
        return line_scatter(list(parts.reshape(ranks, -1, width)), ranks)

    def all_rows(values):
        return jnp.concatenate(line_gather(values, ranks), 0)

    branch = [own_rows(branch_parts[:, cut]) for cut in cuts]
    halves = ((in_own, out_own), (partner(in_own), partner(out_own)))
    scale_branch = [inverse_rms(v) for v in branch]
    residual = [source[cut] + v * w * g_post for cut, v, w in zip(cuts, branch, scale_branch)]
    scale_mid = [inverse_rms(v) for v in residual]
    mids = [all_rows((v * w * g_mid).astype(BF16)) for v, w in zip(residual, scale_mid)]
    hiddens, backs, mixed = [], [], []
    for values_in in mids:
        hidden_of, back_of, total = [], [], 0.0
        for w_in, w_out in halves:
            gate_up = dot(values_in, w_in)
            hidden, back = jax.vjp(geglu, gate_up[:, :f_own], gate_up[:, f_own:])
            hidden_of.append(hidden.astype(BF16))
            back_of.append(back)
            total = total + dot_t(hidden_of[-1], w_out)
        hiddens.append(hidden_of)
        backs.append(back_of)
        mixed.append(own_rows(total))
    scale_mixed = [inverse_rms(v) for v in mixed]
    block_out = [
        (r + v * w * g_out).astype(BF16) for r, v, w in zip(residual, mixed, scale_mixed)
    ]
    ups = [upstream[cut] for cut in cuts]
    grad_out_gain = sum(jnp.sum(u * v * w, 0) for u, v, w in zip(ups, mixed, scale_mixed))
    d_mixeds = [
        all_rows(norm_backward(v, w, u * g_out).astype(BF16))
        for u, v, w in zip(ups, mixed, scale_mixed)
    ]

    def both_cores(mine, others=None):
        return jnp.concatenate([mine, partner(mine if others is None else others)], 0)

    def joined(pieces):
        return jnp.concatenate(pieces, 0)

    def grouped(left):
        left = left.reshape(left.shape[0], ctx_count, fsdp_count, shard_rows)
        return left.transpose(0, 2, 1, 3).reshape(left.shape[0], fsdp_count, ctx_count * shard_rows)

    def weight_grad(left, right):
        product = jnp.einsum("tfr,tn->frn", grouped(left), right, preferred_element_type=F32)
        return product.reshape(width, right.shape[1]).astype(BF16)

    def over_sequences(product):
        total = lax.psum_scatter(product, "fsdp", scatter_dimension=0, tiled=True)
        return total.reshape(ranks, 2, shard_rows, product.shape[1])

    def spread(total):
        mine = jnp.where(first_core, total[:, 0], total[:, 1])
        theirs = partner(jnp.where(first_core, total[:, 1], total[:, 0]))
        both = jnp.stack(ordered(mine, theirs), 1)
        got = []
        for k in range(ranks):
            part = lax.dynamic_index_in_dim(both, rank ^ k, 0, keepdims=False)
            got.append(part if k == 0 else swap(part, "ctx", 2 * k, ctx_count))
        return got

    def put(into, piece, start, adds=False):
        piece = piece.astype(F32)
        if adds:
            piece = piece + lax.dynamic_slice_in_dim(into, start, piece.shape[1], 1)
        return lax.dynamic_update_slice_in_dim(into, piece, start, 1)

    mid_rows = both_cores(joined(mids))
    hidden_rows = both_cores(joined([h[0] for h in hiddens]), joined([h[1] for h in hiddens]))
    down_product = weight_grad(both_cores(joined(d_mixeds)), hidden_rows)
    d_mid, d_gate_ups = [], []
    for values_in, back_of in zip(d_mixeds, backs):
        total, d_gate_up_of = 0.0, []
        for (w_in, w_out), back in zip(halves, back_of):
            d_gate_up = jnp.concatenate(back(dot(values_in, w_out)), 1).astype(BF16)
            d_gate_up_of.append(d_gate_up)
            total = total + dot_t(d_gate_up, w_in)
        d_gate_ups.append(d_gate_up_of)
        d_mid.append(own_rows(total))
    down_total = over_sequences(down_product)
    dgu_rows = both_cores(joined([d[0] for d in d_gate_ups]), joined([d[1] for d in d_gate_ups]))
    gate_up_product = weight_grad(mid_rows, dgu_rows)
    gate_up_total = over_sequences(gate_up_product)

    grad_mid_gain = sum(jnp.sum(d * v * w, 0) for d, v, w in zip(d_mid, residual, scale_mid))
    d_residual = [
        u + norm_backward(v, w, d * g_mid) for u, v, w, d in zip(ups, residual, scale_mid, d_mid)
    ]
    grad_post_gain = sum(
        jnp.sum(d * v * w, 0) for d, v, w in zip(d_residual, branch, scale_branch)
    )
    d_branches = [
        line_gather(norm_backward(v, w, d * g_post).astype(BF16), ranks)
        for d, v, w in zip(d_residual, branch, scale_branch)
    ]
    d_branches = joined([d[k] for k in range(ranks) for d in d_branches])
    d_residual = joined(d_residual)

    down = spread(down_total)
    d_att_own, d_att_other = dot(d_branches, proj_own), dot(d_branches, proj_other)
    d_attended = jnp.concatenate(ordered(d_att_own, d_att_other), 1).astype(BF16)
    d_attended = d_attended.reshape(rows, heads, HEAD_DIM)
    tanh_again, capped_again = score_rows()
    chances_f = jnp.exp(capped_again - log_total)
    d_values = jnp.einsum(
        "gtl,tgd->ld", chances_f.astype(BF16), d_attended, preferred_element_type=F32
    )
    d_chances = jnp.einsum("tgd,ld->gtl", d_attended, values, preferred_element_type=F32)
    row_inner = jnp.sum(chances_f * d_chances, -1, keepdims=True)
    d_raw = (
        chances_f * (d_chances - row_inner) * (1.0 - tanh_again * tanh_again) * scaling
    ).astype(BF16)
    d_query = jnp.einsum("gtl,ld->tgd", d_raw, keys, preferred_element_type=F32)
    d_keys = jnp.einsum("gtl,tgd->ld", d_raw, query, preferred_element_type=F32)
    d_key_value = jnp.concatenate([d_keys, d_values], 1)
    d_key_value = d_key_value[:rows] + partner(d_key_value[rows:].astype(BF16)).astype(F32)
    d_query_raw = rotate_back(d_query, cosine[:, None], sine_table[:, None]).reshape(
        rows, heads * HEAD_DIM
    )
    d_key_raw = rotate_back(d_key_value[:, :HEAD_DIM], cosine, sine_table)
    dq_own, dq_other = ordered(d_query_raw[:, :q_own], d_query_raw[:, q_own:])
    dkv_own, dkv_other = ordered(d_key_raw, d_key_value[:, HEAD_DIM:])
    dproj_own = jnp.concatenate([dq_own, dkv_own], 1).astype(BF16)
    dproj_other = jnp.concatenate([dq_other, dkv_other], 1).astype(BF16)
    d_in = dot_t(dproj_own, qkv_own) + dot_t(dproj_other, qkv_other)
    grad_pre_gain = jnp.sum(d_in * plain_in, 0)
    d_in = own_rows(d_in)
    d_source = d_residual + norm_backward(source, scale_in[:tokens], d_in * g_pre)

    gate_up_terms = spread(gate_up_total)
    gain_terms = jnp.stack([grad_pre_gain, grad_post_gain, grad_mid_gain, grad_out_gain], 1)
    gain_terms = gain_terms.reshape(ctx_count, fsdp_count, shard_rows, 4)
    gain_terms = gain_terms.transpose(1, 0, 2, 3).reshape(fsdp_count, -1, 4)
    lefts = (grouped(both_cores(normed_in)), grouped(both_cores(d_branches)))
    rights = (both_cores(dproj_own, dproj_other), both_cores(att_own, att_other))

    def attn_part(index):
        at = [lax.dynamic_index_in_dim(v, index, 1, keepdims=False) for v in lefts]
        gain_rows = lax.dynamic_index_in_dim(gain_terms, index, 0, keepdims=False)
        pieces = [
            jnp.einsum("tr,tn->rn", v, right, preferred_element_type=F32)
            for v, right in zip(at, rights)
        ]
        return jnp.concatenate(pieces + [gain_rows], 1)

    attn_total = over_sequences(joined([attn_part(i).astype(BF16) for i in range(fsdp_count)]))
    attn_terms = spread(attn_total)

    grad_mlp_out = jnp.zeros((shard_rows, hidden_width), F32)
    grad_mlp_in = jnp.zeros((shard_rows, 2 * hidden_width), F32)
    grad_attn = jnp.zeros((shard_rows, attn_weights.shape[1]), F32)
    grad_gains = jnp.zeros((shard_rows, 4), F32)
    kv_end, out_end = q_own + HEAD_DIM, 2 * q_own + HEAD_DIM
    for k in range(ranks):
        giver = rank ^ k
        for which in (0, 1):
            start = (2 * giver + which) * f_own
            grad_mlp_out = put(grad_mlp_out, down[k][which], start)
            term = gate_up_terms[k][which]
            grad_mlp_in = put(grad_mlp_in, term[:, :f_own], start)
            grad_mlp_in = put(grad_mlp_in, term[:, f_own:], hidden_width + start)
            term = attn_terms[k][which]
            start = (2 * giver + which) * q_own
            grad_attn = put(grad_attn, term[:, :q_own], start)
            grad_attn = put(grad_attn, term[:, kv_end:out_end], qkv_cols + start)
            start = query_cols + which * key_cols + giver // sharing * HEAD_DIM
            grad_attn = put(grad_attn, term[:, q_own:kv_end], start, sharing > 1)
            grad_gains = grad_gains + term[:, out_end:].astype(F32)
    return (
        joined(block_out).reshape(layer_input.shape),
        d_source.reshape(layer_input.shape),
        grad_attn,
        grad_mlp_in,
        grad_mlp_out,
        grad_gains,
    )


def solution(mesh):
    in_specs = (
        P("fsdp", "ctx", None),
        P("fsdp", None),
        P("fsdp", None),
        P("fsdp", None),
        P("fsdp", None),
        P("fsdp", "ctx", None),
    )
    out_specs = (
        P("fsdp", "ctx", None),
        P("fsdp", "ctx", None),
        P(("ctx", "fsdp"), None),
        P(("ctx", "fsdp"), None),
        P(("ctx", "fsdp"), None),
        P(("ctx", "fsdp"), None),
    )
    return jax.shard_map(local, mesh=mesh, in_specs=in_specs, out_specs=out_specs, check_vma=False)
```

```python
import jax
import jax.numpy as jnp
from jax import lax
from jax.experimental import pallas as pl
from jax.experimental.pallas import tpu as pltpu
from jax.sharding import PartitionSpec as P

HEADS = 8
KV_HEADS = 4
HEAD_DIM = 256

EPSILON = 1e-06
SOFT_CAP = 50.0
ROTARY_BASE = 10000.0
MASKED_SCORE = -1e30
STREAMS = 1

F32 = jnp.float32
BF16 = jnp.bfloat16


def positions_of(rows, half_block, ctx_count):
    owners = rows // (2 * half_block)
    within = rows % (2 * half_block)
    return jnp.where(
        within < half_block,
        owners * half_block + within,
        (2 * ctx_count - 1 - owners) * half_block + within - half_block,
    )


def rotary_tables(places, head_dim):
    half_width = head_dim // 2
    frequency = ROTARY_BASE ** (-jnp.arange(half_width, dtype=F32) * 2.0 / head_dim)
    angles = places.astype(F32)[:, None] * frequency[None, :]
    cosine = jnp.concatenate([jnp.cos(angles), jnp.cos(angles)], -1)
    sine_table = jnp.concatenate([jnp.sin(angles), jnp.sin(angles)], -1)
    return (cosine, sine_table)


def turned(values):
    half_width = values.shape[-1] // 2
    return jnp.concatenate([-values[..., half_width:], values[..., :half_width]], -1)


def rotate(values, cosine, sine_table):
    return values * cosine + turned(values) * sine_table


def rotate_back(grads, cosine, sine_table):
    return grads * cosine - turned(grads * sine_table)


def inverse_rms(values):
    return lax.rsqrt(jnp.mean(values * values, -1, keepdims=True) + EPSILON)


def norm_backward(values, scale, grad_normed):
    normed = values * scale
    return scale * (grad_normed - normed * jnp.mean(grad_normed * normed, -1, keepdims=True))


def geglu(gate, upper):
    return jax.nn.gelu(gate, approximate=True) * upper


def dot(a, b):
    return jnp.dot(a, b, preferred_element_type=F32)


def dot_t(a, b):
    return jnp.einsum("tk,dk->td", a, b, preferred_element_type=F32)


def swap(values, axis, distance, count):
    return lax.ppermute(values, axis, [(i, i ^ distance) for i in range(count)])


def line_gather(values, ranks):
    slots = {0: values}
    bit = ranks // 2
    while bit:
        slots.update({k ^ bit: swap(v, "ctx", 2 * bit, 2 * ranks) for k, v in slots.items()})
        bit //= 2
    return [slots[k] for k in range(ranks)]


def line_scatter(parts, ranks):
    sums = {k: v.astype(F32) for k, v in enumerate(parts)}
    bit = 1
    while bit < ranks:
        for k in sorted(sums, reverse=True):
            if k & bit:
                got = swap(sums.pop(k).astype(BF16), "ctx", 2 * bit, 2 * ranks)
                sums[k ^ bit] = sums[k ^ bit] + got.astype(F32)
        bit *= 2
    return sums[0]


def four_gather(values, ctx_count):
    far, near = swap(values, "ctx", 4, ctx_count), swap(values, "ctx", 2, ctx_count)
    far, near = together(far, near)
    return [values, near, far, swap(far, "ctx", 2, ctx_count)]


def four_scatter(parts, ctx_count, with_first=(), with_far=lambda first: ()):
    by_near = swap(parts[3].astype(BF16), "ctx", 2, ctx_count)
    near, far, by_near, with_first = together(parts[1], parts[2], by_near, with_first)
    far = (far.astype(F32) + by_near.astype(F32)).astype(BF16)
    far = swap(far, "ctx", 4, ctx_count)
    near = swap(near.astype(BF16), "ctx", 2, ctx_count)
    near, far, with_far = together(near, far, with_far(with_first))
    return (parts[0], near, far), with_first, with_far


def sum_of(terms):
    return sum(v.astype(F32) for v in terms)


def square_gather(piece, place, beside):
    rows = piece.shape[0]
    half = rows // 2
    near, far = swap(piece, "fsdp", 1, 4), swap(piece, "fsdp", 2, 4)
    first, then = beside
    near, far, first = together(near, far, first)
    corner_a, corner_b = swap(near[:half], "fsdp", 2, 4), swap(far[half:], "fsdp", 1, 4)
    corner_a, corner_b, second = together(corner_a, corner_b, then(first))
    whole = jnp.zeros((4 * rows, piece.shape[1]), piece.dtype)
    for block, at in (
        (piece, place * rows),
        (near, (place ^ 1) * rows),
        (far, (place ^ 2) * rows),
        (corner_a, (place ^ 3) * rows),
        (corner_b, (place ^ 3) * rows + half),
    ):
        whole = lax.dynamic_update_slice_in_dim(whole, block, at, 0)
    return whole, first, second


def corner_scatter(corner, count):
    half = corner.shape[0] // 2
    corner = corner.astype(BF16)
    return swap(corner[:half], "fsdp", 1, count), swap(corner[half:], "fsdp", 2, count)


def rows_scatter(parts, corners, count):
    half = parts[3].shape[0] // 2
    by_near, by_far = corners[0].astype(F32), corners[1].astype(F32)
    near = jnp.concatenate([parts[1][:half], parts[1][half:] + by_far], 0).astype(BF16)
    far = jnp.concatenate([parts[2][:half] + by_near, parts[2][half:]], 0).astype(BF16)
    near, far = swap(near, "fsdp", 1, count), swap(far, "fsdp", 2, count)
    return parts[0] + near.astype(F32) + far.astype(F32)


def together(*values):
    return lax.optimization_barrier(values)


VMEM_BYTES = 60 * 1024 * 1024


def kernel_call(body, grid, in_specs, out_specs, out_shape, scratch, flops, moved, prefetch=0):
    return pl.pallas_call(
        body,
        grid_spec=pltpu.PrefetchScalarGridSpec(
            num_scalar_prefetch=prefetch,
            grid=grid,
            in_specs=in_specs,
            out_specs=out_specs,
            scratch_shapes=scratch,
        ),
        out_shape=out_shape,
        compiler_params=pltpu.CompilerParams(
            vmem_limit_bytes=VMEM_BYTES, dimension_semantics=("arbitrary",) * len(grid)
        ),
        cost_estimate=pl.CostEstimate(flops=flops, bytes_accessed=moved, transcendentals=0),
    )


def mm(a, b):
    return jnp.dot(a, b, preferred_element_type=F32)


def mm_nt(a, b):
    return lax.dot_general(a, b, (((1,), (1,)), ((), ())), preferred_element_type=F32)


def mm_tn(a, b):
    return lax.dot_general(a, b, (((0,), (0,)), ((), ())), preferred_element_type=F32)


def tile_of(size, most):
    return max(t for t in range(128, most + 1, 128) if size % t == 0)


def gelu_parts(gate):
    rate = 0.7978845608028654
    square = gate * gate
    t = jnp.tanh(rate * gate * (1.0 + 0.044715 * square))
    half = 0.5 * (1.0 + t)
    slope = half + 0.5 * gate * (1.0 - t * t) * rate * (1.0 + 3.0 * 0.044715 * square)
    return gate * half, slope


def stack_rows(pieces, into):
    at = 0
    for ref in pieces:
        into[at : at + ref.shape[0]] = ref[...]
        at += ref.shape[0]


def whole_of(values):
    return [pl.BlockSpec(v.shape, lambda *_, n=len(v.shape): (0,) * n) for v in values]


def core_blocks(shape, steps):
    lead = (0,) * (len(shape) - 1)
    return [
        pl.BlockSpec(shape, lambda h, i, c: (*lead, jnp.where(h == 0, i, steps - 1))),
        pl.BlockSpec(shape, lambda h, i, c: (*lead, jnp.where(h == 0, 0, i))),
    ]


def gate_up_forward(values, w_in, core, most=384):
    rows, width = sum(v.shape[0] for v in values), values[0].shape[1]
    size = w_in.shape[2] // 2
    tile = tile_of(size, most)
    steps = size // tile

    def body(core_ref, *refs):
        g, u, hidden0, hidden1, gate_all, up_all, x = refs[len(values) :]

        @pl.when((pl.program_id(0) == 0) & (pl.program_id(1) == 0))
        def _():
            stack_rows(refs[: len(values)], x)

        gate, up = mm(x[...], g[0]), mm(x[...], u[0])
        gate_all[0] = gate
        up_all[0] = up
        hidden = (gelu_parts(gate)[0] * up).astype(BF16)

        @pl.when(pl.program_id(0) == 0)
        def _():
            hidden0[0] = hidden

        @pl.when(pl.program_id(0) == 1)
        def _():
            hidden1[0] = hidden

    saved = pl.BlockSpec((1, rows, tile), lambda h, i, c: (h, 0, i))
    return kernel_call(
        body,
        (2, steps),
        whole_of(values)
        + [
            pl.BlockSpec((1, width, tile), lambda h, i, c: (c[0] ^ h, 0, i)),
            pl.BlockSpec((1, width, tile), lambda h, i, c: (c[0] ^ h, 0, steps + i)),
        ],
        core_blocks((1, rows, tile), steps) + [saved, saved],
        [jax.ShapeDtypeStruct((1, rows, size), BF16)] * 2
        + [jax.ShapeDtypeStruct((2, rows, size), F32)] * 2,
        [pltpu.VMEM((rows, width), BF16)],
        8 * rows * width * size,
        8 * width * size + 20 * rows * size,
        prefetch=1,
    )(core, *values, w_in, w_in)


def down_forward(hidden, w_out, core, earlier=(), most=768):
    _, rows, size = hidden[0].shape
    width = w_out.shape[1]
    tile = tile_of(width, most)

    def body(core_ref, h0, h1, o0, o1, *refs):
        total = (mm_nt(h0[0], o0[0]) + mm_nt(h1[0], o1[0])).astype(BF16)
        refs[-2][...] = total[: rows // 2]
        refs[-1][...] = total[rows // 2 :]

    whole = pl.BlockSpec((1, rows, size), lambda i, c: (0, 0, 0))
    return kernel_call(
        body,
        (width // tile,),
        [
            whole,
            whole,
            pl.BlockSpec((1, tile, size), lambda i, c: (c[0], i, 0)),
            pl.BlockSpec((1, tile, size), lambda i, c: (1 - c[0], i, 0)),
        ]
        + [pl.BlockSpec(memory_space=pl.ANY)] * len(earlier),
        [pl.BlockSpec((rows // 2, tile), lambda i, c: (0, i))] * 2,
        [jax.ShapeDtypeStruct((rows // 2, width), BF16)] * 2,
        [],
        4 * rows * width * size,
        4 * width * size + 4 * rows * size,
        prefetch=1,
    )(core, *hidden, w_out, w_out, *earlier)


def down_backward(d_mixed, gate_all, up_all, w_out, core, most=384):
    rows, width = sum(v.shape[0] for v in d_mixed), d_mixed[0].shape[1]
    size = w_out.shape[2]
    tile = tile_of(size, most)
    steps = size // tile

    def body(core_ref, *refs):
        gate, up, o, dgu0, dgu1, x = refs[len(d_mixed) :]

        @pl.when((pl.program_id(0) == 0) & (pl.program_id(1) == 0))
        def _():
            stack_rows(refs[: len(d_mixed)], x)

        d_hidden = mm(x[...], o[0])
        value, slope = gelu_parts(gate[0])
        d_gate = (d_hidden * up[0] * slope).astype(BF16)
        d_up = (d_hidden * value).astype(BF16)

        @pl.when(pl.program_id(0) == 0)
        def _():
            dgu0[0] = d_gate
            dgu0[1] = d_up

        @pl.when(pl.program_id(0) == 1)
        def _():
            dgu1[0] = d_gate
            dgu1[1] = d_up

    saved = pl.BlockSpec((1, rows, tile), lambda h, i, c: (h, 0, i))
    return kernel_call(
        body,
        (2, steps),
        whole_of(d_mixed)
        + [saved, saved, pl.BlockSpec((1, width, tile), lambda h, i, c: (c[0] ^ h, 0, i))],
        core_blocks((2, rows, tile), steps),
        [jax.ShapeDtypeStruct((2, rows, size), BF16)] * 2,
        [pltpu.VMEM((rows, width), BF16)],
        4 * rows * width * size,
        4 * width * size + 24 * rows * size,
        prefetch=1,
    )(core, *d_mixed, gate_all, up_all, w_out)


def gate_up_backward(dgu, w_in, core, earlier=(), most=768):
    _, rows, size = dgu[0].shape
    width = w_in.shape[1]
    tile = tile_of(width, most)

    def body(core_ref, d0, d1, w0, w1, *refs):
        total = mm_nt(d0[0], w0[0, :, :size]) + mm_nt(d0[1], w0[0, :, size:])
        total += mm_nt(d1[0], w1[0, :, :size]) + mm_nt(d1[1], w1[0, :, size:])
        refs[-2][...] = total[: rows // 2].astype(BF16)
        refs[-1][...] = total[rows // 2 :].astype(BF16)

    whole = pl.BlockSpec((2, rows, size), lambda i, c: (0, 0, 0))
    return kernel_call(
        body,
        (width // tile,),
        [
            whole,
            whole,
            pl.BlockSpec((1, tile, 2 * size), lambda i, c: (c[0], i, 0)),
            pl.BlockSpec((1, tile, 2 * size), lambda i, c: (1 - c[0], i, 0)),
        ]
        + [pl.BlockSpec(memory_space=pl.ANY)] * len(earlier),
        [pl.BlockSpec((rows // 2, tile), lambda i, c: (0, i))] * 2,
        [jax.ShapeDtypeStruct((rows // 2, width), BF16)] * 2,
        [],
        8 * rows * width * size,
        8 * width * size + 8 * rows * size,
        prefetch=1,
    )(core, *dgu, w_in, w_in, *earlier)


def weight_grad_kernel(lefts, rights, ctx_count, fsdp_count, earlier=()):
    width = lefts[0].shape[1]
    groups, _, size = rights[0].shape
    left_counts = [v.shape[0] for v in lefts]
    counts = [v.shape[1] for v in rights]
    starts = [sum(counts[:i]) for i in range(len(counts))]
    shard = width // (ctx_count * fsdp_count)
    halves = 2
    part, ctx_part = width // halves, ctx_count // halves
    tile = tile_of(size, 1152)
    steps = size // tile

    def body(*refs):
        left_refs, right_refs = refs[: len(lefts)], refs[len(lefts) :][: len(rights)]
        out, turned_left = refs[-2:]

        @pl.when((pl.program_id(1) == 0) & (pl.program_id(2) == 0))
        def _():
            at = 0
            for ref, count in zip(left_refs, left_counts):
                turned_left[:, at : at + count] = ref[...].T
                at += count

        product = 0.0
        for ref, start, count in zip(right_refs, starts, counts):
            product = product + mm(turned_left[:, start : start + count], ref[0])
        for f in range(fsdp_count):
            at = [(c * fsdp_count + f) * shard for c in range(ctx_part)]
            out[f] = jnp.concatenate([product[i : i + shard] for i in at], 0).astype(BF16)

    return kernel_call(
        body,
        (halves, groups, steps),
        [pl.BlockSpec((n, part), lambda h, g, t: (0, h)) for n in left_counts]
        + [pl.BlockSpec((1, n, tile), lambda h, g, t: (g, 0, t)) for n in counts]
        + [pl.BlockSpec(memory_space=pl.ANY)] * len(earlier),
        pl.BlockSpec((fsdp_count, ctx_part * shard, tile), lambda h, g, t: (0, h, g * steps + t)),
        jax.ShapeDtypeStruct((fsdp_count, ctx_count * shard, groups * size), BF16),
        [pltpu.VMEM((part, sum(counts)), BF16)],
        2 * sum(counts) * width * groups * size,
        4 * sum(counts) * (width + groups * size) + 2 * width * groups * size,
    )(*lefts, *rights, *earlier)


def rotated(values, cosine, sine, back=False):
    size = values.shape[1] // 2
    low, high = values[:, :size], values[:, size:]
    if back:
        sine = -sine
    return jnp.concatenate([low * cosine - high * sine, high * cosine + low * sine], 1)


def qkv_kernel(inputs, g_pre, attn, cosine, sine, core):
    rows, width = sum(v.shape[0] for v in inputs), inputs[0].shape[1]
    block = rows // 2
    size = HEAD_DIM

    def body(core_ref, s0, s1, s2, s3, gain, w0, w1, cos, sin, normed_out, q0, q1, kv, x):
        take_slots((s0, s1, s2, s3), x)
        source = x[...].astype(F32)
        normed = (source * inverse_rms(source) * gain[...]).astype(BF16)
        normed_out[...] = normed
        first = core_ref[0] == 0
        own, other = mm(normed, w0[...]), mm(normed, w1[...])
        q0[...] = rotated(own[:, :size], cos[...], sin[...]).astype(BF16)
        q1[...] = rotated(other[:, :size], cos[...], sin[...]).astype(BF16)
        key = jnp.where(first, own[:, size:], other[:, size:])
        kv[:, :size] = rotated(key, cos[...], sin[...]).astype(BF16)
        kv[:, size:] = jnp.where(first, other[:, size:], own[:, size:]).astype(BF16)

    def by_rows(columns):
        return pl.BlockSpec((block, columns), lambda i, c: (i, 0))

    return kernel_call(
        body,
        (2,),
        whole_of(inputs)
        + [
            pl.BlockSpec((1, width), lambda i, c: (0, 0)),
            pl.BlockSpec((width, 2 * size), lambda i, c: (0, 0)),
            pl.BlockSpec((width, 2 * size), lambda i, c: (0, 0)),
            by_rows(size // 2),
            by_rows(size // 2),
        ],
        [by_rows(width), by_rows(size), by_rows(size), by_rows(2 * size)],
        [
            jax.ShapeDtypeStruct((rows, width), BF16),
            jax.ShapeDtypeStruct((rows, size), BF16),
            jax.ShapeDtypeStruct((rows, size), BF16),
            jax.ShapeDtypeStruct((rows, 2 * size), BF16),
        ],
        [pltpu.VMEM((block, width), BF16)],
        8 * rows * width * size,
        8 * width * size + 4 * rows * width,
        prefetch=1,
    )(core, *inputs, g_pre, *attn, cosine, sine)


def scores(query, key, key_place, query_place):
    raw = mm_nt(query, key)
    tanh_part = jnp.tanh(raw * (HEAD_DIM**-0.5 / SOFT_CAP))
    return tanh_part, jnp.where(key_place <= query_place, jnp.exp(SOFT_CAP * tanh_part), 0.0)


def attention_specs(rows, width, block):
    def by_rows(columns):
        return pl.BlockSpec((block, columns), lambda i, c: (i, 0))

    size = HEAD_DIM
    kv = pl.BlockSpec((rows, 2 * size), lambda i, c: (0, 0))
    places = pl.BlockSpec((1, rows), lambda i, c: (0, 0))
    weights = [pl.BlockSpec((width, size), lambda i, c: (0, 2))] * 2
    return by_rows, [by_rows(size), by_rows(size), kv, kv, by_rows(1), places, places] + weights


def put_slots(total, slots):
    rows = slots[0].shape[0]
    for step in range(2):

        @pl.when(pl.program_id(0) == step)
        def _():
            slots[2 * step][...] = total[:rows].astype(BF16)
            slots[2 * step + 1][...] = total[rows:].astype(BF16)


def take_slots(slots, into):
    for step in range(2):
        pl.when(pl.program_id(0) == step)(
            lambda pair=slots[2 * step : 2 * step + 2]: stack_rows(pair, into)
        )


def attention_forward(core, queries, kvs, row_places, key_places, attn):
    rows, width, size = queries[0].shape[0], attn[0].shape[0], HEAD_DIM
    block = rows // 2

    def body(core_ref, q0, q1, kv0, kv1, place, places0, places1, w0, w1, att0, att1, *branch):
        total = 0.0
        for q, att, w in ((q0, att0, w0), (q1, att1, w1)):
            parts = [
                scores(q[...], kv[:, :size], places[...], place[...])[1]
                for kv, places in ((kv0, places0), (kv1, places1))
            ]
            scale = 1.0 / (
                jnp.sum(parts[0], -1, keepdims=True) + jnp.sum(parts[1], -1, keepdims=True)
            )
            attended = mm((parts[0] * scale).astype(BF16), kv0[:, size:])
            attended += mm((parts[1] * scale).astype(BF16), kv1[:, size:])
            attended = attended.astype(BF16)
            att[...] = attended
            total = total + mm_nt(attended, w[...])
        put_slots(total, branch)

    by_rows, specs = attention_specs(rows, width, block)
    slots = [jax.ShapeDtypeStruct((rows // 4, width), BF16)] * 4
    return kernel_call(
        body,
        (2,),
        specs,
        [by_rows(size), by_rows(size)] + whole_of(slots),
        [jax.ShapeDtypeStruct((rows, size), BF16)] * 2 + slots,
        [],
        16 * rows * rows * size + 4 * rows * width * size,
        4 * width * size + 2 * rows * width,
        prefetch=1,
    )(core, *queries, *kvs, row_places, *key_places, *attn)


def attention_backward(
    d_branch, core, queries, kvs, row_places, key_places, attn, cosine, sine
):
    rows, width, size = queries[0].shape[0], attn[0].shape[0], HEAD_DIM
    block = rows // 2
    scaling = size**-0.5

    def body(
        core_ref, q0, q1, kv0, kv1, place, places0, places1, w0, w1, s0, s1, s2, s3, cos, sin,
        dq0, dq1, dkv0, dkv1, sum0, sum1, d_out
    ):
        take_slots((s0, s1, s2, s3), d_out)

        @pl.when(pl.program_id(0) == 0)
        def _():
            sum0[...] = jnp.zeros_like(sum0)
            sum1[...] = jnp.zeros_like(sum1)

        for q, dq, w in ((q0, dq0, w0), (q1, dq1, w1)):
            query = q[...]
            d_att = mm(d_out[...], w[...]).astype(BF16)
            parts = [
                scores(query, kv[:, :size], places[...], place[...])
                for kv, places in ((kv0, places0), (kv1, places1))
            ]
            scale = 1.0 / sum(jnp.sum(e, -1, keepdims=True) for _, e in parts)
            chances = [e * scale for _, e in parts]
            d_chances = [mm_nt(d_att, kv[:, size:]) for kv in (kv0, kv1)]
            inner = sum(
                jnp.sum(p * d, -1, keepdims=True) for p, d in zip(chances, d_chances)
            )
            d_query = 0.0
            for (t, _), p, d, kv, sums in zip(
                parts, chances, d_chances, (kv0, kv1), (sum0, sum1)
            ):
                d_raw = (p * (d - inner) * (1.0 - t * t) * scaling).astype(BF16)
                d_query = d_query + mm(d_raw, kv[:, :size])
                sums[:, :size] += mm_tn(d_raw, query)
                sums[:, size:] += mm_tn(p.astype(BF16), d_att)
            dq[...] = rotated(d_query, cos[...], sin[...], back=True).astype(BF16)

        @pl.when(pl.program_id(0) == pl.num_programs(0) - 1)
        def _():
            dkv0[...] = sum0[...]
            dkv1[...] = sum1[...].astype(BF16)

    by_rows, specs = attention_specs(rows, width, block)
    whole = pl.BlockSpec((rows, 2 * size), lambda i, c: (0, 0))
    return kernel_call(
        body,
        (2,),
        specs + whole_of(d_branch) + [by_rows(size // 2), by_rows(size // 2)],
        [by_rows(size), by_rows(size), whole, whole],
        [
            jax.ShapeDtypeStruct((rows, size), BF16),
            jax.ShapeDtypeStruct((rows, size), BF16),
            jax.ShapeDtypeStruct((rows, 2 * size), F32),
            jax.ShapeDtypeStruct((rows, 2 * size), BF16),
        ],
        [pltpu.VMEM((rows, 2 * size), F32)] * 2 + [pltpu.VMEM((block, width), BF16)],
        40 * rows * rows * size + 4 * rows * width * size,
        4 * width * size + 2 * rows * width,
        prefetch=1,
    )(core, *queries, *kvs, row_places, *key_places, *attn, *d_branch, cosine, sine)


def qkv_backward(inputs, dqs, dkv_mine, dkv_got, attn, cosine, sine, core):
    rows, width = sum(v.shape[0] for v in inputs), inputs[0].shape[1]
    block, size = rows // 2, HEAD_DIM

    def body(core_ref, s0, s1, s2, s3, q0, q1, mine, got, w0, w1, cos, sin, *refs):
        d_in, (dp0, dp1, gain, x) = refs[:4], refs[4:]
        take_slots((s0, s1, s2, s3), x)
        both = mine[...] + got[...].astype(F32)
        d_key = rotated(both[:, :size], cos[...], sin[...], back=True)
        first = core_ref[0] == 0
        dp0[0, :, :size] = q0[...]
        dp1[0, :, :size] = q1[...]
        dp0[0, :, size:] = jnp.where(first, d_key, both[:, size:]).astype(BF16)
        dp1[0, :, size:] = jnp.where(first, both[:, size:], d_key).astype(BF16)
        total = mm_nt(dp0[0], w0[...]) + mm_nt(dp1[0], w1[...])
        put_slots(total, d_in)
        source = x[...].astype(F32)
        term = jnp.sum(total * source * inverse_rms(source), 0, keepdims=True)

        @pl.when(pl.program_id(0) == 0)
        def _():
            gain[...] = jnp.zeros_like(gain)

        gain[...] += term

    def by_rows(columns):
        return pl.BlockSpec((block, columns), lambda i, c: (i, 0))

    weights = [pl.BlockSpec((width, 2 * size), lambda i, c: (0, 0))] * 2
    terms = pl.BlockSpec((1, block, 2 * size), lambda i, c: (0, i, 0))
    return kernel_call(
        body,
        (2,),
        whole_of(inputs)
        + [by_rows(size), by_rows(size), by_rows(2 * size), by_rows(2 * size)]
        + weights
        + [by_rows(size // 2), by_rows(size // 2)],
        whole_of(inputs) + [terms, terms, pl.BlockSpec((1, width), lambda i, c: (0, 0))],
        [jax.ShapeDtypeStruct(v.shape, BF16) for v in inputs]
        + [
            jax.ShapeDtypeStruct((1, rows, 2 * size), BF16),
            jax.ShapeDtypeStruct((1, rows, 2 * size), BF16),
            jax.ShapeDtypeStruct((1, width), F32),
        ],
        [pltpu.VMEM((block, width), BF16)],
        8 * rows * width * size,
        8 * width * size + 4 * rows * width,
        prefetch=1,
    )(core, *inputs, *dqs, dkv_mine, dkv_got, *attn, cosine, sine)


def to_owners(total, ctx_count):
    total = total.reshape(ctx_count, -1, total.shape[1])
    return lax.all_to_all(total, "ctx", split_axis=0, concat_axis=0, tiled=True)


def side_by_side(terms):
    return terms.astype(F32).transpose(1, 0, 2).reshape(terms.shape[1], -1)


def attention_outputs(terms, columns):
    count, rows, _ = terms.shape
    size = HEAD_DIM

    def body(t, grad, gains):
        total = 0.0
        for c in range(count):
            part = t[c].astype(F32)
            kv = count * size + (c % 2) * (count // 2) * size + c // 2 * size
            grad[:, c * size : (c + 1) * size] = part[:, :size]
            grad[:, kv : kv + size] = part[:, size : 2 * size]
            out = columns - (count - c) * size
            grad[:, out : out + size] = part[:, 2 * size : 3 * size]
            total = total + part[:, 3 * size :]
        gains[...] = total

    return pl.pallas_call(
        body,
        out_shape=[
            jax.ShapeDtypeStruct((rows, columns), F32),
            jax.ShapeDtypeStruct((rows, terms.shape[2] - 3 * size), F32),
        ],
        compiler_params=pltpu.CompilerParams(vmem_limit_bytes=VMEM_BYTES),
    )(terms)


def local_kernels(
    layer_input, attn_weights, mlp_in_weights, mlp_out_weights, norm_gains, output_grad
):
    tokens, width = layer_input.shape[1:]
    half_block = tokens // 2
    ctx_count = lax.axis_size("ctx")
    fsdp_count = lax.axis_size("fsdp")
    ranks = ctx_count // 2
    place = lax.axis_index("ctx")
    fsdp_place = lax.axis_index("fsdp")
    rank, core = place // 2, place % 2
    query_cols, key_cols = HEADS * HEAD_DIM, KV_HEADS * HEAD_DIM
    qkv_cols = query_cols + 2 * key_cols
    hidden_width = mlp_out_weights.shape[1]
    f_own = hidden_width // ctx_count
    shard_rows = width // (ctx_count * fsdp_count)

    def partner(values):
        return swap(values, "ctx", 1, ctx_count)

    def columns(array, start, size):
        return lax.dynamic_slice_in_dim(array, start, size, 1)

    chip_groups = [
        [(2 * r + c) * fsdp_count + f for c in (0, 1) for f in range(fsdp_count)]
        for r in range(ranks)
    ]

    def chip_gather(piece):
        whole = lax.all_gather(
            piece, ("ctx", "fsdp"), axis=0, tiled=True, axis_index_groups=chip_groups
        )
        return whole.reshape(2, width, piece.shape[1])

    def over_sequences(product):
        product = product.reshape(width, product.shape[2])
        return lax.psum_scatter(product, "fsdp", scatter_dimension=0, tiled=True)

    own_input = layer_input.reshape(tokens, width)
    source = own_input.astype(F32)
    upstream = output_grad.reshape(tokens, width).astype(F32)
    kv_start = query_cols + core * key_cols + rank * HEAD_DIM
    piece = [
        columns(attn_weights, place * HEAD_DIM, HEAD_DIM),
        columns(attn_weights, kv_start, HEAD_DIM),
        columns(attn_weights, qkv_cols + place * HEAD_DIM, HEAD_DIM),
    ]
    piece, place_in = together(jnp.concatenate(piece, 1), place)
    own_gains = norm_gains.T
    if fsdp_count == 4:
        ways = [swap(own_input, "ctx", 4, ctx_count), swap(own_input, "ctx", 2, ctx_count)]

        def onward(got):
            return swap(got[0], "ctx", 2, ctx_count), [swap(own_gains, "fsdp", k, 4) for k in (1, 2, 3)]

        attn_own, (slot_2, slot_1), (slot_3, gains_got) = square_gather(
            piece, fsdp_place, (ways, onward)
        )
        gains = jnp.zeros((4, width), BF16)
        for k, block in enumerate([own_gains, *gains_got]):
            start = (fsdp_place ^ k) * own_gains.shape[1]
            gains = lax.dynamic_update_slice_in_dim(gains, block, start, 1)
        gains = gains.astype(F32)
        inputs = [own_input, slot_1, slot_2, slot_3]
    else:
        attn_own = lax.all_gather(piece, "fsdp", axis=0, tiled=True)
        inputs = line_gather(own_input, ranks)
        gains = lax.all_gather(own_gains, "fsdp", axis=1, tiled=True).astype(F32)
    attn = (attn_own, partner(attn_own))
    g_pre, g_post, g_mid, g_out = [gains[i] for i in range(4)]
    in_all = chip_gather(
        jnp.concatenate(
            [
                columns(mlp_in_weights, place_in * f_own, f_own),
                columns(mlp_in_weights, hidden_width + place_in * f_own, f_own),
            ],
            1,
        )
    )
    out_all = chip_gather(columns(mlp_out_weights, place_in * f_own, f_own))

    def places_of(which):
        owners = (2 * (rank ^ jnp.arange(ranks, dtype=jnp.int32)) + which)[:, None] * tokens
        gathered_rows = owners + jnp.arange(tokens, dtype=jnp.int32)[None, :]
        return positions_of(gathered_rows.reshape(-1), half_block, ctx_count)

    own_places, other_places = places_of(core), places_of(1 - core)
    cosine, sine = rotary_tables(own_places, HEAD_DIM)
    cosine, sine = cosine[:, : HEAD_DIM // 2], sine[:, : HEAD_DIM // 2]
    row_places, key_places = own_places[:, None], (own_places[None, :], other_places[None, :])
    core_word = core.reshape(1).astype(jnp.int32)

    normed_in, *queries, kv_own = qkv_kernel(
        inputs, gains[:1], attn, cosine, sine, core_word
    )
    attention = (core_word, queries, (kv_own, partner(kv_own)), row_places, key_places, attn)
    att_own, att_other, *branch_parts = attention_forward(*attention)

    def own_rows(halves, beside=()):
        parts = [halves[k % 2][k // 2] for k in range(4)]
        terms, _, beside = four_scatter(parts, ctx_count, (), lambda first: beside)
        return sum_of(terms), beside

    def gathered_halves(values, work):
        slots = four_gather(values, ctx_count)
        done = work([slots[0], slots[2]], 0)
        slots[3], done = together(slots[3], done)
        return [slots[0], slots[2], slots[1], slots[3]], (done, work([slots[1], slots[3]], 1))

    branch = sum_of(four_scatter(branch_parts, ctx_count)[0])
    scale_branch = inverse_rms(branch)
    residual = source + branch * scale_branch * g_post
    scale_mid = inverse_rms(residual)
    mids, forward = gathered_halves(
        (residual * scale_mid * g_mid).astype(BF16), lambda v, _: gate_up_forward(v, in_all, core_word)
    )
    mixed_1 = down_forward(forward[1][:2], out_all, core_word)
    mixed_0 = down_forward(forward[0][:2], out_all, core_word, mixed_1)
    hidden_own = [f[0] for f in forward]
    hidden_got = [partner(f[1]) for f in forward]
    mid_got = [partner(v) for v in mids]
    mixed = own_rows((mixed_0, mixed_1))[0]
    mixed, hidden_own, hidden_got, mid_got = together(mixed, hidden_own, hidden_got, mid_got)
    scale_mixed = inverse_rms(mixed)
    block_out = (residual + mixed * scale_mixed * g_out).astype(BF16)
    grad_out_gain = jnp.sum(upstream * mixed * scale_mixed, 0)
    d_mixeds, d_gate_ups = gathered_halves(
        norm_backward(mixed, scale_mixed, upstream * g_out).astype(BF16),
        lambda v, k: down_backward(v, *forward[k][2:], out_all, core_word),
    )

    def weight_grad(lefts, rights, *earlier):
        return weight_grad_kernel(lefts, rights, ctx_count, fsdp_count, earlier)

    down_product = weight_grad(
        [*d_mixeds, *[partner(v) for v in d_mixeds]], hidden_own + hidden_got
    )
    d_gate_ups, down_product = together(d_gate_ups, down_product)
    down_total = over_sequences(down_product)
    d_mid_1 = gate_up_backward(d_gate_ups[1], in_all, core_word)
    d_mid_0 = gate_up_backward(d_gate_ups[0], in_all, core_word, d_mid_1)
    gate_up_product = weight_grad(
        [*mids, *mid_got],
        [v[0] for v in d_gate_ups] + [partner(v[1]) for v in d_gate_ups],
        *d_mid_0,
    )
    d_mid, (gate_up_product,) = own_rows((d_mid_0, d_mid_1), (gate_up_product,))
    gate_up_total = over_sequences(gate_up_product)
    grad_mid_gain = jnp.sum(d_mid * residual * scale_mid, 0)
    d_residual = upstream + norm_backward(residual, scale_mid, d_mid * g_mid)
    grad_post_gain = jnp.sum(d_residual * branch * scale_branch, 0)
    d_branches = four_gather(
        norm_backward(branch, scale_branch, d_residual * g_post).astype(BF16), ctx_count
    )

    d_branches, down_total = together(d_branches, down_total)
    down = to_owners(down_total, ctx_count)
    *d_queries, dkv_own, dkv_other = attention_backward(d_branches, *attention, cosine, sine)
    *d_in, dproj_own, dproj_other, grad_pre_gain = qkv_backward(
        inputs, d_queries, dkv_own, partner(dkv_other), attn, cosine, sine, core_word
    )

    gain_terms = jnp.stack([grad_pre_gain[0], grad_post_gain, grad_mid_gain, grad_out_gain], 1)
    gain_terms = gain_terms.reshape(ctx_count, fsdp_count, shard_rows, 4)
    gain_terms = gain_terms.transpose(1, 0, 2, 3).reshape(fsdp_count, -1, 4)
    out_product = weight_grad(
        [*d_branches, *[partner(v) for v in d_branches]], [att_own[None], partner(att_other)[None]]
    )
    product = weight_grad([normed_in, partner(normed_in)], [dproj_own, partner(dproj_other)])
    product = jnp.concatenate([product, out_product, gain_terms.astype(BF16)], 2)

    def part(product, k):
        return lax.dynamic_index_in_dim(product, fsdp_place ^ k, 0, keepdims=False)

    def corners_of(first):
        return gate_up_total, corner_scatter(part(first[1], 3), 4) if fsdp_count == 4 else ()

    d_in, (down, product), (gate_up_total, corners) = four_scatter(
        d_in, ctx_count, (down, product), corners_of
    )
    gate_up_terms = to_owners(gate_up_total, ctx_count)
    if fsdp_count == 4:
        parts = [part(product, k).astype(F32) for k in range(4)]
        attn_total = rows_scatter(parts, corners, 4).astype(BF16)
    else:
        attn_total = over_sequences(product)
    gate_up_terms, attn_total = together(gate_up_terms, attn_total)
    attn_terms = to_owners(attn_total, ctx_count)
    d_in = sum_of(d_in)
    d_source = d_residual + norm_backward(source, inverse_rms(source), d_in * g_pre)

    grad_mlp_out = side_by_side(down)
    grad_mlp_in = jnp.concatenate(
        [side_by_side(gate_up_terms[:, :, :f_own]), side_by_side(gate_up_terms[:, :, f_own:])], 1
    )
    grad_attn, grad_gains = attention_outputs(attn_terms, attn_weights.shape[1])
    return (
        block_out.reshape(layer_input.shape),
        d_source.reshape(layer_input.shape),
        grad_attn,
        grad_mlp_in,
        grad_mlp_out,
        grad_gains,
    )


def local(layer_input, attn_weights, mlp_in_weights, mlp_out_weights, norm_gains, output_grad):
    ctx_count, fsdp_count = lax.axis_size("ctx"), lax.axis_size("fsdp")
    width, hidden_width = layer_input.shape[2], mlp_out_weights.shape[1]
    fits = (
        ctx_count == HEADS == 2 * KV_HEADS == 8
        and hidden_width % (128 * ctx_count) == 0
        and width % 256 == 0
        and width % (8 * ctx_count * fsdp_count) == 0
        and (width // fsdp_count) % 32 == 0
    )
    path = local_kernels if fits else local_general
    return path(
        layer_input, attn_weights, mlp_in_weights, mlp_out_weights, norm_gains, output_grad
    )


def local_general(layer_input, attn_weights, mlp_in_weights, mlp_out_weights, norm_gains, output_grad):
    tokens, width = layer_input.shape[1:]
    half_block = tokens // 2
    ctx_count = lax.axis_size("ctx")
    fsdp_count = lax.axis_size("fsdp")
    ranks = ctx_count // 2
    place = lax.axis_index("ctx")
    rank, core = place // 2, place % 2
    first_core = core == 0
    query_cols, key_cols = HEADS * HEAD_DIM, KV_HEADS * HEAD_DIM
    qkv_cols = query_cols + 2 * key_cols
    heads = HEADS // ranks
    sharing = ranks // KV_HEADS
    hidden_width = mlp_out_weights.shape[1]
    q_own = query_cols // ctx_count
    f_own = hidden_width // ctx_count
    shard_rows = width // (ctx_count * fsdp_count)
    scaling = HEAD_DIM**-0.5

    def partner(values):
        return swap(values, "ctx", 1, ctx_count)

    def columns(array, start, size):
        return lax.dynamic_slice_in_dim(array, start, size, 1)


    kv_start = query_cols + core * key_cols + rank // sharing * HEAD_DIM
    attn_piece = (
        columns(attn_weights, place * q_own, q_own),
        columns(attn_weights, kv_start, HEAD_DIM),
        columns(attn_weights, qkv_cols + place * q_own, q_own),
    )
    attn_own = lax.all_gather(jnp.concatenate(attn_piece, 1), "fsdp", axis=0, tiled=True)
    in_piece = (
        columns(mlp_in_weights, place * f_own, f_own),
        columns(mlp_in_weights, hidden_width + place * f_own, f_own),
    )
    in_piece = jnp.concatenate(in_piece, 1)
    out_piece = columns(mlp_out_weights, place * f_own, f_own)
    in_own = lax.all_gather(in_piece, "fsdp", axis=0, tiled=True)
    out_own = lax.all_gather(out_piece, "fsdp", axis=0, tiled=True)
    gains = lax.all_gather(norm_gains, "fsdp", axis=0, tiled=True).astype(F32)
    g_pre, g_post, g_mid, g_out = [gains[:, i] for i in range(4)]
    attn_other = partner(attn_own)
    qkv_own, proj_own = attn_own[:, : q_own + HEAD_DIM], attn_own[:, q_own + HEAD_DIM :]
    qkv_other, proj_other = attn_other[:, : q_own + HEAD_DIM], attn_other[:, q_own + HEAD_DIM :]

    own_input = layer_input.reshape(tokens, width)
    source = own_input.astype(F32)
    upstream = output_grad.reshape(tokens, width).astype(F32)
    inputs = jnp.concatenate(line_gather(own_input, ranks), 0).astype(F32)
    scale_in = inverse_rms(inputs)
    plain_in = inputs * scale_in
    normed_in = (plain_in * g_pre).astype(BF16)

    def places_of(which):
        slots = rank ^ jnp.arange(ranks, dtype=jnp.int32)
        owners = (2 * slots + which)[:, None] * tokens
        rows = owners + jnp.arange(tokens, dtype=jnp.int32)[None, :]
        return positions_of(rows.reshape(-1), half_block, ctx_count)

    own_places, other_places = places_of(core), places_of(1 - core)
    cosine, sine_table = rotary_tables(own_places, HEAD_DIM)
    all_places = jnp.concatenate([own_places, other_places], 0)
    allowed = all_places[None, :] <= own_places[:, None]
    rows = ranks * tokens

    def ordered(mine, theirs):
        return jnp.where(first_core, mine, theirs), jnp.where(first_core, theirs, mine)

    proj_a, proj_b = dot(normed_in, qkv_own), dot(normed_in, qkv_other)
    query_raw = jnp.concatenate(ordered(proj_a[:, :q_own], proj_b[:, :q_own]), 1)
    key_raw, value_raw = ordered(proj_a[:, q_own:], proj_b[:, q_own:])
    query = rotate(
        query_raw.reshape(rows, heads, HEAD_DIM), cosine[:, None], sine_table[:, None]
    ).astype(BF16)
    key_own = rotate(key_raw, cosine, sine_table).astype(BF16)
    value_own = value_raw.astype(BF16)
    key_value = jnp.concatenate([key_own, value_own], 1)
    key_value = jnp.concatenate([key_value, partner(key_value)], 0)
    keys, values = key_value[:, :HEAD_DIM], key_value[:, HEAD_DIM:]

    def score_rows():
        raw_scores = jnp.einsum("tgd,ld->gtl", query, keys, preferred_element_type=F32)
        tanh_part = jnp.tanh(raw_scores * scaling / SOFT_CAP)
        return tanh_part, jnp.where(allowed, SOFT_CAP * tanh_part, MASKED_SCORE)

    tanh_part, capped = score_rows()
    row_max = jnp.max(capped, -1, keepdims=True)
    weights = jnp.exp(capped - row_max)
    row_total = jnp.sum(weights, -1, keepdims=True)
    log_total = row_max + jnp.log(row_total)
    chances = (weights / row_total).astype(BF16)
    attended = jnp.einsum("gtl,ld->tgd", chances, values, preferred_element_type=F32)
    attended = attended.reshape(rows, heads * HEAD_DIM).astype(BF16)
    att_own, att_other = ordered(attended[:, :q_own], attended[:, q_own:])
    branch_parts = (dot_t(att_own, proj_own) + dot_t(att_other, proj_other)).reshape(
        ranks, tokens, width
    )

    span = tokens // STREAMS
    cuts = [slice(s * span, (s + 1) * span) for s in range(STREAMS)]

    def own_rows(parts):
        return line_scatter(list(parts.reshape(ranks, -1, width)), ranks)

    def all_rows(values):
        return jnp.concatenate(line_gather(values, ranks), 0)

    branch = [own_rows(branch_parts[:, cut]) for cut in cuts]
    halves = ((in_own, out_own), (partner(in_own), partner(out_own)))
    scale_branch = [inverse_rms(v) for v in branch]
    residual = [source[cut] + v * w * g_post for cut, v, w in zip(cuts, branch, scale_branch)]
    scale_mid = [inverse_rms(v) for v in residual]
    mids = [all_rows((v * w * g_mid).astype(BF16)) for v, w in zip(residual, scale_mid)]
    hiddens, backs, mixed = [], [], []
    for values_in in mids:
        hidden_of, back_of, total = [], [], 0.0
        for w_in, w_out in halves:
            gate_up = dot(values_in, w_in)
            hidden, back = jax.vjp(geglu, gate_up[:, :f_own], gate_up[:, f_own:])
            hidden_of.append(hidden.astype(BF16))
            back_of.append(back)
            total = total + dot_t(hidden_of[-1], w_out)
        hiddens.append(hidden_of)
        backs.append(back_of)
        mixed.append(own_rows(total))
    scale_mixed = [inverse_rms(v) for v in mixed]
    block_out = [
        (r + v * w * g_out).astype(BF16) for r, v, w in zip(residual, mixed, scale_mixed)
    ]
    ups = [upstream[cut] for cut in cuts]
    grad_out_gain = sum(jnp.sum(u * v * w, 0) for u, v, w in zip(ups, mixed, scale_mixed))
    d_mixeds = [
        all_rows(norm_backward(v, w, u * g_out).astype(BF16))
        for u, v, w in zip(ups, mixed, scale_mixed)
    ]

    def both_cores(mine, others=None):
        return jnp.concatenate([mine, partner(mine if others is None else others)], 0)

    def joined(pieces):
        return jnp.concatenate(pieces, 0)

    def grouped(left):
        left = left.reshape(left.shape[0], ctx_count, fsdp_count, shard_rows)
        return left.transpose(0, 2, 1, 3).reshape(left.shape[0], fsdp_count, ctx_count * shard_rows)

    def weight_grad(left, right):
        product = jnp.einsum("tfr,tn->frn", grouped(left), right, preferred_element_type=F32)
        return product.reshape(width, right.shape[1]).astype(BF16)

    def over_sequences(product):
        total = lax.psum_scatter(product, "fsdp", scatter_dimension=0, tiled=True)
        return total.reshape(ranks, 2, shard_rows, product.shape[1])

    def spread(total):
        mine = jnp.where(first_core, total[:, 0], total[:, 1])
        theirs = partner(jnp.where(first_core, total[:, 1], total[:, 0]))
        both = jnp.stack(ordered(mine, theirs), 1)
        got = []
        for k in range(ranks):
            part = lax.dynamic_index_in_dim(both, rank ^ k, 0, keepdims=False)
            got.append(part if k == 0 else swap(part, "ctx", 2 * k, ctx_count))
        return got

    def put(into, piece, start, adds=False):
        piece = piece.astype(F32)
        if adds:
            piece = piece + lax.dynamic_slice_in_dim(into, start, piece.shape[1], 1)
        return lax.dynamic_update_slice_in_dim(into, piece, start, 1)

    mid_rows = both_cores(joined(mids))
    hidden_rows = both_cores(joined([h[0] for h in hiddens]), joined([h[1] for h in hiddens]))
    down_product = weight_grad(both_cores(joined(d_mixeds)), hidden_rows)
    d_mid, d_gate_ups = [], []
    for values_in, back_of in zip(d_mixeds, backs):
        total, d_gate_up_of = 0.0, []
        for (w_in, w_out), back in zip(halves, back_of):
            d_gate_up = jnp.concatenate(back(dot(values_in, w_out)), 1).astype(BF16)
            d_gate_up_of.append(d_gate_up)
            total = total + dot_t(d_gate_up, w_in)
        d_gate_ups.append(d_gate_up_of)
        d_mid.append(own_rows(total))
    down_total = over_sequences(down_product)
    dgu_rows = both_cores(joined([d[0] for d in d_gate_ups]), joined([d[1] for d in d_gate_ups]))
    gate_up_product = weight_grad(mid_rows, dgu_rows)
    gate_up_total = over_sequences(gate_up_product)

    grad_mid_gain = sum(jnp.sum(d * v * w, 0) for d, v, w in zip(d_mid, residual, scale_mid))
    d_residual = [
        u + norm_backward(v, w, d * g_mid) for u, v, w, d in zip(ups, residual, scale_mid, d_mid)
    ]
    grad_post_gain = sum(
        jnp.sum(d * v * w, 0) for d, v, w in zip(d_residual, branch, scale_branch)
    )
    d_branches = [
        line_gather(norm_backward(v, w, d * g_post).astype(BF16), ranks)
        for d, v, w in zip(d_residual, branch, scale_branch)
    ]
    d_branches = joined([d[k] for k in range(ranks) for d in d_branches])
    d_residual = joined(d_residual)

    down = spread(down_total)
    d_att_own, d_att_other = dot(d_branches, proj_own), dot(d_branches, proj_other)
    d_attended = jnp.concatenate(ordered(d_att_own, d_att_other), 1).astype(BF16)
    d_attended = d_attended.reshape(rows, heads, HEAD_DIM)
    tanh_again, capped_again = score_rows()
    chances_f = jnp.exp(capped_again - log_total)
    d_values = jnp.einsum(
        "gtl,tgd->ld", chances_f.astype(BF16), d_attended, preferred_element_type=F32
    )
    d_chances = jnp.einsum("tgd,ld->gtl", d_attended, values, preferred_element_type=F32)
    row_inner = jnp.sum(chances_f * d_chances, -1, keepdims=True)
    d_raw = (
        chances_f * (d_chances - row_inner) * (1.0 - tanh_again * tanh_again) * scaling
    ).astype(BF16)
    d_query = jnp.einsum("gtl,ld->tgd", d_raw, keys, preferred_element_type=F32)
    d_keys = jnp.einsum("gtl,tgd->ld", d_raw, query, preferred_element_type=F32)
    d_key_value = jnp.concatenate([d_keys, d_values], 1)
    d_key_value = d_key_value[:rows] + partner(d_key_value[rows:].astype(BF16)).astype(F32)
    d_query_raw = rotate_back(d_query, cosine[:, None], sine_table[:, None]).reshape(
        rows, heads * HEAD_DIM
    )
    d_key_raw = rotate_back(d_key_value[:, :HEAD_DIM], cosine, sine_table)
    dq_own, dq_other = ordered(d_query_raw[:, :q_own], d_query_raw[:, q_own:])
    dkv_own, dkv_other = ordered(d_key_raw, d_key_value[:, HEAD_DIM:])
    dproj_own = jnp.concatenate([dq_own, dkv_own], 1).astype(BF16)
    dproj_other = jnp.concatenate([dq_other, dkv_other], 1).astype(BF16)
    d_in = dot_t(dproj_own, qkv_own) + dot_t(dproj_other, qkv_other)
    grad_pre_gain = jnp.sum(d_in * plain_in, 0)
    d_in = own_rows(d_in)
    d_source = d_residual + norm_backward(source, scale_in[:tokens], d_in * g_pre)

    gate_up_terms = spread(gate_up_total)
    gain_terms = jnp.stack([grad_pre_gain, grad_post_gain, grad_mid_gain, grad_out_gain], 1)
    gain_terms = gain_terms.reshape(ctx_count, fsdp_count, shard_rows, 4)
    gain_terms = gain_terms.transpose(1, 0, 2, 3).reshape(fsdp_count, -1, 4)
    lefts = (grouped(both_cores(normed_in)), grouped(both_cores(d_branches)))
    rights = (both_cores(dproj_own, dproj_other), both_cores(att_own, att_other))

    def attn_part(index):
        at = [lax.dynamic_index_in_dim(v, index, 1, keepdims=False) for v in lefts]
        gain_rows = lax.dynamic_index_in_dim(gain_terms, index, 0, keepdims=False)
        pieces = [
            jnp.einsum("tr,tn->rn", v, right, preferred_element_type=F32)
            for v, right in zip(at, rights)
        ]
        return jnp.concatenate(pieces + [gain_rows], 1)

    attn_total = over_sequences(joined([attn_part(i).astype(BF16) for i in range(fsdp_count)]))
    attn_terms = spread(attn_total)

    grad_mlp_out = jnp.zeros((shard_rows, hidden_width), F32)
    grad_mlp_in = jnp.zeros((shard_rows, 2 * hidden_width), F32)
    grad_attn = jnp.zeros((shard_rows, attn_weights.shape[1]), F32)
    grad_gains = jnp.zeros((shard_rows, 4), F32)
    kv_end, out_end = q_own + HEAD_DIM, 2 * q_own + HEAD_DIM
    for k in range(ranks):
        giver = rank ^ k
        for which in (0, 1):
            start = (2 * giver + which) * f_own
            grad_mlp_out = put(grad_mlp_out, down[k][which], start)
            term = gate_up_terms[k][which]
            grad_mlp_in = put(grad_mlp_in, term[:, :f_own], start)
            grad_mlp_in = put(grad_mlp_in, term[:, f_own:], hidden_width + start)
            term = attn_terms[k][which]
            start = (2 * giver + which) * q_own
            grad_attn = put(grad_attn, term[:, :q_own], start)
            grad_attn = put(grad_attn, term[:, kv_end:out_end], qkv_cols + start)
            start = query_cols + which * key_cols + giver // sharing * HEAD_DIM
            grad_attn = put(grad_attn, term[:, q_own:kv_end], start, sharing > 1)
            grad_gains = grad_gains + term[:, out_end:].astype(F32)
    return (
        joined(block_out).reshape(layer_input.shape),
        d_source.reshape(layer_input.shape),
        grad_attn,
        grad_mlp_in,
        grad_mlp_out,
        grad_gains,
    )


def solution(mesh):
    in_specs = (
        P("fsdp", "ctx", None),
        P("fsdp", None),
        P("fsdp", None),
        P("fsdp", None),
        P("fsdp", None),
        P("fsdp", "ctx", None),
    )
    out_specs = (
        P("fsdp", "ctx", None),
        P("fsdp", "ctx", None),
        P(("ctx", "fsdp"), None),
        P(("ctx", "fsdp"), None),
        P(("ctx", "fsdp"), None),
        P(("ctx", "fsdp"), None),
    )
    return jax.shard_map(local, mesh=mesh, in_specs=in_specs, out_specs=out_specs, check_vma=False)
```

```python
import jax
import jax.numpy as jnp
from jax import lax
from jax.experimental import pallas as pl
from jax.experimental.pallas import tpu as pltpu
from jax.sharding import PartitionSpec as P

HEADS = 8
KV_HEADS = 4
HEAD_DIM = 256

EPSILON = 1e-06
SOFT_CAP = 50.0
ROTARY_BASE = 10000.0
MASKED_SCORE = -1e30
STREAMS = 1

F32 = jnp.float32
BF16 = jnp.bfloat16


def positions_of(rows, half_block, ctx_count):
    owners = rows // (2 * half_block)
    within = rows % (2 * half_block)
    return jnp.where(
        within < half_block,
        owners * half_block + within,
        (2 * ctx_count - 1 - owners) * half_block + within - half_block,
    )


def rotary_tables(places, head_dim):
    half_width = head_dim // 2
    frequency = ROTARY_BASE ** (-jnp.arange(half_width, dtype=F32) * 2.0 / head_dim)
    angles = places.astype(F32)[:, None] * frequency[None, :]
    cosine = jnp.concatenate([jnp.cos(angles), jnp.cos(angles)], -1)
    sine_table = jnp.concatenate([jnp.sin(angles), jnp.sin(angles)], -1)
    return (cosine, sine_table)


def turned(values):
    half_width = values.shape[-1] // 2
    return jnp.concatenate([-values[..., half_width:], values[..., :half_width]], -1)


def rotate(values, cosine, sine_table):
    return values * cosine + turned(values) * sine_table


def rotate_back(grads, cosine, sine_table):
    return grads * cosine - turned(grads * sine_table)


def inverse_rms(values):
    return lax.rsqrt(jnp.mean(values * values, -1, keepdims=True) + EPSILON)


def norm_backward(values, scale, grad_normed):
    normed = values * scale
    return scale * (grad_normed - normed * jnp.mean(grad_normed * normed, -1, keepdims=True))


def geglu(gate, upper):
    return jax.nn.gelu(gate, approximate=True) * upper


def dot(a, b):
    return jnp.dot(a, b, preferred_element_type=F32)


def dot_t(a, b):
    return jnp.einsum("tk,dk->td", a, b, preferred_element_type=F32)


def swap(values, axis, distance, count):
    return lax.ppermute(values, axis, [(i, i ^ distance) for i in range(count)])


def line_gather(values, ranks):
    slots = {0: values}
    bit = ranks // 2
    while bit:
        slots.update({k ^ bit: swap(v, "ctx", 2 * bit, 2 * ranks) for k, v in slots.items()})
        bit //= 2
    return [slots[k] for k in range(ranks)]


def line_scatter(parts, ranks):
    sums = {k: v.astype(F32) for k, v in enumerate(parts)}
    bit = 1
    while bit < ranks:
        for k in sorted(sums, reverse=True):
            if k & bit:
                got = swap(sums.pop(k).astype(BF16), "ctx", 2 * bit, 2 * ranks)
                sums[k ^ bit] = sums[k ^ bit] + got.astype(F32)
        bit *= 2
    return sums[0]


def four_gather(values, ctx_count):
    far, near = swap(values, "ctx", 4, ctx_count), swap(values, "ctx", 2, ctx_count)
    far, near = together(far, near)
    return [values, near, far, swap(far, "ctx", 2, ctx_count)]


def four_scatter(parts, ctx_count, with_first=(), with_far=lambda first: ()):
    by_near = swap(parts[3].astype(BF16), "ctx", 2, ctx_count)
    near, far, by_near, with_first = together(parts[1], parts[2], by_near, with_first)
    far = (far.astype(F32) + by_near.astype(F32)).astype(BF16)
    far = swap(far, "ctx", 4, ctx_count)
    near = swap(near.astype(BF16), "ctx", 2, ctx_count)
    near, far, with_far = together(near, far, with_far(with_first))
    return (parts[0], near, far), with_first, with_far


def sum_of(terms):
    return sum(v.astype(F32) for v in terms)


def square_gather(piece, place, beside):
    rows = piece.shape[0]
    half = rows // 2
    near, far = swap(piece, "fsdp", 1, 4), swap(piece, "fsdp", 2, 4)
    first, then = beside
    near, far, first = together(near, far, first)
    corner_a, corner_b = swap(near[:half], "fsdp", 2, 4), swap(far[half:], "fsdp", 1, 4)
    corner_a, corner_b, second = together(corner_a, corner_b, then(first))
    whole = jnp.zeros((4 * rows, piece.shape[1]), piece.dtype)
    for block, at in (
        (piece, place * rows),
        (near, (place ^ 1) * rows),
        (far, (place ^ 2) * rows),
        (corner_a, (place ^ 3) * rows),
        (corner_b, (place ^ 3) * rows + half),
    ):
        whole = lax.dynamic_update_slice_in_dim(whole, block, at, 0)
    return whole, first, second


def corner_scatter(corner, count):
    half = corner.shape[0] // 2
    corner = corner.astype(BF16)
    return swap(corner[:half], "fsdp", 1, count), swap(corner[half:], "fsdp", 2, count)


def rows_scatter(parts, corners, count):
    half = parts[3].shape[0] // 2
    by_near, by_far = corners[0].astype(F32), corners[1].astype(F32)
    near = jnp.concatenate([parts[1][:half], parts[1][half:] + by_far], 0).astype(BF16)
    far = jnp.concatenate([parts[2][:half] + by_near, parts[2][half:]], 0).astype(BF16)
    near, far = swap(near, "fsdp", 1, count), swap(far, "fsdp", 2, count)
    return parts[0] + near.astype(F32) + far.astype(F32)


def together(*values):
    return lax.optimization_barrier(values)


VMEM_BYTES = 60 * 1024 * 1024


def kernel_call(body, grid, in_specs, out_specs, out_shape, scratch, flops, moved, prefetch=0):
    return pl.pallas_call(
        body,
        grid_spec=pltpu.PrefetchScalarGridSpec(
            num_scalar_prefetch=prefetch,
            grid=grid,
            in_specs=in_specs,
            out_specs=out_specs,
            scratch_shapes=scratch,
        ),
        out_shape=out_shape,
        compiler_params=pltpu.CompilerParams(
            vmem_limit_bytes=VMEM_BYTES, dimension_semantics=("arbitrary",) * len(grid)
        ),
        cost_estimate=pl.CostEstimate(flops=flops, bytes_accessed=moved, transcendentals=0),
    )


def mm(a, b):
    return jnp.dot(a, b, preferred_element_type=F32)


def mm_nt(a, b):
    return lax.dot_general(a, b, (((1,), (1,)), ((), ())), preferred_element_type=F32)


def mm_tn(a, b):
    return lax.dot_general(a, b, (((0,), (0,)), ((), ())), preferred_element_type=F32)


def tile_of(size, most):
    return max(t for t in range(128, most + 1, 128) if size % t == 0)


def gelu_parts(gate):
    rate = 0.7978845608028654
    square = gate * gate
    t = jnp.tanh(rate * gate * (1.0 + 0.044715 * square))
    half = 0.5 * (1.0 + t)
    slope = half + 0.5 * gate * (1.0 - t * t) * rate * (1.0 + 3.0 * 0.044715 * square)
    return gate * half, slope


def stack_rows(pieces, into):
    at = 0
    for ref in pieces:
        into[at : at + ref.shape[0]] = ref[...]
        at += ref.shape[0]


def whole_of(values):
    return [pl.BlockSpec(v.shape, lambda *_, n=len(v.shape): (0,) * n) for v in values]


def core_blocks(shape, steps):
    lead = (0,) * (len(shape) - 1)
    return [
        pl.BlockSpec(shape, lambda h, i, c: (*lead, jnp.where(h == 0, i, steps - 1))),
        pl.BlockSpec(shape, lambda h, i, c: (*lead, jnp.where(h == 0, 0, i))),
    ]


def gate_up_forward(values, w_in, core, most=384):
    rows, width = sum(v.shape[0] for v in values), values[0].shape[1]
    size = w_in.shape[2] // 2
    tile = tile_of(size, most)
    steps = size // tile

    def body(core_ref, *refs):
        g, u, hidden0, hidden1, gate_all, up_all, x = refs[len(values) :]

        @pl.when((pl.program_id(0) == 0) & (pl.program_id(1) == 0))
        def _():
            stack_rows(refs[: len(values)], x)

        gate, up = mm(x[...], g[0]), mm(x[...], u[0])
        gate_all[0] = gate
        up_all[0] = up
        hidden = (gelu_parts(gate)[0] * up).astype(BF16)

        @pl.when(pl.program_id(0) == 0)
        def _():
            hidden0[0] = hidden

        @pl.when(pl.program_id(0) == 1)
        def _():
            hidden1[0] = hidden

    saved = pl.BlockSpec((1, rows, tile), lambda h, i, c: (h, 0, i))
    return kernel_call(
        body,
        (2, steps),
        whole_of(values)
        + [
            pl.BlockSpec((1, width, tile), lambda h, i, c: (c[0] ^ h, 0, i)),
            pl.BlockSpec((1, width, tile), lambda h, i, c: (c[0] ^ h, 0, steps + i)),
        ],
        core_blocks((1, rows, tile), steps) + [saved, saved],
        [jax.ShapeDtypeStruct((1, rows, size), BF16)] * 2
        + [jax.ShapeDtypeStruct((2, rows, size), F32)] * 2,
        [pltpu.VMEM((rows, width), BF16)],
        8 * rows * width * size,
        8 * width * size + 20 * rows * size,
        prefetch=1,
    )(core, *values, w_in, w_in)


def down_forward(hidden, w_out, core, earlier=(), most=768):
    _, rows, size = hidden[0].shape
    width = w_out.shape[1]
    tile = tile_of(width, most)

    def body(core_ref, h0, h1, o0, o1, *refs):
        total = (mm_nt(h0[0], o0[0]) + mm_nt(h1[0], o1[0])).astype(BF16)
        refs[-2][...] = total[: rows // 2]
        refs[-1][...] = total[rows // 2 :]

    whole = pl.BlockSpec((1, rows, size), lambda i, c: (0, 0, 0))
    return kernel_call(
        body,
        (width // tile,),
        [
            whole,
            whole,
            pl.BlockSpec((1, tile, size), lambda i, c: (c[0], i, 0)),
            pl.BlockSpec((1, tile, size), lambda i, c: (1 - c[0], i, 0)),
        ]
        + [pl.BlockSpec(memory_space=pl.ANY)] * len(earlier),
        [pl.BlockSpec((rows // 2, tile), lambda i, c: (0, i))] * 2,
        [jax.ShapeDtypeStruct((rows // 2, width), BF16)] * 2,
        [],
        4 * rows * width * size,
        4 * width * size + 4 * rows * size,
        prefetch=1,
    )(core, *hidden, w_out, w_out, *earlier)


def down_backward(d_mixed, gate_all, up_all, w_out, core, most=1152):
    rows, width = sum(v.shape[0] for v in d_mixed), d_mixed[0].shape[1]
    size = w_out.shape[2]
    tile = tile_of(size, most)
    steps = size // tile

    def body(core_ref, *refs):
        gate, up, o, dgu0, dgu1, x = refs[len(d_mixed) :]

        @pl.when((pl.program_id(0) == 0) & (pl.program_id(1) == 0))
        def _():
            stack_rows(refs[: len(d_mixed)], x)

        d_hidden = mm(x[...], o[0])
        value, slope = gelu_parts(gate[0])
        d_gate = (d_hidden * up[0] * slope).astype(BF16)
        d_up = (d_hidden * value).astype(BF16)

        @pl.when(pl.program_id(0) == 0)
        def _():
            dgu0[0] = d_gate
            dgu0[1] = d_up

        @pl.when(pl.program_id(0) == 1)
        def _():
            dgu1[0] = d_gate
            dgu1[1] = d_up

    saved = pl.BlockSpec((1, rows, tile), lambda h, i, c: (h, 0, i))
    return kernel_call(
        body,
        (2, steps),
        whole_of(d_mixed)
        + [saved, saved, pl.BlockSpec((1, width, tile), lambda h, i, c: (c[0] ^ h, 0, i))],
        core_blocks((2, rows, tile), steps),
        [jax.ShapeDtypeStruct((2, rows, size), BF16)] * 2,
        [pltpu.VMEM((rows, width), BF16)],
        4 * rows * width * size,
        4 * width * size + 24 * rows * size,
        prefetch=1,
    )(core, *d_mixed, gate_all, up_all, w_out)


def gate_up_backward(dgu, w_in, core, earlier=(), most=768):
    _, rows, size = dgu[0].shape
    width = w_in.shape[1]
    tile = tile_of(width, most)

    def body(core_ref, d0, d1, w0, w1, *refs):
        total = mm_nt(d0[0], w0[0, :, :size]) + mm_nt(d0[1], w0[0, :, size:])
        total += mm_nt(d1[0], w1[0, :, :size]) + mm_nt(d1[1], w1[0, :, size:])
        refs[-2][...] = total[: rows // 2].astype(BF16)
        refs[-1][...] = total[rows // 2 :].astype(BF16)

    whole = pl.BlockSpec((2, rows, size), lambda i, c: (0, 0, 0))
    return kernel_call(
        body,
        (width // tile,),
        [
            whole,
            whole,
            pl.BlockSpec((1, tile, 2 * size), lambda i, c: (c[0], i, 0)),
            pl.BlockSpec((1, tile, 2 * size), lambda i, c: (1 - c[0], i, 0)),
        ]
        + [pl.BlockSpec(memory_space=pl.ANY)] * len(earlier),
        [pl.BlockSpec((rows // 2, tile), lambda i, c: (0, i))] * 2,
        [jax.ShapeDtypeStruct((rows // 2, width), BF16)] * 2,
        [],
        8 * rows * width * size,
        8 * width * size + 8 * rows * size,
        prefetch=1,
    )(core, *dgu, w_in, w_in, *earlier)


def weight_grad_kernel(lefts, rights, ctx_count, fsdp_count, earlier=()):
    width = lefts[0].shape[1]
    groups, _, size = rights[0].shape
    left_counts = [v.shape[0] for v in lefts]
    counts = [v.shape[1] for v in rights]
    starts = [sum(counts[:i]) for i in range(len(counts))]
    shard = width // (ctx_count * fsdp_count)
    halves = 2
    part, ctx_part = width // halves, ctx_count // halves
    tile = tile_of(size, 1152)
    steps = size // tile

    def body(*refs):
        left_refs, right_refs = refs[: len(lefts)], refs[len(lefts) :][: len(rights)]
        out, turned_left = refs[-2:]

        @pl.when((pl.program_id(1) == 0) & (pl.program_id(2) == 0))
        def _():
            at = 0
            for ref, count in zip(left_refs, left_counts):
                turned_left[:, at : at + count] = ref[...].T
                at += count

        product = 0.0
        for ref, start, count in zip(right_refs, starts, counts):
            product = product + mm(turned_left[:, start : start + count], ref[0])
        for f in range(fsdp_count):
            at = [(c * fsdp_count + f) * shard for c in range(ctx_part)]
            out[f] = jnp.concatenate([product[i : i + shard] for i in at], 0).astype(BF16)

    return kernel_call(
        body,
        (halves, groups, steps),
        [pl.BlockSpec((n, part), lambda h, g, t: (0, h)) for n in left_counts]
        + [pl.BlockSpec((1, n, tile), lambda h, g, t: (g, 0, t)) for n in counts]
        + [pl.BlockSpec(memory_space=pl.ANY)] * len(earlier),
        pl.BlockSpec((fsdp_count, ctx_part * shard, tile), lambda h, g, t: (0, h, g * steps + t)),
        jax.ShapeDtypeStruct((fsdp_count, ctx_count * shard, groups * size), BF16),
        [pltpu.VMEM((part, sum(counts)), BF16)],
        2 * sum(counts) * width * groups * size,
        4 * sum(counts) * (width + groups * size) + 2 * width * groups * size,
    )(*lefts, *rights, *earlier)


def rotated(values, cosine, sine, back=False):
    size = values.shape[1] // 2
    low, high = values[:, :size], values[:, size:]
    if back:
        sine = -sine
    return jnp.concatenate([low * cosine - high * sine, high * cosine + low * sine], 1)


def qkv_kernel(inputs, g_pre, attn, cosine, sine, core):
    rows, width = sum(v.shape[0] for v in inputs), inputs[0].shape[1]
    block = rows // 2
    size = HEAD_DIM

    def body(core_ref, s0, s1, s2, s3, gain, w0, w1, cos, sin, normed_out, q0, q1, kv, x):
        take_slots((s0, s1, s2, s3), x)
        source = x[...].astype(F32)
        normed = (source * inverse_rms(source) * gain[...]).astype(BF16)
        normed_out[...] = normed
        first = core_ref[0] == 0
        own, other = mm(normed, w0[...]), mm(normed, w1[...])
        q0[...] = rotated(own[:, :size], cos[...], sin[...]).astype(BF16)
        q1[...] = rotated(other[:, :size], cos[...], sin[...]).astype(BF16)
        key = jnp.where(first, own[:, size:], other[:, size:])
        kv[:, :size] = rotated(key, cos[...], sin[...]).astype(BF16)
        kv[:, size:] = jnp.where(first, other[:, size:], own[:, size:]).astype(BF16)

    def by_rows(columns):
        return pl.BlockSpec((block, columns), lambda i, c: (i, 0))

    return kernel_call(
        body,
        (2,),
        whole_of(inputs)
        + [
            pl.BlockSpec((1, width), lambda i, c: (0, 0)),
            pl.BlockSpec((width, 2 * size), lambda i, c: (0, 0)),
            pl.BlockSpec((width, 2 * size), lambda i, c: (0, 0)),
            by_rows(size // 2),
            by_rows(size // 2),
        ],
        [by_rows(width), by_rows(size), by_rows(size), by_rows(2 * size)],
        [
            jax.ShapeDtypeStruct((rows, width), BF16),
            jax.ShapeDtypeStruct((rows, size), BF16),
            jax.ShapeDtypeStruct((rows, size), BF16),
            jax.ShapeDtypeStruct((rows, 2 * size), BF16),
        ],
        [pltpu.VMEM((block, width), BF16)],
        8 * rows * width * size,
        8 * width * size + 4 * rows * width,
        prefetch=1,
    )(core, *inputs, g_pre, *attn, cosine, sine)


def scores(query, key, key_place, query_place):
    raw = mm_nt(query, key)
    tanh_part = jnp.tanh(raw * (HEAD_DIM**-0.5 / SOFT_CAP))
    return tanh_part, jnp.where(key_place <= query_place, jnp.exp(SOFT_CAP * tanh_part), 0.0)


def attention_specs(rows, width, block):
    def by_rows(columns):
        return pl.BlockSpec((block, columns), lambda i, c: (i, 0))

    size = HEAD_DIM
    kv = pl.BlockSpec((rows, 2 * size), lambda i, c: (0, 0))
    places = pl.BlockSpec((1, rows), lambda i, c: (0, 0))
    weights = [pl.BlockSpec((width, size), lambda i, c: (0, 2))] * 2
    return by_rows, [by_rows(size), by_rows(size), kv, kv, by_rows(1), places, places] + weights


def put_slots(total, slots):
    rows = slots[0].shape[0]
    for step in range(2):

        @pl.when(pl.program_id(0) == step)
        def _():
            slots[2 * step][...] = total[:rows].astype(BF16)
            slots[2 * step + 1][...] = total[rows:].astype(BF16)


def take_slots(slots, into):
    for step in range(2):
        pl.when(pl.program_id(0) == step)(
            lambda pair=slots[2 * step : 2 * step + 2]: stack_rows(pair, into)
        )


def attention_forward(core, queries, kvs, row_places, key_places, attn):
    rows, width, size = queries[0].shape[0], attn[0].shape[0], HEAD_DIM
    block = rows // 2

    def body(core_ref, q0, q1, kv0, kv1, place, places0, places1, w0, w1, att0, att1, *branch):
        total = 0.0
        for q, att, w in ((q0, att0, w0), (q1, att1, w1)):
            parts = [
                scores(q[...], kv[:, :size], places[...], place[...])[1]
                for kv, places in ((kv0, places0), (kv1, places1))
            ]
            scale = 1.0 / (
                jnp.sum(parts[0], -1, keepdims=True) + jnp.sum(parts[1], -1, keepdims=True)
            )
            attended = mm((parts[0] * scale).astype(BF16), kv0[:, size:])
            attended += mm((parts[1] * scale).astype(BF16), kv1[:, size:])
            attended = attended.astype(BF16)
            att[...] = attended
            total = total + mm_nt(attended, w[...])
        put_slots(total, branch)

    by_rows, specs = attention_specs(rows, width, block)
    slots = [jax.ShapeDtypeStruct((rows // 4, width), BF16)] * 4
    return kernel_call(
        body,
        (2,),
        specs,
        [by_rows(size), by_rows(size)] + whole_of(slots),
        [jax.ShapeDtypeStruct((rows, size), BF16)] * 2 + slots,
        [],
        16 * rows * rows * size + 4 * rows * width * size,
        4 * width * size + 2 * rows * width,
        prefetch=1,
    )(core, *queries, *kvs, row_places, *key_places, *attn)


def attention_backward(
    d_branch, core, queries, kvs, row_places, key_places, attn, cosine, sine
):
    rows, width, size = queries[0].shape[0], attn[0].shape[0], HEAD_DIM
    block = rows // 2
    scaling = size**-0.5

    def body(
        core_ref, q0, q1, kv0, kv1, place, places0, places1, w0, w1, s0, s1, s2, s3, cos, sin,
        dq0, dq1, dkv0, dkv1, sum0, sum1, d_out
    ):
        take_slots((s0, s1, s2, s3), d_out)

        @pl.when(pl.program_id(0) == 0)
        def _():
            sum0[...] = jnp.zeros_like(sum0)
            sum1[...] = jnp.zeros_like(sum1)

        for q, dq, w in ((q0, dq0, w0), (q1, dq1, w1)):
            query = q[...]
            d_att = mm(d_out[...], w[...]).astype(BF16)
            parts = [
                scores(query, kv[:, :size], places[...], place[...])
                for kv, places in ((kv0, places0), (kv1, places1))
            ]
            scale = 1.0 / sum(jnp.sum(e, -1, keepdims=True) for _, e in parts)
            chances = [e * scale for _, e in parts]
            d_chances = [mm_nt(d_att, kv[:, size:]) for kv in (kv0, kv1)]
            inner = sum(
                jnp.sum(p * d, -1, keepdims=True) for p, d in zip(chances, d_chances)
            )
            d_query = 0.0
            for (t, _), p, d, kv, sums in zip(
                parts, chances, d_chances, (kv0, kv1), (sum0, sum1)
            ):
                d_raw = (p * (d - inner) * (1.0 - t * t) * scaling).astype(BF16)
                d_query = d_query + mm(d_raw, kv[:, :size])
                sums[:, :size] += mm_tn(d_raw, query)
                sums[:, size:] += mm_tn(p.astype(BF16), d_att)
            dq[...] = rotated(d_query, cos[...], sin[...], back=True).astype(BF16)

        @pl.when(pl.program_id(0) == pl.num_programs(0) - 1)
        def _():
            dkv0[...] = sum0[...]
            dkv1[...] = sum1[...].astype(BF16)

    by_rows, specs = attention_specs(rows, width, block)
    whole = pl.BlockSpec((rows, 2 * size), lambda i, c: (0, 0))
    return kernel_call(
        body,
        (2,),
        specs + whole_of(d_branch) + [by_rows(size // 2), by_rows(size // 2)],
        [by_rows(size), by_rows(size), whole, whole],
        [
            jax.ShapeDtypeStruct((rows, size), BF16),
            jax.ShapeDtypeStruct((rows, size), BF16),
            jax.ShapeDtypeStruct((rows, 2 * size), F32),
            jax.ShapeDtypeStruct((rows, 2 * size), BF16),
        ],
        [pltpu.VMEM((rows, 2 * size), F32)] * 2 + [pltpu.VMEM((block, width), BF16)],
        40 * rows * rows * size + 4 * rows * width * size,
        4 * width * size + 2 * rows * width,
        prefetch=1,
    )(core, *queries, *kvs, row_places, *key_places, *attn, *d_branch, cosine, sine)


def qkv_backward(inputs, dqs, dkv_mine, dkv_got, attn, cosine, sine, core):
    rows, width = sum(v.shape[0] for v in inputs), inputs[0].shape[1]
    block, size = rows // 2, HEAD_DIM

    def body(core_ref, s0, s1, s2, s3, q0, q1, mine, got, w0, w1, cos, sin, *refs):
        d_in, (dp0, dp1, gain, x) = refs[:4], refs[4:]
        take_slots((s0, s1, s2, s3), x)
        both = mine[...] + got[...].astype(F32)
        d_key = rotated(both[:, :size], cos[...], sin[...], back=True)
        first = core_ref[0] == 0
        dp0[0, :, :size] = q0[...]
        dp1[0, :, :size] = q1[...]
        dp0[0, :, size:] = jnp.where(first, d_key, both[:, size:]).astype(BF16)
        dp1[0, :, size:] = jnp.where(first, both[:, size:], d_key).astype(BF16)
        total = mm_nt(dp0[0], w0[...]) + mm_nt(dp1[0], w1[...])
        put_slots(total, d_in)
        source = x[...].astype(F32)
        term = jnp.sum(total * source * inverse_rms(source), 0, keepdims=True)

        @pl.when(pl.program_id(0) == 0)
        def _():
            gain[...] = jnp.zeros_like(gain)

        gain[...] += term

    def by_rows(columns):
        return pl.BlockSpec((block, columns), lambda i, c: (i, 0))

    weights = [pl.BlockSpec((width, 2 * size), lambda i, c: (0, 0))] * 2
    terms = pl.BlockSpec((1, block, 2 * size), lambda i, c: (0, i, 0))
    return kernel_call(
        body,
        (2,),
        whole_of(inputs)
        + [by_rows(size), by_rows(size), by_rows(2 * size), by_rows(2 * size)]
        + weights
        + [by_rows(size // 2), by_rows(size // 2)],
        whole_of(inputs) + [terms, terms, pl.BlockSpec((1, width), lambda i, c: (0, 0))],
        [jax.ShapeDtypeStruct(v.shape, BF16) for v in inputs]
        + [
            jax.ShapeDtypeStruct((1, rows, 2 * size), BF16),
            jax.ShapeDtypeStruct((1, rows, 2 * size), BF16),
            jax.ShapeDtypeStruct((1, width), F32),
        ],
        [pltpu.VMEM((block, width), BF16)],
        8 * rows * width * size,
        8 * width * size + 4 * rows * width,
        prefetch=1,
    )(core, *inputs, *dqs, dkv_mine, dkv_got, *attn, cosine, sine)


def to_owners(total, ctx_count):
    total = total.reshape(ctx_count, -1, total.shape[1])
    return lax.all_to_all(total, "ctx", split_axis=0, concat_axis=0, tiled=True)


def side_by_side(terms):
    return terms.astype(F32).transpose(1, 0, 2).reshape(terms.shape[1], -1)


def attention_outputs(terms, columns):
    count, rows, _ = terms.shape
    size = HEAD_DIM

    def body(t, grad, gains):
        total = 0.0
        for c in range(count):
            part = t[c].astype(F32)
            kv = count * size + (c % 2) * (count // 2) * size + c // 2 * size
            grad[:, c * size : (c + 1) * size] = part[:, :size]
            grad[:, kv : kv + size] = part[:, size : 2 * size]
            out = columns - (count - c) * size
            grad[:, out : out + size] = part[:, 2 * size : 3 * size]
            total = total + part[:, 3 * size :]
        gains[...] = total

    return pl.pallas_call(
        body,
        out_shape=[
            jax.ShapeDtypeStruct((rows, columns), F32),
            jax.ShapeDtypeStruct((rows, terms.shape[2] - 3 * size), F32),
        ],
        compiler_params=pltpu.CompilerParams(vmem_limit_bytes=VMEM_BYTES),
    )(terms)


def local_kernels(
    layer_input, attn_weights, mlp_in_weights, mlp_out_weights, norm_gains, output_grad
):
    tokens, width = layer_input.shape[1:]
    half_block = tokens // 2
    ctx_count = lax.axis_size("ctx")
    fsdp_count = lax.axis_size("fsdp")
    ranks = ctx_count // 2
    place = lax.axis_index("ctx")
    fsdp_place = lax.axis_index("fsdp")
    rank, core = place // 2, place % 2
    query_cols, key_cols = HEADS * HEAD_DIM, KV_HEADS * HEAD_DIM
    qkv_cols = query_cols + 2 * key_cols
    hidden_width = mlp_out_weights.shape[1]
    f_own = hidden_width // ctx_count
    shard_rows = width // (ctx_count * fsdp_count)

    def partner(values):
        return swap(values, "ctx", 1, ctx_count)

    def columns(array, start, size):
        return lax.dynamic_slice_in_dim(array, start, size, 1)

    chip_groups = [
        [(2 * r + c) * fsdp_count + f for c in (0, 1) for f in range(fsdp_count)]
        for r in range(ranks)
    ]

    def chip_gather(piece):
        whole = lax.all_gather(
            piece, ("ctx", "fsdp"), axis=0, tiled=True, axis_index_groups=chip_groups
        )
        return whole.reshape(2, width, piece.shape[1])

    def over_sequences(product):
        product = product.reshape(width, product.shape[2])
        return lax.psum_scatter(product, "fsdp", scatter_dimension=0, tiled=True)

    own_input = layer_input.reshape(tokens, width)
    source = own_input.astype(F32)
    upstream = output_grad.reshape(tokens, width).astype(F32)
    kv_start = query_cols + core * key_cols + rank * HEAD_DIM
    piece = [
        columns(attn_weights, place * HEAD_DIM, HEAD_DIM),
        columns(attn_weights, kv_start, HEAD_DIM),
        columns(attn_weights, qkv_cols + place * HEAD_DIM, HEAD_DIM),
    ]
    piece, place_in = together(jnp.concatenate(piece, 1), place)
    own_gains = norm_gains.T
    if fsdp_count == 4:
        ways = [swap(own_input, "ctx", 4, ctx_count), swap(own_input, "ctx", 2, ctx_count)]

        def onward(got):
            return swap(got[0], "ctx", 2, ctx_count), [swap(own_gains, "fsdp", k, 4) for k in (1, 2, 3)]

        attn_own, (slot_2, slot_1), (slot_3, gains_got) = square_gather(
            piece, fsdp_place, (ways, onward)
        )
        gains = jnp.zeros((4, width), BF16)
        for k, block in enumerate([own_gains, *gains_got]):
            start = (fsdp_place ^ k) * own_gains.shape[1]
            gains = lax.dynamic_update_slice_in_dim(gains, block, start, 1)
        gains = gains.astype(F32)
        inputs = [own_input, slot_1, slot_2, slot_3]
    else:
        attn_own = lax.all_gather(piece, "fsdp", axis=0, tiled=True)
        inputs = line_gather(own_input, ranks)
        gains = lax.all_gather(own_gains, "fsdp", axis=1, tiled=True).astype(F32)
    attn = (attn_own, partner(attn_own))
    g_pre, g_post, g_mid, g_out = [gains[i] for i in range(4)]
    in_all = chip_gather(
        jnp.concatenate(
            [
                columns(mlp_in_weights, place_in * f_own, f_own),
                columns(mlp_in_weights, hidden_width + place_in * f_own, f_own),
            ],
            1,
        )
    )
    out_all = chip_gather(columns(mlp_out_weights, place_in * f_own, f_own))

    def places_of(which):
        owners = (2 * (rank ^ jnp.arange(ranks, dtype=jnp.int32)) + which)[:, None] * tokens
        gathered_rows = owners + jnp.arange(tokens, dtype=jnp.int32)[None, :]
        return positions_of(gathered_rows.reshape(-1), half_block, ctx_count)

    own_places, other_places = places_of(core), places_of(1 - core)
    cosine, sine = rotary_tables(own_places, HEAD_DIM)
    cosine, sine = cosine[:, : HEAD_DIM // 2], sine[:, : HEAD_DIM // 2]
    row_places, key_places = own_places[:, None], (own_places[None, :], other_places[None, :])
    core_word = core.reshape(1).astype(jnp.int32)

    normed_in, *queries, kv_own = qkv_kernel(
        inputs, gains[:1], attn, cosine, sine, core_word
    )
    attention = (core_word, queries, (kv_own, partner(kv_own)), row_places, key_places, attn)
    att_own, att_other, *branch_parts = attention_forward(*attention)

    def own_rows(halves, beside=()):
        parts = [halves[k % 2][k // 2] for k in range(4)]
        terms, _, beside = four_scatter(parts, ctx_count, (), lambda first: beside)
        return sum_of(terms), beside

    def gathered_halves(values, work):
        slots = four_gather(values, ctx_count)
        done = work([slots[0], slots[2]], 0)
        slots[3], done = together(slots[3], done)
        return [slots[0], slots[2], slots[1], slots[3]], (done, work([slots[1], slots[3]], 1))

    branch = sum_of(four_scatter(branch_parts, ctx_count)[0])
    scale_branch = inverse_rms(branch)
    residual = source + branch * scale_branch * g_post
    scale_mid = inverse_rms(residual)
    mids, forward = gathered_halves(
        (residual * scale_mid * g_mid).astype(BF16), lambda v, _: gate_up_forward(v, in_all, core_word)
    )
    mixed_1 = down_forward(forward[1][:2], out_all, core_word)
    mixed_0 = down_forward(forward[0][:2], out_all, core_word, mixed_1)
    hidden_own = [f[0] for f in forward]
    hidden_got = [partner(f[1]) for f in forward]
    mid_got = [partner(v) for v in mids]
    mixed = own_rows((mixed_0, mixed_1))[0]
    mixed, hidden_own, hidden_got, mid_got = together(mixed, hidden_own, hidden_got, mid_got)
    scale_mixed = inverse_rms(mixed)
    block_out = (residual + mixed * scale_mixed * g_out).astype(BF16)
    grad_out_gain = jnp.sum(upstream * mixed * scale_mixed, 0)
    d_mixeds, d_gate_ups = gathered_halves(
        norm_backward(mixed, scale_mixed, upstream * g_out).astype(BF16),
        lambda v, k: down_backward(v, *forward[k][2:], out_all, core_word),
    )

    def weight_grad(lefts, rights, *earlier):
        return weight_grad_kernel(lefts, rights, ctx_count, fsdp_count, earlier)

    down_product = weight_grad(
        [*d_mixeds, *[partner(v) for v in d_mixeds]], hidden_own + hidden_got
    )
    d_gate_ups, down_product = together(d_gate_ups, down_product)
    down_total = over_sequences(down_product)
    d_mid_1 = gate_up_backward(d_gate_ups[1], in_all, core_word)
    d_mid_0 = gate_up_backward(d_gate_ups[0], in_all, core_word, d_mid_1)
    gate_up_product = weight_grad(
        [*mids, *mid_got],
        [v[0] for v in d_gate_ups] + [partner(v[1]) for v in d_gate_ups],
        *d_mid_0,
    )
    d_mid, (gate_up_product,) = own_rows((d_mid_0, d_mid_1), (gate_up_product,))
    gate_up_total = over_sequences(gate_up_product)
    grad_mid_gain = jnp.sum(d_mid * residual * scale_mid, 0)
    d_residual = upstream + norm_backward(residual, scale_mid, d_mid * g_mid)
    grad_post_gain = jnp.sum(d_residual * branch * scale_branch, 0)
    d_branches = four_gather(
        norm_backward(branch, scale_branch, d_residual * g_post).astype(BF16), ctx_count
    )

    d_branches, down_total = together(d_branches, down_total)
    down = to_owners(down_total, ctx_count)
    *d_queries, dkv_own, dkv_other = attention_backward(d_branches, *attention, cosine, sine)
    *d_in, dproj_own, dproj_other, grad_pre_gain = qkv_backward(
        inputs, d_queries, dkv_own, partner(dkv_other), attn, cosine, sine, core_word
    )

    gain_terms = jnp.stack([grad_pre_gain[0], grad_post_gain, grad_mid_gain, grad_out_gain], 1)
    gain_terms = gain_terms.reshape(ctx_count, fsdp_count, shard_rows, 4)
    gain_terms = gain_terms.transpose(1, 0, 2, 3).reshape(fsdp_count, -1, 4)
    out_product = weight_grad(
        [*d_branches, *[partner(v) for v in d_branches]], [att_own[None], partner(att_other)[None]]
    )
    product = weight_grad([normed_in, partner(normed_in)], [dproj_own, partner(dproj_other)])
    product = jnp.concatenate([product, out_product, gain_terms.astype(BF16)], 2)

    def part(product, k):
        return lax.dynamic_index_in_dim(product, fsdp_place ^ k, 0, keepdims=False)

    def corners_of(first):
        return gate_up_total, corner_scatter(part(first[1], 3), 4) if fsdp_count == 4 else ()

    d_in, (down, product), (gate_up_total, corners) = four_scatter(
        d_in, ctx_count, (down, product), corners_of
    )
    gate_up_terms = to_owners(gate_up_total, ctx_count)
    if fsdp_count == 4:
        parts = [part(product, k).astype(F32) for k in range(4)]
        attn_total = rows_scatter(parts, corners, 4).astype(BF16)
    else:
        attn_total = over_sequences(product)
    gate_up_terms, attn_total = together(gate_up_terms, attn_total)
    attn_terms = to_owners(attn_total, ctx_count)
    d_in = sum_of(d_in)
    d_source = d_residual + norm_backward(source, inverse_rms(source), d_in * g_pre)

    grad_mlp_out = side_by_side(down)
    grad_mlp_in = jnp.concatenate(
        [side_by_side(gate_up_terms[:, :, :f_own]), side_by_side(gate_up_terms[:, :, f_own:])], 1
    )
    grad_attn, grad_gains = attention_outputs(attn_terms, attn_weights.shape[1])
    return (
        block_out.reshape(layer_input.shape),
        d_source.reshape(layer_input.shape),
        grad_attn,
        grad_mlp_in,
        grad_mlp_out,
        grad_gains,
    )


def local(layer_input, attn_weights, mlp_in_weights, mlp_out_weights, norm_gains, output_grad):
    ctx_count, fsdp_count = lax.axis_size("ctx"), lax.axis_size("fsdp")
    width, hidden_width = layer_input.shape[2], mlp_out_weights.shape[1]
    fits = (
        ctx_count == HEADS == 2 * KV_HEADS == 8
        and hidden_width % (128 * ctx_count) == 0
        and width % 256 == 0
        and width % (8 * ctx_count * fsdp_count) == 0
        and (width // fsdp_count) % 32 == 0
    )
    path = local_kernels if fits else local_general
    return path(
        layer_input, attn_weights, mlp_in_weights, mlp_out_weights, norm_gains, output_grad
    )


def local_general(layer_input, attn_weights, mlp_in_weights, mlp_out_weights, norm_gains, output_grad):
    tokens, width = layer_input.shape[1:]
    half_block = tokens // 2
    ctx_count = lax.axis_size("ctx")
    fsdp_count = lax.axis_size("fsdp")
    ranks = ctx_count // 2
    place = lax.axis_index("ctx")
    rank, core = place // 2, place % 2
    first_core = core == 0
    query_cols, key_cols = HEADS * HEAD_DIM, KV_HEADS * HEAD_DIM
    qkv_cols = query_cols + 2 * key_cols
    heads = HEADS // ranks
    sharing = ranks // KV_HEADS
    hidden_width = mlp_out_weights.shape[1]
    q_own = query_cols // ctx_count
    f_own = hidden_width // ctx_count
    shard_rows = width // (ctx_count * fsdp_count)
    scaling = HEAD_DIM**-0.5

    def partner(values):
        return swap(values, "ctx", 1, ctx_count)

    def columns(array, start, size):
        return lax.dynamic_slice_in_dim(array, start, size, 1)


    kv_start = query_cols + core * key_cols + rank // sharing * HEAD_DIM
    attn_piece = (
        columns(attn_weights, place * q_own, q_own),
        columns(attn_weights, kv_start, HEAD_DIM),
        columns(attn_weights, qkv_cols + place * q_own, q_own),
    )
    attn_own = lax.all_gather(jnp.concatenate(attn_piece, 1), "fsdp", axis=0, tiled=True)
    in_piece = (
        columns(mlp_in_weights, place * f_own, f_own),
        columns(mlp_in_weights, hidden_width + place * f_own, f_own),
    )
    in_piece = jnp.concatenate(in_piece, 1)
    out_piece = columns(mlp_out_weights, place * f_own, f_own)
    in_own = lax.all_gather(in_piece, "fsdp", axis=0, tiled=True)
    out_own = lax.all_gather(out_piece, "fsdp", axis=0, tiled=True)
    gains = lax.all_gather(norm_gains, "fsdp", axis=0, tiled=True).astype(F32)
    g_pre, g_post, g_mid, g_out = [gains[:, i] for i in range(4)]
    attn_other = partner(attn_own)
    qkv_own, proj_own = attn_own[:, : q_own + HEAD_DIM], attn_own[:, q_own + HEAD_DIM :]
    qkv_other, proj_other = attn_other[:, : q_own + HEAD_DIM], attn_other[:, q_own + HEAD_DIM :]

    own_input = layer_input.reshape(tokens, width)
    source = own_input.astype(F32)
    upstream = output_grad.reshape(tokens, width).astype(F32)
    inputs = jnp.concatenate(line_gather(own_input, ranks), 0).astype(F32)
    scale_in = inverse_rms(inputs)
    plain_in = inputs * scale_in
    normed_in = (plain_in * g_pre).astype(BF16)

    def places_of(which):
        slots = rank ^ jnp.arange(ranks, dtype=jnp.int32)
        owners = (2 * slots + which)[:, None] * tokens
        rows = owners + jnp.arange(tokens, dtype=jnp.int32)[None, :]
        return positions_of(rows.reshape(-1), half_block, ctx_count)

    own_places, other_places = places_of(core), places_of(1 - core)
    cosine, sine_table = rotary_tables(own_places, HEAD_DIM)
    all_places = jnp.concatenate([own_places, other_places], 0)
    allowed = all_places[None, :] <= own_places[:, None]
    rows = ranks * tokens

    def ordered(mine, theirs):
        return jnp.where(first_core, mine, theirs), jnp.where(first_core, theirs, mine)

    proj_a, proj_b = dot(normed_in, qkv_own), dot(normed_in, qkv_other)
    query_raw = jnp.concatenate(ordered(proj_a[:, :q_own], proj_b[:, :q_own]), 1)
    key_raw, value_raw = ordered(proj_a[:, q_own:], proj_b[:, q_own:])
    query = rotate(
        query_raw.reshape(rows, heads, HEAD_DIM), cosine[:, None], sine_table[:, None]
    ).astype(BF16)
    key_own = rotate(key_raw, cosine, sine_table).astype(BF16)
    value_own = value_raw.astype(BF16)
    key_value = jnp.concatenate([key_own, value_own], 1)
    key_value = jnp.concatenate([key_value, partner(key_value)], 0)
    keys, values = key_value[:, :HEAD_DIM], key_value[:, HEAD_DIM:]

    def score_rows():
        raw_scores = jnp.einsum("tgd,ld->gtl", query, keys, preferred_element_type=F32)
        tanh_part = jnp.tanh(raw_scores * scaling / SOFT_CAP)
        return tanh_part, jnp.where(allowed, SOFT_CAP * tanh_part, MASKED_SCORE)

    tanh_part, capped = score_rows()
    row_max = jnp.max(capped, -1, keepdims=True)
    weights = jnp.exp(capped - row_max)
    row_total = jnp.sum(weights, -1, keepdims=True)
    log_total = row_max + jnp.log(row_total)
    chances = (weights / row_total).astype(BF16)
    attended = jnp.einsum("gtl,ld->tgd", chances, values, preferred_element_type=F32)
    attended = attended.reshape(rows, heads * HEAD_DIM).astype(BF16)
    att_own, att_other = ordered(attended[:, :q_own], attended[:, q_own:])
    branch_parts = (dot_t(att_own, proj_own) + dot_t(att_other, proj_other)).reshape(
        ranks, tokens, width
    )

    span = tokens // STREAMS
    cuts = [slice(s * span, (s + 1) * span) for s in range(STREAMS)]

    def own_rows(parts):
        return line_scatter(list(parts.reshape(ranks, -1, width)), ranks)

    def all_rows(values):
        return jnp.concatenate(line_gather(values, ranks), 0)

    branch = [own_rows(branch_parts[:, cut]) for cut in cuts]
    halves = ((in_own, out_own), (partner(in_own), partner(out_own)))
    scale_branch = [inverse_rms(v) for v in branch]
    residual = [source[cut] + v * w * g_post for cut, v, w in zip(cuts, branch, scale_branch)]
    scale_mid = [inverse_rms(v) for v in residual]
    mids = [all_rows((v * w * g_mid).astype(BF16)) for v, w in zip(residual, scale_mid)]
    hiddens, backs, mixed = [], [], []
    for values_in in mids:
        hidden_of, back_of, total = [], [], 0.0
        for w_in, w_out in halves:
            gate_up = dot(values_in, w_in)
            hidden, back = jax.vjp(geglu, gate_up[:, :f_own], gate_up[:, f_own:])
            hidden_of.append(hidden.astype(BF16))
            back_of.append(back)
            total = total + dot_t(hidden_of[-1], w_out)
        hiddens.append(hidden_of)
        backs.append(back_of)
        mixed.append(own_rows(total))
    scale_mixed = [inverse_rms(v) for v in mixed]
    block_out = [
        (r + v * w * g_out).astype(BF16) for r, v, w in zip(residual, mixed, scale_mixed)
    ]
    ups = [upstream[cut] for cut in cuts]
    grad_out_gain = sum(jnp.sum(u * v * w, 0) for u, v, w in zip(ups, mixed, scale_mixed))
    d_mixeds = [
        all_rows(norm_backward(v, w, u * g_out).astype(BF16))
        for u, v, w in zip(ups, mixed, scale_mixed)
    ]

    def both_cores(mine, others=None):
        return jnp.concatenate([mine, partner(mine if others is None else others)], 0)

    def joined(pieces):
        return jnp.concatenate(pieces, 0)

    def grouped(left):
        left = left.reshape(left.shape[0], ctx_count, fsdp_count, shard_rows)
        return left.transpose(0, 2, 1, 3).reshape(left.shape[0], fsdp_count, ctx_count * shard_rows)

    def weight_grad(left, right):
        product = jnp.einsum("tfr,tn->frn", grouped(left), right, preferred_element_type=F32)
        return product.reshape(width, right.shape[1]).astype(BF16)

    def over_sequences(product):
        total = lax.psum_scatter(product, "fsdp", scatter_dimension=0, tiled=True)
        return total.reshape(ranks, 2, shard_rows, product.shape[1])

    def spread(total):
        mine = jnp.where(first_core, total[:, 0], total[:, 1])
        theirs = partner(jnp.where(first_core, total[:, 1], total[:, 0]))
        both = jnp.stack(ordered(mine, theirs), 1)
        got = []
        for k in range(ranks):
            part = lax.dynamic_index_in_dim(both, rank ^ k, 0, keepdims=False)
            got.append(part if k == 0 else swap(part, "ctx", 2 * k, ctx_count))
        return got

    def put(into, piece, start, adds=False):
        piece = piece.astype(F32)
        if adds:
            piece = piece + lax.dynamic_slice_in_dim(into, start, piece.shape[1], 1)
        return lax.dynamic_update_slice_in_dim(into, piece, start, 1)

    mid_rows = both_cores(joined(mids))
    hidden_rows = both_cores(joined([h[0] for h in hiddens]), joined([h[1] for h in hiddens]))
    down_product = weight_grad(both_cores(joined(d_mixeds)), hidden_rows)
    d_mid, d_gate_ups = [], []
    for values_in, back_of in zip(d_mixeds, backs):
        total, d_gate_up_of = 0.0, []
        for (w_in, w_out), back in zip(halves, back_of):
            d_gate_up = jnp.concatenate(back(dot(values_in, w_out)), 1).astype(BF16)
            d_gate_up_of.append(d_gate_up)
            total = total + dot_t(d_gate_up, w_in)
        d_gate_ups.append(d_gate_up_of)
        d_mid.append(own_rows(total))
    down_total = over_sequences(down_product)
    dgu_rows = both_cores(joined([d[0] for d in d_gate_ups]), joined([d[1] for d in d_gate_ups]))
    gate_up_product = weight_grad(mid_rows, dgu_rows)
    gate_up_total = over_sequences(gate_up_product)

    grad_mid_gain = sum(jnp.sum(d * v * w, 0) for d, v, w in zip(d_mid, residual, scale_mid))
    d_residual = [
        u + norm_backward(v, w, d * g_mid) for u, v, w, d in zip(ups, residual, scale_mid, d_mid)
    ]
    grad_post_gain = sum(
        jnp.sum(d * v * w, 0) for d, v, w in zip(d_residual, branch, scale_branch)
    )
    d_branches = [
        line_gather(norm_backward(v, w, d * g_post).astype(BF16), ranks)
        for d, v, w in zip(d_residual, branch, scale_branch)
    ]
    d_branches = joined([d[k] for k in range(ranks) for d in d_branches])
    d_residual = joined(d_residual)

    down = spread(down_total)
    d_att_own, d_att_other = dot(d_branches, proj_own), dot(d_branches, proj_other)
    d_attended = jnp.concatenate(ordered(d_att_own, d_att_other), 1).astype(BF16)
    d_attended = d_attended.reshape(rows, heads, HEAD_DIM)
    tanh_again, capped_again = score_rows()
    chances_f = jnp.exp(capped_again - log_total)
    d_values = jnp.einsum(
        "gtl,tgd->ld", chances_f.astype(BF16), d_attended, preferred_element_type=F32
    )
    d_chances = jnp.einsum("tgd,ld->gtl", d_attended, values, preferred_element_type=F32)
    row_inner = jnp.sum(chances_f * d_chances, -1, keepdims=True)
    d_raw = (
        chances_f * (d_chances - row_inner) * (1.0 - tanh_again * tanh_again) * scaling
    ).astype(BF16)
    d_query = jnp.einsum("gtl,ld->tgd", d_raw, keys, preferred_element_type=F32)
    d_keys = jnp.einsum("gtl,tgd->ld", d_raw, query, preferred_element_type=F32)
    d_key_value = jnp.concatenate([d_keys, d_values], 1)
    d_key_value = d_key_value[:rows] + partner(d_key_value[rows:].astype(BF16)).astype(F32)
    d_query_raw = rotate_back(d_query, cosine[:, None], sine_table[:, None]).reshape(
        rows, heads * HEAD_DIM
    )
    d_key_raw = rotate_back(d_key_value[:, :HEAD_DIM], cosine, sine_table)
    dq_own, dq_other = ordered(d_query_raw[:, :q_own], d_query_raw[:, q_own:])
    dkv_own, dkv_other = ordered(d_key_raw, d_key_value[:, HEAD_DIM:])
    dproj_own = jnp.concatenate([dq_own, dkv_own], 1).astype(BF16)
    dproj_other = jnp.concatenate([dq_other, dkv_other], 1).astype(BF16)
    d_in = dot_t(dproj_own, qkv_own) + dot_t(dproj_other, qkv_other)
    grad_pre_gain = jnp.sum(d_in * plain_in, 0)
    d_in = own_rows(d_in)
    d_source = d_residual + norm_backward(source, scale_in[:tokens], d_in * g_pre)

    gate_up_terms = spread(gate_up_total)
    gain_terms = jnp.stack([grad_pre_gain, grad_post_gain, grad_mid_gain, grad_out_gain], 1)
    gain_terms = gain_terms.reshape(ctx_count, fsdp_count, shard_rows, 4)
    gain_terms = gain_terms.transpose(1, 0, 2, 3).reshape(fsdp_count, -1, 4)
    lefts = (grouped(both_cores(normed_in)), grouped(both_cores(d_branches)))
    rights = (both_cores(dproj_own, dproj_other), both_cores(att_own, att_other))

    def attn_part(index):
        at = [lax.dynamic_index_in_dim(v, index, 1, keepdims=False) for v in lefts]
        gain_rows = lax.dynamic_index_in_dim(gain_terms, index, 0, keepdims=False)
        pieces = [
            jnp.einsum("tr,tn->rn", v, right, preferred_element_type=F32)
            for v, right in zip(at, rights)
        ]
        return jnp.concatenate(pieces + [gain_rows], 1)

    attn_total = over_sequences(joined([attn_part(i).astype(BF16) for i in range(fsdp_count)]))
    attn_terms = spread(attn_total)

    grad_mlp_out = jnp.zeros((shard_rows, hidden_width), F32)
    grad_mlp_in = jnp.zeros((shard_rows, 2 * hidden_width), F32)
    grad_attn = jnp.zeros((shard_rows, attn_weights.shape[1]), F32)
    grad_gains = jnp.zeros((shard_rows, 4), F32)
    kv_end, out_end = q_own + HEAD_DIM, 2 * q_own + HEAD_DIM
    for k in range(ranks):
        giver = rank ^ k
        for which in (0, 1):
            start = (2 * giver + which) * f_own
            grad_mlp_out = put(grad_mlp_out, down[k][which], start)
            term = gate_up_terms[k][which]
            grad_mlp_in = put(grad_mlp_in, term[:, :f_own], start)
            grad_mlp_in = put(grad_mlp_in, term[:, f_own:], hidden_width + start)
            term = attn_terms[k][which]
            start = (2 * giver + which) * q_own
            grad_attn = put(grad_attn, term[:, :q_own], start)
            grad_attn = put(grad_attn, term[:, kv_end:out_end], qkv_cols + start)
            start = query_cols + which * key_cols + giver // sharing * HEAD_DIM
            grad_attn = put(grad_attn, term[:, q_own:kv_end], start, sharing > 1)
            grad_gains = grad_gains + term[:, out_end:].astype(F32)
    return (
        joined(block_out).reshape(layer_input.shape),
        d_source.reshape(layer_input.shape),
        grad_attn,
        grad_mlp_in,
        grad_mlp_out,
        grad_gains,
    )


def solution(mesh):
    in_specs = (
        P("fsdp", "ctx", None),
        P("fsdp", None),
        P("fsdp", None),
        P("fsdp", None),
        P("fsdp", None),
        P("fsdp", "ctx", None),
    )
    out_specs = (
        P("fsdp", "ctx", None),
        P("fsdp", "ctx", None),
        P(("ctx", "fsdp"), None),
        P(("ctx", "fsdp"), None),
        P(("ctx", "fsdp"), None),
        P(("ctx", "fsdp"), None),
    )
    return jax.shard_map(local, mesh=mesh, in_specs=in_specs, out_specs=out_specs, check_vma=False)
```

```python
import jax
import jax.numpy as jnp
from jax import lax
from jax.experimental import pallas as pl
from jax.experimental.pallas import tpu as pltpu
from jax.sharding import PartitionSpec as P

HEADS = 8
KV_HEADS = 4
HEAD_DIM = 256

EPSILON = 1e-06
SOFT_CAP = 50.0
ROTARY_BASE = 10000.0
MASKED_SCORE = -1e30
STREAMS = 1

F32 = jnp.float32
BF16 = jnp.bfloat16


def positions_of(rows, half_block, ctx_count):
    owners = rows // (2 * half_block)
    within = rows % (2 * half_block)
    return jnp.where(
        within < half_block,
        owners * half_block + within,
        (2 * ctx_count - 1 - owners) * half_block + within - half_block,
    )


def rotary_tables(places, head_dim):
    half_width = head_dim // 2
    frequency = ROTARY_BASE ** (-jnp.arange(half_width, dtype=F32) * 2.0 / head_dim)
    angles = places.astype(F32)[:, None] * frequency[None, :]
    cosine = jnp.concatenate([jnp.cos(angles), jnp.cos(angles)], -1)
    sine_table = jnp.concatenate([jnp.sin(angles), jnp.sin(angles)], -1)
    return (cosine, sine_table)


def turned(values):
    half_width = values.shape[-1] // 2
    return jnp.concatenate([-values[..., half_width:], values[..., :half_width]], -1)


def rotate(values, cosine, sine_table):
    return values * cosine + turned(values) * sine_table


def rotate_back(grads, cosine, sine_table):
    return grads * cosine - turned(grads * sine_table)


def inverse_rms(values):
    return lax.rsqrt(jnp.mean(values * values, -1, keepdims=True) + EPSILON)


def norm_backward(values, scale, grad_normed):
    normed = values * scale
    return scale * (grad_normed - normed * jnp.mean(grad_normed * normed, -1, keepdims=True))


def geglu(gate, upper):
    return jax.nn.gelu(gate, approximate=True) * upper


def dot(a, b):
    return jnp.dot(a, b, preferred_element_type=F32)


def dot_t(a, b):
    return jnp.einsum("tk,dk->td", a, b, preferred_element_type=F32)


def swap(values, axis, distance, count):
    return lax.ppermute(values, axis, [(i, i ^ distance) for i in range(count)])


def line_gather(values, ranks):
    slots = {0: values}
    bit = ranks // 2
    while bit:
        slots.update({k ^ bit: swap(v, "ctx", 2 * bit, 2 * ranks) for k, v in slots.items()})
        bit //= 2
    return [slots[k] for k in range(ranks)]


def line_scatter(parts, ranks):
    sums = {k: v.astype(F32) for k, v in enumerate(parts)}
    bit = 1
    while bit < ranks:
        for k in sorted(sums, reverse=True):
            if k & bit:
                got = swap(sums.pop(k).astype(BF16), "ctx", 2 * bit, 2 * ranks)
                sums[k ^ bit] = sums[k ^ bit] + got.astype(F32)
        bit *= 2
    return sums[0]


def four_gather(values, ctx_count):
    far, near = swap(values, "ctx", 4, ctx_count), swap(values, "ctx", 2, ctx_count)
    far, near = together(far, near)
    return [values, near, far, swap(far, "ctx", 2, ctx_count)]


def four_scatter(parts, ctx_count, with_first=(), with_far=lambda first: ()):
    by_near = swap(parts[3].astype(BF16), "ctx", 2, ctx_count)
    near, far, by_near, with_first = together(parts[1], parts[2], by_near, with_first)
    far = (far.astype(F32) + by_near.astype(F32)).astype(BF16)
    far = swap(far, "ctx", 4, ctx_count)
    near = swap(near.astype(BF16), "ctx", 2, ctx_count)
    near, far, with_far = together(near, far, with_far(with_first))
    return (parts[0], near, far), with_first, with_far


def sum_of(terms):
    return sum(v.astype(F32) for v in terms)


def square_gather(piece, place, beside):
    rows = piece.shape[0]
    half = rows // 2
    near, far = swap(piece, "fsdp", 1, 4), swap(piece, "fsdp", 2, 4)
    first, then = beside
    near, far, first = together(near, far, first)
    corner_a, corner_b = swap(near[:half], "fsdp", 2, 4), swap(far[half:], "fsdp", 1, 4)
    corner_a, corner_b, second = together(corner_a, corner_b, then(first))
    whole = jnp.zeros((4 * rows, piece.shape[1]), piece.dtype)
    for block, at in (
        (piece, place * rows),
        (near, (place ^ 1) * rows),
        (far, (place ^ 2) * rows),
        (corner_a, (place ^ 3) * rows),
        (corner_b, (place ^ 3) * rows + half),
    ):
        whole = lax.dynamic_update_slice_in_dim(whole, block, at, 0)
    return whole, first, second


def corner_scatter(corner, count):
    half = corner.shape[0] // 2
    corner = corner.astype(BF16)
    return swap(corner[:half], "fsdp", 1, count), swap(corner[half:], "fsdp", 2, count)


def rows_scatter(parts, corners, count):
    half = parts[3].shape[0] // 2
    by_near, by_far = corners[0].astype(F32), corners[1].astype(F32)
    near = jnp.concatenate([parts[1][:half], parts[1][half:] + by_far], 0).astype(BF16)
    far = jnp.concatenate([parts[2][:half] + by_near, parts[2][half:]], 0).astype(BF16)
    near, far = swap(near, "fsdp", 1, count), swap(far, "fsdp", 2, count)
    return parts[0] + near.astype(F32) + far.astype(F32)


def together(*values):
    return lax.optimization_barrier(values)


VMEM_BYTES = 60 * 1024 * 1024


def kernel_call(body, grid, in_specs, out_specs, out_shape, scratch, flops, moved, prefetch=0):
    return pl.pallas_call(
        body,
        grid_spec=pltpu.PrefetchScalarGridSpec(
            num_scalar_prefetch=prefetch,
            grid=grid,
            in_specs=in_specs,
            out_specs=out_specs,
            scratch_shapes=scratch,
        ),
        out_shape=out_shape,
        compiler_params=pltpu.CompilerParams(
            vmem_limit_bytes=VMEM_BYTES, dimension_semantics=("arbitrary",) * len(grid)
        ),
        cost_estimate=pl.CostEstimate(flops=flops, bytes_accessed=moved, transcendentals=0),
    )


def mm(a, b):
    return jnp.dot(a, b, preferred_element_type=F32)


def mm_nt(a, b):
    return lax.dot_general(a, b, (((1,), (1,)), ((), ())), preferred_element_type=F32)


def mm_tn(a, b):
    return lax.dot_general(a, b, (((0,), (0,)), ((), ())), preferred_element_type=F32)


def tile_of(size, most):
    return max(t for t in range(128, most + 1, 128) if size % t == 0)


def gelu_parts(gate):
    rate = 0.7978845608028654
    square = gate * gate
    t = jnp.tanh(rate * gate * (1.0 + 0.044715 * square))
    half = 0.5 * (1.0 + t)
    slope = half + 0.5 * gate * (1.0 - t * t) * rate * (1.0 + 3.0 * 0.044715 * square)
    return gate * half, slope


def stack_rows(pieces, into):
    at = 0
    for ref in pieces:
        into[at : at + ref.shape[0]] = ref[...]
        at += ref.shape[0]


def whole_of(values):
    return [pl.BlockSpec(v.shape, lambda *_, n=len(v.shape): (0,) * n) for v in values]


def core_blocks(shape, steps):
    lead = (0,) * (len(shape) - 1)
    return [
        pl.BlockSpec(shape, lambda h, i, c: (*lead, jnp.where(h == 0, i, steps - 1))),
        pl.BlockSpec(shape, lambda h, i, c: (*lead, jnp.where(h == 0, 0, i))),
    ]


def gate_up_forward(values, w_in, core, most=384):
    rows, width = sum(v.shape[0] for v in values), values[0].shape[1]
    size = w_in.shape[2] // 2
    tile = tile_of(size, most)
    steps = size // tile

    def body(core_ref, *refs):
        g, u, hidden0, hidden1, gate_all, up_all, x = refs[len(values) :]

        @pl.when((pl.program_id(0) == 0) & (pl.program_id(1) == 0))
        def _():
            stack_rows(refs[: len(values)], x)

        gate, up = mm(x[...], g[0]), mm(x[...], u[0])
        gate_all[0] = gate
        up_all[0] = up
        hidden = (gelu_parts(gate)[0] * up).astype(BF16)

        @pl.when(pl.program_id(0) == 0)
        def _():
            hidden0[0] = hidden

        @pl.when(pl.program_id(0) == 1)
        def _():
            hidden1[0] = hidden

    saved = pl.BlockSpec((1, rows, tile), lambda h, i, c: (h, 0, i))
    return kernel_call(
        body,
        (2, steps),
        whole_of(values)
        + [
            pl.BlockSpec((1, width, tile), lambda h, i, c: (c[0] ^ h, 0, i)),
            pl.BlockSpec((1, width, tile), lambda h, i, c: (c[0] ^ h, 0, steps + i)),
        ],
        core_blocks((1, rows, tile), steps) + [saved, saved],
        [jax.ShapeDtypeStruct((1, rows, size), BF16)] * 2
        + [jax.ShapeDtypeStruct((2, rows, size), F32)] * 2,
        [pltpu.VMEM((rows, width), BF16)],
        8 * rows * width * size,
        8 * width * size + 20 * rows * size,
        prefetch=1,
    )(core, *values, w_in, w_in)


def down_forward(hidden, w_out, core, earlier=(), most=768):
    _, rows, size = hidden[0].shape
    width = w_out.shape[1]
    tile = tile_of(width, most)

    def body(core_ref, h0, h1, o0, o1, *refs):
        total = (mm_nt(h0[0], o0[0]) + mm_nt(h1[0], o1[0])).astype(BF16)
        refs[-2][...] = total[: rows // 2]
        refs[-1][...] = total[rows // 2 :]

    whole = pl.BlockSpec((1, rows, size), lambda i, c: (0, 0, 0))
    return kernel_call(
        body,
        (width // tile,),
        [
            whole,
            whole,
            pl.BlockSpec((1, tile, size), lambda i, c: (c[0], i, 0)),
            pl.BlockSpec((1, tile, size), lambda i, c: (1 - c[0], i, 0)),
        ]
        + [pl.BlockSpec(memory_space=pl.ANY)] * len(earlier),
        [pl.BlockSpec((rows // 2, tile), lambda i, c: (0, i))] * 2,
        [jax.ShapeDtypeStruct((rows // 2, width), BF16)] * 2,
        [],
        4 * rows * width * size,
        4 * width * size + 4 * rows * size,
        prefetch=1,
    )(core, *hidden, w_out, w_out, *earlier)


def down_backward(d_mixed, gate_all, up_all, w_out, core, most=1152):
    rows, width = sum(v.shape[0] for v in d_mixed), d_mixed[0].shape[1]
    size = w_out.shape[2]
    tile = tile_of(size, most)
    steps = size // tile

    def body(core_ref, *refs):
        gate, up, o, dgu0, dgu1, x = refs[len(d_mixed) :]

        @pl.when((pl.program_id(0) == 0) & (pl.program_id(1) == 0))
        def _():
            stack_rows(refs[: len(d_mixed)], x)

        d_hidden = mm(x[...], o[0])
        value, slope = gelu_parts(gate[0])
        d_gate = (d_hidden * up[0] * slope).astype(BF16)
        d_up = (d_hidden * value).astype(BF16)

        @pl.when(pl.program_id(0) == 0)
        def _():
            dgu0[0] = d_gate
            dgu0[1] = d_up

        @pl.when(pl.program_id(0) == 1)
        def _():
            dgu1[0] = d_gate
            dgu1[1] = d_up

    saved = pl.BlockSpec((1, rows, tile), lambda h, i, c: (h, 0, i))
    return kernel_call(
        body,
        (2, steps),
        whole_of(d_mixed)
        + [saved, saved, pl.BlockSpec((1, width, tile), lambda h, i, c: (c[0] ^ h, 0, i))],
        core_blocks((2, rows, tile), steps),
        [jax.ShapeDtypeStruct((2, rows, size), BF16)] * 2,
        [pltpu.VMEM((rows, width), BF16)],
        4 * rows * width * size,
        4 * width * size + 24 * rows * size,
        prefetch=1,
    )(core, *d_mixed, gate_all, up_all, w_out)


def gate_up_backward(dgu, w_in, core, earlier=(), most=768):
    _, rows, size = dgu[0].shape
    width = w_in.shape[1]
    tile = tile_of(width, most)

    def body(core_ref, d0, d1, w0, w1, *refs):
        total = mm_nt(d0[0], w0[0, :, :size]) + mm_nt(d0[1], w0[0, :, size:])
        total += mm_nt(d1[0], w1[0, :, :size]) + mm_nt(d1[1], w1[0, :, size:])
        refs[-2][...] = total[: rows // 2].astype(BF16)
        refs[-1][...] = total[rows // 2 :].astype(BF16)

    whole = pl.BlockSpec((2, rows, size), lambda i, c: (0, 0, 0))
    return kernel_call(
        body,
        (width // tile,),
        [
            whole,
            whole,
            pl.BlockSpec((1, tile, 2 * size), lambda i, c: (c[0], i, 0)),
            pl.BlockSpec((1, tile, 2 * size), lambda i, c: (1 - c[0], i, 0)),
        ]
        + [pl.BlockSpec(memory_space=pl.ANY)] * len(earlier),
        [pl.BlockSpec((rows // 2, tile), lambda i, c: (0, i))] * 2,
        [jax.ShapeDtypeStruct((rows // 2, width), BF16)] * 2,
        [],
        8 * rows * width * size,
        8 * width * size + 8 * rows * size,
        prefetch=1,
    )(core, *dgu, w_in, w_in, *earlier)


def weight_grad_kernel(lefts, rights, ctx_count, fsdp_count, earlier=()):
    width = lefts[0].shape[1]
    groups, _, size = rights[0].shape
    left_counts = [v.shape[0] for v in lefts]
    counts = [v.shape[1] for v in rights]
    starts = [sum(counts[:i]) for i in range(len(counts))]
    shard = width // (ctx_count * fsdp_count)
    halves = 2
    part, ctx_part = width // halves, ctx_count // halves
    tile = tile_of(size, 1152)
    steps = size // tile

    def body(*refs):
        left_refs, right_refs = refs[: len(lefts)], refs[len(lefts) :][: len(rights)]
        out, turned_left = refs[-2:]

        @pl.when((pl.program_id(1) == 0) & (pl.program_id(2) == 0))
        def _():
            at = 0
            for ref, count in zip(left_refs, left_counts):
                turned_left[:, at : at + count] = ref[...].T
                at += count

        product = 0.0
        for ref, start, count in zip(right_refs, starts, counts):
            product = product + mm(turned_left[:, start : start + count], ref[0])
        for f in range(fsdp_count):
            at = [(c * fsdp_count + f) * shard for c in range(ctx_part)]
            out[f] = jnp.concatenate([product[i : i + shard] for i in at], 0).astype(BF16)

    return kernel_call(
        body,
        (halves, groups, steps),
        [pl.BlockSpec((n, part), lambda h, g, t: (0, h)) for n in left_counts]
        + [pl.BlockSpec((1, n, tile), lambda h, g, t: (g, 0, t)) for n in counts]
        + [pl.BlockSpec(memory_space=pl.ANY)] * len(earlier),
        pl.BlockSpec((fsdp_count, ctx_part * shard, tile), lambda h, g, t: (0, h, g * steps + t)),
        jax.ShapeDtypeStruct((fsdp_count, ctx_count * shard, groups * size), BF16),
        [pltpu.VMEM((part, sum(counts)), BF16)],
        2 * sum(counts) * width * groups * size,
        4 * sum(counts) * (width + groups * size) + 2 * width * groups * size,
    )(*lefts, *rights, *earlier)


def rotated(values, cosine, sine, back=False):
    size = values.shape[1] // 2
    low, high = values[:, :size], values[:, size:]
    if back:
        sine = -sine
    return jnp.concatenate([low * cosine - high * sine, high * cosine + low * sine], 1)


def qkv_kernel(inputs, g_pre, attn, cosine, sine, core):
    rows, width = sum(v.shape[0] for v in inputs), inputs[0].shape[1]
    block = rows // 2
    size = HEAD_DIM

    def body(core_ref, s0, s1, s2, s3, gain, w0, w1, cos, sin, normed_out, q0, q1, kv, x):
        take_slots((s0, s1, s2, s3), x)
        source = x[...].astype(F32)
        normed = (source * inverse_rms(source) * gain[...]).astype(BF16)
        normed_out[...] = normed
        first = core_ref[0] == 0
        own, other = mm(normed, w0[...]), mm(normed, w1[...])
        q0[...] = rotated(own[:, :size], cos[...], sin[...]).astype(BF16)
        q1[...] = rotated(other[:, :size], cos[...], sin[...]).astype(BF16)
        key = jnp.where(first, own[:, size:], other[:, size:])
        kv[:, :size] = rotated(key, cos[...], sin[...]).astype(BF16)
        kv[:, size:] = jnp.where(first, other[:, size:], own[:, size:]).astype(BF16)

    def by_rows(columns):
        return pl.BlockSpec((block, columns), lambda i, c: (i, 0))

    return kernel_call(
        body,
        (2,),
        whole_of(inputs)
        + [
            pl.BlockSpec((1, width), lambda i, c: (0, 0)),
            pl.BlockSpec((width, 2 * size), lambda i, c: (0, 0)),
            pl.BlockSpec((width, 2 * size), lambda i, c: (0, 0)),
            by_rows(size // 2),
            by_rows(size // 2),
        ],
        [by_rows(width), by_rows(size), by_rows(size), by_rows(2 * size)],
        [
            jax.ShapeDtypeStruct((rows, width), BF16),
            jax.ShapeDtypeStruct((rows, size), BF16),
            jax.ShapeDtypeStruct((rows, size), BF16),
            jax.ShapeDtypeStruct((rows, 2 * size), BF16),
        ],
        [pltpu.VMEM((block, width), BF16)],
        8 * rows * width * size,
        8 * width * size + 4 * rows * width,
        prefetch=1,
    )(core, *inputs, g_pre, *attn, cosine, sine)


def scores(query, key, key_place, query_place):
    raw = mm_nt(query, key)
    tanh_part = jnp.tanh(raw * (HEAD_DIM**-0.5 / SOFT_CAP))
    return tanh_part, jnp.where(key_place <= query_place, jnp.exp(SOFT_CAP * tanh_part), 0.0)


def attention_specs(rows, width, block):
    def by_rows(columns):
        return pl.BlockSpec((block, columns), lambda i, c: (i, 0))

    size = HEAD_DIM
    kv = pl.BlockSpec((rows, 2 * size), lambda i, c: (0, 0))
    places = pl.BlockSpec((1, rows), lambda i, c: (0, 0))
    weights = [pl.BlockSpec((width, size), lambda i, c: (0, 2))] * 2
    return by_rows, [by_rows(size), by_rows(size), kv, kv, by_rows(1), places, places] + weights


def put_slots(total, slots):
    rows = slots[0].shape[0]
    for step in range(2):

        @pl.when(pl.program_id(0) == step)
        def _():
            slots[2 * step][...] = total[:rows].astype(BF16)
            slots[2 * step + 1][...] = total[rows:].astype(BF16)


def take_slots(slots, into):
    for step in range(2):
        pl.when(pl.program_id(0) == step)(
            lambda pair=slots[2 * step : 2 * step + 2]: stack_rows(pair, into)
        )


def attention_forward(core, queries, kvs, row_places, key_places, attn):
    rows, width, size = queries[0].shape[0], attn[0].shape[0], HEAD_DIM
    block = rows // 2

    def body(core_ref, q0, q1, kv0, kv1, place, places0, places1, w0, w1, att0, att1, *branch):
        total = 0.0
        for q, att, w in ((q0, att0, w0), (q1, att1, w1)):
            parts = [
                scores(q[...], kv[:, :size], places[...], place[...])[1]
                for kv, places in ((kv0, places0), (kv1, places1))
            ]
            scale = 1.0 / (
                jnp.sum(parts[0], -1, keepdims=True) + jnp.sum(parts[1], -1, keepdims=True)
            )
            attended = mm((parts[0] * scale).astype(BF16), kv0[:, size:])
            attended += mm((parts[1] * scale).astype(BF16), kv1[:, size:])
            attended = attended.astype(BF16)
            att[...] = attended
            total = total + mm_nt(attended, w[...])
        put_slots(total, branch)

    by_rows, specs = attention_specs(rows, width, block)
    slots = [jax.ShapeDtypeStruct((rows // 4, width), BF16)] * 4
    return kernel_call(
        body,
        (2,),
        specs,
        [by_rows(size), by_rows(size)] + whole_of(slots),
        [jax.ShapeDtypeStruct((rows, size), BF16)] * 2 + slots,
        [],
        16 * rows * rows * size + 4 * rows * width * size,
        4 * width * size + 2 * rows * width,
        prefetch=1,
    )(core, *queries, *kvs, row_places, *key_places, *attn)


def attention_backward(
    d_branch, core, queries, kvs, row_places, key_places, attn, cosine, sine
):
    rows, width, size = queries[0].shape[0], attn[0].shape[0], HEAD_DIM
    block = rows // 2
    scaling = size**-0.5

    def body(
        core_ref, q0, q1, kv0, kv1, place, places0, places1, w0, w1, s0, s1, s2, s3, cos, sin,
        dq0, dq1, dkv0, dkv1, sum0, sum1, d_out
    ):
        take_slots((s0, s1, s2, s3), d_out)

        @pl.when(pl.program_id(0) == 0)
        def _():
            sum0[...] = jnp.zeros_like(sum0)
            sum1[...] = jnp.zeros_like(sum1)

        for q, dq, w in ((q0, dq0, w0), (q1, dq1, w1)):
            query = q[...]
            d_att = mm(d_out[...], w[...]).astype(BF16)
            parts = [
                scores(query, kv[:, :size], places[...], place[...])
                for kv, places in ((kv0, places0), (kv1, places1))
            ]
            scale = 1.0 / sum(jnp.sum(e, -1, keepdims=True) for _, e in parts)
            chances = [e * scale for _, e in parts]
            d_chances = [mm_nt(d_att, kv[:, size:]) for kv in (kv0, kv1)]
            inner = sum(
                jnp.sum(p * d, -1, keepdims=True) for p, d in zip(chances, d_chances)
            )
            d_query = 0.0
            for (t, _), p, d, kv, sums in zip(
                parts, chances, d_chances, (kv0, kv1), (sum0, sum1)
            ):
                d_raw = (p * (d - inner) * (1.0 - t * t) * scaling).astype(BF16)
                d_query = d_query + mm(d_raw, kv[:, :size])
                sums[:, :size] += mm_tn(d_raw, query)
                sums[:, size:] += mm_tn(p.astype(BF16), d_att)
            dq[...] = rotated(d_query, cos[...], sin[...], back=True).astype(BF16)

        @pl.when(pl.program_id(0) == pl.num_programs(0) - 1)
        def _():
            dkv0[...] = sum0[...]
            dkv1[...] = sum1[...].astype(BF16)

    by_rows, specs = attention_specs(rows, width, block)
    whole = pl.BlockSpec((rows, 2 * size), lambda i, c: (0, 0))
    return kernel_call(
        body,
        (2,),
        specs + whole_of(d_branch) + [by_rows(size // 2), by_rows(size // 2)],
        [by_rows(size), by_rows(size), whole, whole],
        [
            jax.ShapeDtypeStruct((rows, size), BF16),
            jax.ShapeDtypeStruct((rows, size), BF16),
            jax.ShapeDtypeStruct((rows, 2 * size), F32),
            jax.ShapeDtypeStruct((rows, 2 * size), BF16),
        ],
        [pltpu.VMEM((rows, 2 * size), F32)] * 2 + [pltpu.VMEM((block, width), BF16)],
        40 * rows * rows * size + 4 * rows * width * size,
        4 * width * size + 2 * rows * width,
        prefetch=1,
    )(core, *queries, *kvs, row_places, *key_places, *attn, *d_branch, cosine, sine)


def qkv_backward(inputs, dqs, dkv_mine, dkv_got, attn, cosine, sine, core):
    rows, width = sum(v.shape[0] for v in inputs), inputs[0].shape[1]
    block, size = rows // 2, HEAD_DIM

    def body(core_ref, s0, s1, s2, s3, q0, q1, mine, got, w0, w1, cos, sin, *refs):
        d_in, (dp0, dp1, gain, x) = refs[:4], refs[4:]
        take_slots((s0, s1, s2, s3), x)
        both = mine[...] + got[...].astype(F32)
        d_key = rotated(both[:, :size], cos[...], sin[...], back=True)
        first = core_ref[0] == 0
        dp0[0, :, :size] = q0[...]
        dp1[0, :, :size] = q1[...]
        dp0[0, :, size:] = jnp.where(first, d_key, both[:, size:]).astype(BF16)
        dp1[0, :, size:] = jnp.where(first, both[:, size:], d_key).astype(BF16)
        total = mm_nt(dp0[0], w0[...]) + mm_nt(dp1[0], w1[...])
        put_slots(total, d_in)
        source = x[...].astype(F32)
        term = jnp.sum(total * source * inverse_rms(source), 0, keepdims=True)

        @pl.when(pl.program_id(0) == 0)
        def _():
            gain[...] = jnp.zeros_like(gain)

        gain[...] += term

    def by_rows(columns):
        return pl.BlockSpec((block, columns), lambda i, c: (i, 0))

    weights = [pl.BlockSpec((width, 2 * size), lambda i, c: (0, 0))] * 2
    terms = pl.BlockSpec((1, block, 2 * size), lambda i, c: (0, i, 0))
    return kernel_call(
        body,
        (2,),
        whole_of(inputs)
        + [by_rows(size), by_rows(size), by_rows(2 * size), by_rows(2 * size)]
        + weights
        + [by_rows(size // 2), by_rows(size // 2)],
        whole_of(inputs) + [terms, terms, pl.BlockSpec((1, width), lambda i, c: (0, 0))],
        [jax.ShapeDtypeStruct(v.shape, BF16) for v in inputs]
        + [
            jax.ShapeDtypeStruct((1, rows, 2 * size), BF16),
            jax.ShapeDtypeStruct((1, rows, 2 * size), BF16),
            jax.ShapeDtypeStruct((1, width), F32),
        ],
        [pltpu.VMEM((block, width), BF16)],
        8 * rows * width * size,
        8 * width * size + 4 * rows * width,
        prefetch=1,
    )(core, *inputs, *dqs, dkv_mine, dkv_got, *attn, cosine, sine)


def to_owners(total, ctx_count):
    total = total.reshape(ctx_count, -1, total.shape[1])
    return lax.all_to_all(total, "ctx", split_axis=0, concat_axis=0, tiled=True)


def side_by_side(terms):
    return terms.astype(F32).transpose(1, 0, 2).reshape(terms.shape[1], -1)


def whole_kernel(body, out_shape, *values):
    return pl.pallas_call(
        body,
        out_shape=out_shape,
        compiler_params=pltpu.CompilerParams(vmem_limit_bytes=VMEM_BYTES),
        cost_estimate=pl.CostEstimate(
            flops=0, bytes_accessed=sum(v.size * v.dtype.itemsize for v in values), transcendentals=0
        ),
    )(*values)


def residual_backward(terms, residual, branch, upstream, g_mid, g_post):
    def body(t0, t1, t2, res, br, up, gm, gp, d_res, d_br, gain_mid, gain_post):
        d_mid = sum_of((t0[...], t1[...], t2[...]))
        value, scale = res[...], inverse_rms(res[...])
        gain_mid[...] = jnp.sum(d_mid * value * scale, 0, keepdims=True)
        total = up[...].astype(F32) + norm_backward(value, scale, d_mid * gm[...])
        d_res[...] = total
        value, scale = br[...], inverse_rms(br[...])
        gain_post[...] = jnp.sum(total * value * scale, 0, keepdims=True)
        d_br[...] = norm_backward(value, scale, total * gp[...]).astype(BF16)

    shape, width = residual.shape, residual.shape[1]
    outs = [jax.ShapeDtypeStruct(shape, F32), jax.ShapeDtypeStruct(shape, BF16)]
    outs += [jax.ShapeDtypeStruct((1, width), F32)] * 2
    return whole_kernel(body, outs, *terms, residual, branch, upstream, g_mid, g_post)


def attention_outputs(terms, columns):
    count, rows, _ = terms.shape
    size = HEAD_DIM

    def body(t, grad, gains):
        total = 0.0
        for c in range(count):
            part = t[c].astype(F32)
            kv = count * size + (c % 2) * (count // 2) * size + c // 2 * size
            grad[:, c * size : (c + 1) * size] = part[:, :size]
            grad[:, kv : kv + size] = part[:, size : 2 * size]
            out = columns - (count - c) * size
            grad[:, out : out + size] = part[:, 2 * size : 3 * size]
            total = total + part[:, 3 * size :]
        gains[...] = total

    return pl.pallas_call(
        body,
        out_shape=[
            jax.ShapeDtypeStruct((rows, columns), F32),
            jax.ShapeDtypeStruct((rows, terms.shape[2] - 3 * size), F32),
        ],
        compiler_params=pltpu.CompilerParams(vmem_limit_bytes=VMEM_BYTES),
    )(terms)


def local_kernels(
    layer_input, attn_weights, mlp_in_weights, mlp_out_weights, norm_gains, output_grad
):
    tokens, width = layer_input.shape[1:]
    half_block = tokens // 2
    ctx_count = lax.axis_size("ctx")
    fsdp_count = lax.axis_size("fsdp")
    ranks = ctx_count // 2
    place = lax.axis_index("ctx")
    fsdp_place = lax.axis_index("fsdp")
    rank, core = place // 2, place % 2
    query_cols, key_cols = HEADS * HEAD_DIM, KV_HEADS * HEAD_DIM
    qkv_cols = query_cols + 2 * key_cols
    hidden_width = mlp_out_weights.shape[1]
    f_own = hidden_width // ctx_count
    shard_rows = width // (ctx_count * fsdp_count)

    def partner(values):
        return swap(values, "ctx", 1, ctx_count)

    def columns(array, start, size):
        return lax.dynamic_slice_in_dim(array, start, size, 1)

    chip_groups = [
        [(2 * r + c) * fsdp_count + f for c in (0, 1) for f in range(fsdp_count)]
        for r in range(ranks)
    ]

    def chip_gather(piece):
        whole = lax.all_gather(
            piece, ("ctx", "fsdp"), axis=0, tiled=True, axis_index_groups=chip_groups
        )
        return whole.reshape(2, width, piece.shape[1])

    def over_sequences(product):
        product = product.reshape(width, product.shape[2])
        return lax.psum_scatter(product, "fsdp", scatter_dimension=0, tiled=True)

    own_input = layer_input.reshape(tokens, width)
    source = own_input.astype(F32)
    upstream = output_grad.reshape(tokens, width).astype(F32)
    kv_start = query_cols + core * key_cols + rank * HEAD_DIM
    piece = [
        columns(attn_weights, place * HEAD_DIM, HEAD_DIM),
        columns(attn_weights, kv_start, HEAD_DIM),
        columns(attn_weights, qkv_cols + place * HEAD_DIM, HEAD_DIM),
    ]
    piece, place_in = together(jnp.concatenate(piece, 1), place)
    own_gains = norm_gains.T
    if fsdp_count == 4:
        ways = [swap(own_input, "ctx", 4, ctx_count), swap(own_input, "ctx", 2, ctx_count)]

        def onward(got):
            return swap(got[0], "ctx", 2, ctx_count), [swap(own_gains, "fsdp", k, 4) for k in (1, 2, 3)]

        attn_own, (slot_2, slot_1), (slot_3, gains_got) = square_gather(
            piece, fsdp_place, (ways, onward)
        )
        gains = jnp.zeros((4, width), BF16)
        for k, block in enumerate([own_gains, *gains_got]):
            start = (fsdp_place ^ k) * own_gains.shape[1]
            gains = lax.dynamic_update_slice_in_dim(gains, block, start, 1)
        gains = gains.astype(F32)
        inputs = [own_input, slot_1, slot_2, slot_3]
    else:
        attn_own = lax.all_gather(piece, "fsdp", axis=0, tiled=True)
        inputs = line_gather(own_input, ranks)
        gains = lax.all_gather(own_gains, "fsdp", axis=1, tiled=True).astype(F32)
    attn = (attn_own, partner(attn_own))
    g_pre, g_post, g_mid, g_out = [gains[i] for i in range(4)]
    in_all = chip_gather(
        jnp.concatenate(
            [
                columns(mlp_in_weights, place_in * f_own, f_own),
                columns(mlp_in_weights, hidden_width + place_in * f_own, f_own),
            ],
            1,
        )
    )
    out_all = chip_gather(columns(mlp_out_weights, place_in * f_own, f_own))

    def places_of(which):
        owners = (2 * (rank ^ jnp.arange(ranks, dtype=jnp.int32)) + which)[:, None] * tokens
        gathered_rows = owners + jnp.arange(tokens, dtype=jnp.int32)[None, :]
        return positions_of(gathered_rows.reshape(-1), half_block, ctx_count)

    own_places, other_places = places_of(core), places_of(1 - core)
    cosine, sine = rotary_tables(own_places, HEAD_DIM)
    cosine, sine = cosine[:, : HEAD_DIM // 2], sine[:, : HEAD_DIM // 2]
    row_places, key_places = own_places[:, None], (own_places[None, :], other_places[None, :])
    core_word = core.reshape(1).astype(jnp.int32)

    normed_in, *queries, kv_own = qkv_kernel(
        inputs, gains[:1], attn, cosine, sine, core_word
    )
    attention = (core_word, queries, (kv_own, partner(kv_own)), row_places, key_places, attn)
    att_own, att_other, *branch_parts = attention_forward(*attention)

    def own_rows(halves, beside=()):
        parts = [halves[k % 2][k // 2] for k in range(4)]
        terms, _, beside = four_scatter(parts, ctx_count, (), lambda first: beside)
        return terms, beside

    def gathered_halves(values, work):
        slots = four_gather(values, ctx_count)
        done = work([slots[0], slots[2]], 0)
        slots[3], done = together(slots[3], done)
        return [slots[0], slots[2], slots[1], slots[3]], (done, work([slots[1], slots[3]], 1))

    branch = sum_of(four_scatter(branch_parts, ctx_count)[0])
    scale_branch = inverse_rms(branch)
    residual = source + branch * scale_branch * g_post
    scale_mid = inverse_rms(residual)
    mids, forward = gathered_halves(
        (residual * scale_mid * g_mid).astype(BF16), lambda v, _: gate_up_forward(v, in_all, core_word)
    )
    mixed_1 = down_forward(forward[1][:2], out_all, core_word)
    mixed_0 = down_forward(forward[0][:2], out_all, core_word, mixed_1)
    hidden_own = [f[0] for f in forward]
    hidden_got = [partner(f[1]) for f in forward]
    mid_got = [partner(v) for v in mids]
    mixed = sum_of(own_rows((mixed_0, mixed_1))[0])
    mixed, hidden_own, hidden_got, mid_got = together(mixed, hidden_own, hidden_got, mid_got)
    scale_mixed = inverse_rms(mixed)
    block_out = (residual + mixed * scale_mixed * g_out).astype(BF16)
    grad_out_gain = jnp.sum(upstream * mixed * scale_mixed, 0)
    d_mixeds, d_gate_ups = gathered_halves(
        norm_backward(mixed, scale_mixed, upstream * g_out).astype(BF16),
        lambda v, k: down_backward(v, *forward[k][2:], out_all, core_word),
    )

    def weight_grad(lefts, rights, *earlier):
        return weight_grad_kernel(lefts, rights, ctx_count, fsdp_count, earlier)

    down_product = weight_grad(
        [*d_mixeds, *[partner(v) for v in d_mixeds]], hidden_own + hidden_got
    )
    d_gate_ups, down_product = together(d_gate_ups, down_product)
    down_total = over_sequences(down_product)
    d_mid_1 = gate_up_backward(d_gate_ups[1], in_all, core_word)
    d_mid_0 = gate_up_backward(d_gate_ups[0], in_all, core_word, d_mid_1)
    gate_up_product = weight_grad(
        [*mids, *mid_got],
        [v[0] for v in d_gate_ups] + [partner(v[1]) for v in d_gate_ups],
        *d_mid_0,
    )
    d_mid, (gate_up_product,) = own_rows((d_mid_0, d_mid_1), (gate_up_product,))
    gate_up_total = over_sequences(gate_up_product)
    d_residual, d_branch, grad_mid_gain, grad_post_gain = residual_backward(
        d_mid, residual, branch, output_grad.reshape(tokens, width), gains[2:3], gains[1:2]
    )
    d_branches = four_gather(d_branch, ctx_count)

    d_branches, down_total = together(d_branches, down_total)
    down = to_owners(down_total, ctx_count)
    *d_queries, dkv_own, dkv_other = attention_backward(d_branches, *attention, cosine, sine)
    *d_in, dproj_own, dproj_other, grad_pre_gain = qkv_backward(
        inputs, d_queries, dkv_own, partner(dkv_other), attn, cosine, sine, core_word
    )

    gain_terms = jnp.stack([grad_pre_gain[0], grad_post_gain[0], grad_mid_gain[0], grad_out_gain], 1)
    gain_terms = gain_terms.reshape(ctx_count, fsdp_count, shard_rows, 4)
    gain_terms = gain_terms.transpose(1, 0, 2, 3).reshape(fsdp_count, -1, 4)
    out_product = weight_grad(
        [*d_branches, *[partner(v) for v in d_branches]], [att_own[None], partner(att_other)[None]]
    )
    product = weight_grad([normed_in, partner(normed_in)], [dproj_own, partner(dproj_other)])
    product = jnp.concatenate([product, out_product, gain_terms.astype(BF16)], 2)

    def part(product, k):
        return lax.dynamic_index_in_dim(product, fsdp_place ^ k, 0, keepdims=False)

    def corners_of(first):
        return gate_up_total, corner_scatter(part(first[1], 3), 4) if fsdp_count == 4 else ()

    d_in, (down, product), (gate_up_total, corners) = four_scatter(
        d_in, ctx_count, (down, product), corners_of
    )
    gate_up_terms = to_owners(gate_up_total, ctx_count)
    if fsdp_count == 4:
        parts = [part(product, k).astype(F32) for k in range(4)]
        attn_total = rows_scatter(parts, corners, 4).astype(BF16)
    else:
        attn_total = over_sequences(product)
    gate_up_terms, attn_total = together(gate_up_terms, attn_total)
    attn_terms = to_owners(attn_total, ctx_count)
    d_in = sum_of(d_in)
    d_source = d_residual + norm_backward(source, inverse_rms(source), d_in * g_pre)

    grad_mlp_out = side_by_side(down)
    grad_mlp_in = jnp.concatenate(
        [side_by_side(gate_up_terms[:, :, :f_own]), side_by_side(gate_up_terms[:, :, f_own:])], 1
    )
    grad_attn, grad_gains = attention_outputs(attn_terms, attn_weights.shape[1])
    return (
        block_out.reshape(layer_input.shape),
        d_source.reshape(layer_input.shape),
        grad_attn,
        grad_mlp_in,
        grad_mlp_out,
        grad_gains,
    )


def local(layer_input, attn_weights, mlp_in_weights, mlp_out_weights, norm_gains, output_grad):
    ctx_count, fsdp_count = lax.axis_size("ctx"), lax.axis_size("fsdp")
    width, hidden_width = layer_input.shape[2], mlp_out_weights.shape[1]
    fits = (
        ctx_count == HEADS == 2 * KV_HEADS == 8
        and hidden_width % (128 * ctx_count) == 0
        and width % 256 == 0
        and width % (8 * ctx_count * fsdp_count) == 0
        and (width // fsdp_count) % 32 == 0
    )
    path = local_kernels if fits else local_general
    return path(
        layer_input, attn_weights, mlp_in_weights, mlp_out_weights, norm_gains, output_grad
    )


def local_general(layer_input, attn_weights, mlp_in_weights, mlp_out_weights, norm_gains, output_grad):
    tokens, width = layer_input.shape[1:]
    half_block = tokens // 2
    ctx_count = lax.axis_size("ctx")
    fsdp_count = lax.axis_size("fsdp")
    ranks = ctx_count // 2
    place = lax.axis_index("ctx")
    rank, core = place // 2, place % 2
    first_core = core == 0
    query_cols, key_cols = HEADS * HEAD_DIM, KV_HEADS * HEAD_DIM
    qkv_cols = query_cols + 2 * key_cols
    heads = HEADS // ranks
    sharing = ranks // KV_HEADS
    hidden_width = mlp_out_weights.shape[1]
    q_own = query_cols // ctx_count
    f_own = hidden_width // ctx_count
    shard_rows = width // (ctx_count * fsdp_count)
    scaling = HEAD_DIM**-0.5

    def partner(values):
        return swap(values, "ctx", 1, ctx_count)

    def columns(array, start, size):
        return lax.dynamic_slice_in_dim(array, start, size, 1)


    kv_start = query_cols + core * key_cols + rank // sharing * HEAD_DIM
    attn_piece = (
        columns(attn_weights, place * q_own, q_own),
        columns(attn_weights, kv_start, HEAD_DIM),
        columns(attn_weights, qkv_cols + place * q_own, q_own),
    )
    attn_own = lax.all_gather(jnp.concatenate(attn_piece, 1), "fsdp", axis=0, tiled=True)
    in_piece = (
        columns(mlp_in_weights, place * f_own, f_own),
        columns(mlp_in_weights, hidden_width + place * f_own, f_own),
    )
    in_piece = jnp.concatenate(in_piece, 1)
    out_piece = columns(mlp_out_weights, place * f_own, f_own)
    in_own = lax.all_gather(in_piece, "fsdp", axis=0, tiled=True)
    out_own = lax.all_gather(out_piece, "fsdp", axis=0, tiled=True)
    gains = lax.all_gather(norm_gains, "fsdp", axis=0, tiled=True).astype(F32)
    g_pre, g_post, g_mid, g_out = [gains[:, i] for i in range(4)]
    attn_other = partner(attn_own)
    qkv_own, proj_own = attn_own[:, : q_own + HEAD_DIM], attn_own[:, q_own + HEAD_DIM :]
    qkv_other, proj_other = attn_other[:, : q_own + HEAD_DIM], attn_other[:, q_own + HEAD_DIM :]

    own_input = layer_input.reshape(tokens, width)
    source = own_input.astype(F32)
    upstream = output_grad.reshape(tokens, width).astype(F32)
    inputs = jnp.concatenate(line_gather(own_input, ranks), 0).astype(F32)
    scale_in = inverse_rms(inputs)
    plain_in = inputs * scale_in
    normed_in = (plain_in * g_pre).astype(BF16)

    def places_of(which):
        slots = rank ^ jnp.arange(ranks, dtype=jnp.int32)
        owners = (2 * slots + which)[:, None] * tokens
        rows = owners + jnp.arange(tokens, dtype=jnp.int32)[None, :]
        return positions_of(rows.reshape(-1), half_block, ctx_count)

    own_places, other_places = places_of(core), places_of(1 - core)
    cosine, sine_table = rotary_tables(own_places, HEAD_DIM)
    all_places = jnp.concatenate([own_places, other_places], 0)
    allowed = all_places[None, :] <= own_places[:, None]
    rows = ranks * tokens

    def ordered(mine, theirs):
        return jnp.where(first_core, mine, theirs), jnp.where(first_core, theirs, mine)

    proj_a, proj_b = dot(normed_in, qkv_own), dot(normed_in, qkv_other)
    query_raw = jnp.concatenate(ordered(proj_a[:, :q_own], proj_b[:, :q_own]), 1)
    key_raw, value_raw = ordered(proj_a[:, q_own:], proj_b[:, q_own:])
    query = rotate(
        query_raw.reshape(rows, heads, HEAD_DIM), cosine[:, None], sine_table[:, None]
    ).astype(BF16)
    key_own = rotate(key_raw, cosine, sine_table).astype(BF16)
    value_own = value_raw.astype(BF16)
    key_value = jnp.concatenate([key_own, value_own], 1)
    key_value = jnp.concatenate([key_value, partner(key_value)], 0)
    keys, values = key_value[:, :HEAD_DIM], key_value[:, HEAD_DIM:]

    def score_rows():
        raw_scores = jnp.einsum("tgd,ld->gtl", query, keys, preferred_element_type=F32)
        tanh_part = jnp.tanh(raw_scores * scaling / SOFT_CAP)
        return tanh_part, jnp.where(allowed, SOFT_CAP * tanh_part, MASKED_SCORE)

    tanh_part, capped = score_rows()
    row_max = jnp.max(capped, -1, keepdims=True)
    weights = jnp.exp(capped - row_max)
    row_total = jnp.sum(weights, -1, keepdims=True)
    log_total = row_max + jnp.log(row_total)
    chances = (weights / row_total).astype(BF16)
    attended = jnp.einsum("gtl,ld->tgd", chances, values, preferred_element_type=F32)
    attended = attended.reshape(rows, heads * HEAD_DIM).astype(BF16)
    att_own, att_other = ordered(attended[:, :q_own], attended[:, q_own:])
    branch_parts = (dot_t(att_own, proj_own) + dot_t(att_other, proj_other)).reshape(
        ranks, tokens, width
    )

    span = tokens // STREAMS
    cuts = [slice(s * span, (s + 1) * span) for s in range(STREAMS)]

    def own_rows(parts):
        return line_scatter(list(parts.reshape(ranks, -1, width)), ranks)

    def all_rows(values):
        return jnp.concatenate(line_gather(values, ranks), 0)

    branch = [own_rows(branch_parts[:, cut]) for cut in cuts]
    halves = ((in_own, out_own), (partner(in_own), partner(out_own)))
    scale_branch = [inverse_rms(v) for v in branch]
    residual = [source[cut] + v * w * g_post for cut, v, w in zip(cuts, branch, scale_branch)]
    scale_mid = [inverse_rms(v) for v in residual]
    mids = [all_rows((v * w * g_mid).astype(BF16)) for v, w in zip(residual, scale_mid)]
    hiddens, backs, mixed = [], [], []
    for values_in in mids:
        hidden_of, back_of, total = [], [], 0.0
        for w_in, w_out in halves:
            gate_up = dot(values_in, w_in)
            hidden, back = jax.vjp(geglu, gate_up[:, :f_own], gate_up[:, f_own:])
            hidden_of.append(hidden.astype(BF16))
            back_of.append(back)
            total = total + dot_t(hidden_of[-1], w_out)
        hiddens.append(hidden_of)
        backs.append(back_of)
        mixed.append(own_rows(total))
    scale_mixed = [inverse_rms(v) for v in mixed]
    block_out = [
        (r + v * w * g_out).astype(BF16) for r, v, w in zip(residual, mixed, scale_mixed)
    ]
    ups = [upstream[cut] for cut in cuts]
    grad_out_gain = sum(jnp.sum(u * v * w, 0) for u, v, w in zip(ups, mixed, scale_mixed))
    d_mixeds = [
        all_rows(norm_backward(v, w, u * g_out).astype(BF16))
        for u, v, w in zip(ups, mixed, scale_mixed)
    ]

    def both_cores(mine, others=None):
        return jnp.concatenate([mine, partner(mine if others is None else others)], 0)

    def joined(pieces):
        return jnp.concatenate(pieces, 0)

    def grouped(left):
        left = left.reshape(left.shape[0], ctx_count, fsdp_count, shard_rows)
        return left.transpose(0, 2, 1, 3).reshape(left.shape[0], fsdp_count, ctx_count * shard_rows)

    def weight_grad(left, right):
        product = jnp.einsum("tfr,tn->frn", grouped(left), right, preferred_element_type=F32)
        return product.reshape(width, right.shape[1]).astype(BF16)

    def over_sequences(product):
        total = lax.psum_scatter(product, "fsdp", scatter_dimension=0, tiled=True)
        return total.reshape(ranks, 2, shard_rows, product.shape[1])

    def spread(total):
        mine = jnp.where(first_core, total[:, 0], total[:, 1])
        theirs = partner(jnp.where(first_core, total[:, 1], total[:, 0]))
        both = jnp.stack(ordered(mine, theirs), 1)
        got = []
        for k in range(ranks):
            part = lax.dynamic_index_in_dim(both, rank ^ k, 0, keepdims=False)
            got.append(part if k == 0 else swap(part, "ctx", 2 * k, ctx_count))
        return got

    def put(into, piece, start, adds=False):
        piece = piece.astype(F32)
        if adds:
            piece = piece + lax.dynamic_slice_in_dim(into, start, piece.shape[1], 1)
        return lax.dynamic_update_slice_in_dim(into, piece, start, 1)

    mid_rows = both_cores(joined(mids))
    hidden_rows = both_cores(joined([h[0] for h in hiddens]), joined([h[1] for h in hiddens]))
    down_product = weight_grad(both_cores(joined(d_mixeds)), hidden_rows)
    d_mid, d_gate_ups = [], []
    for values_in, back_of in zip(d_mixeds, backs):
        total, d_gate_up_of = 0.0, []
        for (w_in, w_out), back in zip(halves, back_of):
            d_gate_up = jnp.concatenate(back(dot(values_in, w_out)), 1).astype(BF16)
            d_gate_up_of.append(d_gate_up)
            total = total + dot_t(d_gate_up, w_in)
        d_gate_ups.append(d_gate_up_of)
        d_mid.append(own_rows(total))
    down_total = over_sequences(down_product)
    dgu_rows = both_cores(joined([d[0] for d in d_gate_ups]), joined([d[1] for d in d_gate_ups]))
    gate_up_product = weight_grad(mid_rows, dgu_rows)
    gate_up_total = over_sequences(gate_up_product)

    grad_mid_gain = sum(jnp.sum(d * v * w, 0) for d, v, w in zip(d_mid, residual, scale_mid))
    d_residual = [
        u + norm_backward(v, w, d * g_mid) for u, v, w, d in zip(ups, residual, scale_mid, d_mid)
    ]
    grad_post_gain = sum(
        jnp.sum(d * v * w, 0) for d, v, w in zip(d_residual, branch, scale_branch)
    )
    d_branches = [
        line_gather(norm_backward(v, w, d * g_post).astype(BF16), ranks)
        for d, v, w in zip(d_residual, branch, scale_branch)
    ]
    d_branches = joined([d[k] for k in range(ranks) for d in d_branches])
    d_residual = joined(d_residual)

    down = spread(down_total)
    d_att_own, d_att_other = dot(d_branches, proj_own), dot(d_branches, proj_other)
    d_attended = jnp.concatenate(ordered(d_att_own, d_att_other), 1).astype(BF16)
    d_attended = d_attended.reshape(rows, heads, HEAD_DIM)
    tanh_again, capped_again = score_rows()
    chances_f = jnp.exp(capped_again - log_total)
    d_values = jnp.einsum(
        "gtl,tgd->ld", chances_f.astype(BF16), d_attended, preferred_element_type=F32
    )
    d_chances = jnp.einsum("tgd,ld->gtl", d_attended, values, preferred_element_type=F32)
    row_inner = jnp.sum(chances_f * d_chances, -1, keepdims=True)
    d_raw = (
        chances_f * (d_chances - row_inner) * (1.0 - tanh_again * tanh_again) * scaling
    ).astype(BF16)
    d_query = jnp.einsum("gtl,ld->tgd", d_raw, keys, preferred_element_type=F32)
    d_keys = jnp.einsum("gtl,tgd->ld", d_raw, query, preferred_element_type=F32)
    d_key_value = jnp.concatenate([d_keys, d_values], 1)
    d_key_value = d_key_value[:rows] + partner(d_key_value[rows:].astype(BF16)).astype(F32)
    d_query_raw = rotate_back(d_query, cosine[:, None], sine_table[:, None]).reshape(
        rows, heads * HEAD_DIM
    )
    d_key_raw = rotate_back(d_key_value[:, :HEAD_DIM], cosine, sine_table)
    dq_own, dq_other = ordered(d_query_raw[:, :q_own], d_query_raw[:, q_own:])
    dkv_own, dkv_other = ordered(d_key_raw, d_key_value[:, HEAD_DIM:])
    dproj_own = jnp.concatenate([dq_own, dkv_own], 1).astype(BF16)
    dproj_other = jnp.concatenate([dq_other, dkv_other], 1).astype(BF16)
    d_in = dot_t(dproj_own, qkv_own) + dot_t(dproj_other, qkv_other)
    grad_pre_gain = jnp.sum(d_in * plain_in, 0)
    d_in = own_rows(d_in)
    d_source = d_residual + norm_backward(source, scale_in[:tokens], d_in * g_pre)

    gate_up_terms = spread(gate_up_total)
    gain_terms = jnp.stack([grad_pre_gain, grad_post_gain, grad_mid_gain, grad_out_gain], 1)
    gain_terms = gain_terms.reshape(ctx_count, fsdp_count, shard_rows, 4)
    gain_terms = gain_terms.transpose(1, 0, 2, 3).reshape(fsdp_count, -1, 4)
    lefts = (grouped(both_cores(normed_in)), grouped(both_cores(d_branches)))
    rights = (both_cores(dproj_own, dproj_other), both_cores(att_own, att_other))

    def attn_part(index):
        at = [lax.dynamic_index_in_dim(v, index, 1, keepdims=False) for v in lefts]
        gain_rows = lax.dynamic_index_in_dim(gain_terms, index, 0, keepdims=False)
        pieces = [
            jnp.einsum("tr,tn->rn", v, right, preferred_element_type=F32)
            for v, right in zip(at, rights)
        ]
        return jnp.concatenate(pieces + [gain_rows], 1)

    attn_total = over_sequences(joined([attn_part(i).astype(BF16) for i in range(fsdp_count)]))
    attn_terms = spread(attn_total)

    grad_mlp_out = jnp.zeros((shard_rows, hidden_width), F32)
    grad_mlp_in = jnp.zeros((shard_rows, 2 * hidden_width), F32)
    grad_attn = jnp.zeros((shard_rows, attn_weights.shape[1]), F32)
    grad_gains = jnp.zeros((shard_rows, 4), F32)
    kv_end, out_end = q_own + HEAD_DIM, 2 * q_own + HEAD_DIM
    for k in range(ranks):
        giver = rank ^ k
        for which in (0, 1):
            start = (2 * giver + which) * f_own
            grad_mlp_out = put(grad_mlp_out, down[k][which], start)
            term = gate_up_terms[k][which]
            grad_mlp_in = put(grad_mlp_in, term[:, :f_own], start)
            grad_mlp_in = put(grad_mlp_in, term[:, f_own:], hidden_width + start)
            term = attn_terms[k][which]
            start = (2 * giver + which) * q_own
            grad_attn = put(grad_attn, term[:, :q_own], start)
            grad_attn = put(grad_attn, term[:, kv_end:out_end], qkv_cols + start)
            start = query_cols + which * key_cols + giver // sharing * HEAD_DIM
            grad_attn = put(grad_attn, term[:, q_own:kv_end], start, sharing > 1)
            grad_gains = grad_gains + term[:, out_end:].astype(F32)
    return (
        joined(block_out).reshape(layer_input.shape),
        d_source.reshape(layer_input.shape),
        grad_attn,
        grad_mlp_in,
        grad_mlp_out,
        grad_gains,
    )


def solution(mesh):
    in_specs = (
        P("fsdp", "ctx", None),
        P("fsdp", None),
        P("fsdp", None),
        P("fsdp", None),
        P("fsdp", None),
        P("fsdp", "ctx", None),
    )
    out_specs = (
        P("fsdp", "ctx", None),
        P("fsdp", "ctx", None),
        P(("ctx", "fsdp"), None),
        P(("ctx", "fsdp"), None),
        P(("ctx", "fsdp"), None),
        P(("ctx", "fsdp"), None),
    )
    return jax.shard_map(local, mesh=mesh, in_specs=in_specs, out_specs=out_specs, check_vma=False)
```
